32 devices in a mesh: dp: 8 (over z, y), seq: 4 (over x, core).
Axes of the slice: x: 2, y: 2, z: 4, core: 2. Of those that a mesh axis runs over, the one named last changes fastest.
Arguments:
- tokens: bfloat16 [32768, 512], P(('dp', 'seq')), may hold values from -6 to 6
- memory: bfloat16 [8192, 512], P(('dp', 'seq')), may hold values from -6 to 6
- lengths: int32 [64], P(('dp', 'seq')), may hold values from 128 to 512
- neighbours: int32 [32768, 4], P(('dp', 'seq')), may hold values from 0 to 1023
- out_grad: bfloat16 [32768, 512], P(('dp', 'seq')), may hold values from -6 to 6
- gain_one: bfloat16 [512], P(('dp', 'seq')), may hold values from 0.5 to 1.5
- gain_two: bfloat16 [512], P(('dp', 'seq')), may hold values from 0.5 to 1.5
- w_query: bfloat16 [512, 512], P(('dp', 'seq')), may hold values from -0.5 to 0.5
- w_key: bfloat16 [512, 512], P(('dp', 'seq')), may hold values from -0.25 to 0.25
- w_value: bfloat16 [512, 512], P(('dp', 'seq')), may hold values from -0.25 to 0.25
- w_gate: bfloat16 [512, 8], P(('dp', 'seq')), may hold values from -0.25 to 0.25
- w_out: bfloat16 [512, 512], P(('dp', 'seq')), may hold values from -0.5 to 0.5
- w_up: bfloat16 [512, 2048], P(('dp', 'seq')), may hold values from -0.25 to 0.25
- w_down: bfloat16 [2048, 512], P(('dp', 'seq')), may hold values from -0.125 to 0.125
Outputs:
- block_out: bfloat16 [32768, 512], P(('dp', 'seq'))
- grad_tokens: float32 [32768, 512], P(('dp', 'seq'))
- grad_gain_one: float32 [512], P(('dp', 'seq'))
- grad_gain_two: float32 [512], P(('dp', 'seq'))
- grad_w_query: float32 [512, 512], P(('dp', 'seq'))
- grad_w_key: float32 [512, 512], P(('dp', 'seq'))
- grad_w_value: float32 [512, 512], P(('dp', 'seq'))
- grad_w_gate: float32 [512, 8], P(('dp', 'seq'))
- grad_w_out: float32 [512, 512], P(('dp', 'seq'))
- grad_w_up: float32 [512, 2048], P(('dp', 'seq'))
- grad_w_down: float32 [2048, 512], P(('dp', 'seq'))
The draws below stay inside these ranges and needn't reach their ends.
Inputs may be any that keep to these rules, and one draw needn't show every extreme that they name: `neighbours`: A token's neighbour ids number the memory states of its own group.
All inputs are finite; a program needn't handle non-finite values.
Results may differ from the reference program's by a relative error of at most 0.013.
The reference program's roundings to bfloat16 on the way count: a program that leaves them out, or rounds other values in their place, can miss the bound.
Values may be sent and summed in bfloat16 or wider, within the bound.
No kernel may reach another device: no remote copies, remote signals or barrier semaphores. Data moves between devices by JAX's collectives and lax.ppermute only.
A program may use at most 192 MiB of HBM per device.

```python
import jax
import jax.numpy as jnp
from jax import lax

D = 512
H = 8
DH = 64
FF = 2048
KNN = 4
LEN = 512
MEMORY_SLOTS = 1024
GROUP = 4096
TOKENS = 32768
SEGS = 64
N_DP = 8


def plant(array, own_key, least, top_value):
    longest = array.shape.index(max(array.shape))
    spots = []
    for shift in (0, 1):
        where = [jax.random.randint(jax.random.fold_in(own_key, axis), (), 0, length) for axis, length in enumerate(array.shape)]
        where[longest] = (where[longest] + shift) % array.shape[longest]
        spots.append(tuple(where))
    return array.at[spots[0]].set(least).at[spots[1]].set(top_value)


def block_levels(stream_key, extent, pieces, low, largest):
    def one(axis_at, parts):
        heights = jax.random.uniform(jax.random.fold_in(jax.random.fold_in(stream_key, 6), axis_at), (parts,), jnp.float32, low / len(pieces), largest / len(pieces))
        return jnp.repeat(jnp.exp(heights), extent[axis_at] // parts).reshape((-1,) + (1,) * (len(extent) - axis_at - 1))

    gain = one(*pieces[0])
    for cut in pieces[1:]:
        gain = gain * one(*cut)
    return gain


def scatter_about(stream_key, extent, width, reach, cuts=(), kind=jnp.bfloat16):
    level = block_levels(stream_key, extent, cuts, -0.22, 0.18) if cuts else 1.0
    entries = jax.random.normal(stream_key, extent, jnp.float32) * width * level
    return jnp.minimum(jnp.maximum(entries, -reach), reach).astype(kind)


def setup_inputs(seed: int = 0) -> dict:
    key_list = jax.random.split(jax.random.key(seed), 15)
    return {
        "tokens": scatter_about(key_list[0], (TOKENS, D), 1.0, 6.0, ((0, 32),)),
        "memory": scatter_about(key_list[1], (N_DP * MEMORY_SLOTS, D), 1.0, 6.0, ((0, 32),)),
        "lengths": plant(jax.random.randint(key_list[2], (SEGS,), LEN // 4, LEN + 1), jax.random.fold_in(key_list[2], 1), LEN // 4, LEN).astype(jnp.int32),
        "neighbours": plant(jax.random.randint(key_list[3], (TOKENS, KNN), 0, MEMORY_SLOTS), jax.random.fold_in(key_list[3], 1), 0, MEMORY_SLOTS - 1).astype(jnp.int32),
        "out_grad": scatter_about(key_list[4], (TOKENS, D), 1.0, 6.0, ((0, 32),)),
        "gain_one": jnp.clip(1.0 + 0.1 * jax.random.normal(key_list[5], (D,), jnp.float32), 0.5, 1.5).astype(jnp.bfloat16),
        "gain_two": jnp.clip(1.0 + 0.1 * jax.random.normal(key_list[6], (D,), jnp.float32), 0.5, 1.5).astype(jnp.bfloat16),
        "w_query": scatter_about(key_list[7], (D, D), (D // 4) ** -0.5, 0.5, ((0, 32),)),
        "w_key": scatter_about(key_list[8], (D, D), D ** -0.5, 0.25, ((0, 32),)),
        "w_value": scatter_about(key_list[9], (D, D), D ** -0.5, 0.25, ((0, 32),)),
        "w_gate": scatter_about(key_list[10], (D, H), D ** -0.5, 0.25, ((0, 32),)),
        "w_out": scatter_about(key_list[11], (D, D), (D // 4) ** -0.5, 0.5, ((0, 32),)),
        "w_up": scatter_about(key_list[12], (D, FF), D ** -0.5, 0.25, ((0, 32),)),
        "w_down": scatter_about(key_list[13], (FF, D), FF ** -0.5, 0.125, ((0, 32),)),
    }


@jax.custom_vjp
def low(v):
    return lax.optimization_barrier(v.astype(jnp.bfloat16)).astype(jnp.float32)

@jax.custom_vjp
def low_back(v):
    return v

def low_keep(v):
    return (low(v), None)

def low_pass(kept, grad):
    return (grad,)

def back_keep(v):
    return (v, None)

def back_low(kept, grad):
    return (low(grad),)
low.defvjp(low_keep, low_pass)
low_back.defvjp(back_keep, back_low)
EPSILON = 1e-06
TOP_PRECISION = lax.Precision.HIGHEST

def matmul(left, right):
    return jnp.dot(left, right, precision=TOP_PRECISION, preferred_element_type=jnp.float32)

def group_block(params, rows, seg_lengths, neighbour_ids, mem_keys, mem_values):
    gain_one, gain_two, w_query, w_key, w_value, w_gate, w_out, w_up, w_down = params
    score_scale = DH ** (-0.5)
    segments = rows.shape[0] // LEN
    inv_one = lax.rsqrt(lax.optimization_barrier(jnp.mean(rows * rows, axis=-1, keepdims=True)) + EPSILON)
    normed = low(rows * inv_one * gain_one)
    queries = low_back(low(matmul(normed, w_query)))
    keys = low_back(low(matmul(normed, w_key)))
    values = low_back(low(matmul(normed, w_value)))
    gate = jax.nn.sigmoid(low_back(matmul(normed, w_gate)))
    query_head_rows = queries.reshape(segments, LEN, H, DH)
    key_heads = keys.reshape(segments, LEN, H, DH)
    value_heads = values.reshape(segments, LEN, H, DH)
    memory_key_heads = mem_keys.reshape(MEMORY_SLOTS, H, DH)
    memory_value_heads = mem_values.reshape(MEMORY_SLOTS, H, DH)
    memory_scores = jnp.einsum('prcv,fcv->pcrf', query_head_rows, memory_key_heads, precision=TOP_PRECISION) * score_scale
    score_loc = jnp.einsum('sqhd,skhd->shqk', query_head_rows, key_heads, precision=TOP_PRECISION) * score_scale
    scores = low_back(jnp.concatenate([memory_scores, score_loc], axis=-1))
    position = jnp.arange(LEN)
    allowed = (position[None, None, :] <= position[None, :, None]) & (position[None, None, :] < seg_lengths[:, None, None])
    allowed = jnp.concatenate([jnp.ones((segments, LEN, MEMORY_SLOTS), bool), allowed], axis=-1)[:, None]
    scores = jnp.where(allowed, scores, -1e+30)
    attention_probabilities = low(jax.nn.softmax(scores, axis=-1))
    context_output = jnp.einsum('pxoj,jxu->poxu', attention_probabilities[..., :MEMORY_SLOTS], memory_value_heads, precision=TOP_PRECISION)
    context_output = context_output + jnp.einsum('shqk,skhd->sqhd', attention_probabilities[..., MEMORY_SLOTS:], value_heads, precision=TOP_PRECISION)
    context_output = low_back(context_output).reshape(-1, H, DH)
    query_rows = queries.reshape(-1, H, DH)
    near_keys = jnp.take(mem_keys, neighbour_ids, axis=0).reshape(-1, KNN, H, DH)
    near_values = jnp.take(mem_values, neighbour_ids, axis=0).reshape(-1, KNN, H, DH)
    near_scores = jnp.einsum('nhd,njhd->nhj', query_rows, near_keys, precision=TOP_PRECISION) * score_scale
    near_probs = jax.nn.softmax(near_scores, axis=-1)
    recalled = jnp.einsum('nhj,njhd->nhd', near_probs, near_values, precision=TOP_PRECISION)
    blend = (1.0 - gate)[:, :, None] * context_output + gate[:, :, None] * recalled
    mixed = low(blend.reshape(-1, D))
    hidden = rows + low_back(matmul(mixed, w_out))
    inv_two = lax.rsqrt(lax.optimization_barrier(jnp.mean(hidden * hidden, axis=-1, keepdims=True)) + EPSILON)
    normed_two = low(hidden * inv_two * gain_two)
    pre_act = low_back(matmul(normed_two, w_up))
    activated = low(jax.nn.gelu(pre_act, approximate=True))
    return hidden + low_back(matmul(activated, w_down))

def forward(params, rows, memory, lengths, neighbours):
    mem_keys = low(matmul(memory, params[3]))
    mem_values = low(matmul(memory, params[4]))
    checked = jax.checkpoint(group_block)

    def step(carry, item):
        group_rows, group_lengths, group_ids, group_keys, group_values = item
        return (carry, checked(params, group_rows, group_lengths, group_ids, group_keys, group_values))
    items = (rows.reshape(N_DP, GROUP, D), lengths.reshape(N_DP, -1), neighbours.reshape(N_DP, GROUP, KNN), mem_keys.reshape(N_DP, MEMORY_SLOTS, D), mem_values.reshape(N_DP, MEMORY_SLOTS, D))
    _, outputs = lax.scan(step, jnp.zeros((), jnp.float32), items)
    return outputs.reshape(TOKENS, D)

def reference(tokens, memory, lengths, neighbours, out_grad, gain_one, gain_two, w_query, w_key, w_value, w_gate, w_out, w_up, w_down):
    params = tuple((weight.astype(jnp.float32) for weight in (gain_one, gain_two, w_query, w_key, w_value, w_gate, w_out, w_up, w_down)))
    memory_f = memory.astype(jnp.float32)

    def run(weights, rows):
        return forward(weights, rows, memory_f, lengths, neighbours)
    result, pull = jax.vjp(run, params, tokens.astype(jnp.float32))
    grads, grad_rows = pull(out_grad.astype(jnp.float32))
    return (result.astype(jnp.bfloat16), grad_rows, grads[0], grads[1], grads[2], grads[3], grads[4], grads[5], grads[6], grads[7], grads[8])
```

```python
import functools
import math

import jax
import jax.numpy as jnp
from jax import lax
from jax.experimental import pallas as pl
from jax.experimental.pallas import tpu as pltpu
from jax.sharding import PartitionSpec as P


EPSILON = 1e-06
MASKED = -1e30
LOG2E = math.log2(math.e)
F32 = jnp.float32
BF16 = jnp.bfloat16
VMEM_BYTES = 58 << 20
SIDE = 128
TILE = 256


def dot(left, right, left_dim=1, right_dim=0):
    return lax.dot_general(
        left, right, (((left_dim,), (right_dim,)), ((), ())), preferred_element_type=F32
    )


def call(kernel, outs, grid=None, in_specs=None, out_specs=None, scratch=(), flops=0, byte_count=0):
    options = {}
    if grid is not None:
        options = dict(grid=grid, in_specs=in_specs, out_specs=out_specs)
    return pl.pallas_call(
        kernel,
        out_shape=[jax.ShapeDtypeStruct(shape, kind) for shape, kind in outs],
        scratch_shapes=list(scratch),
        compiler_params=pltpu.CompilerParams(vmem_limit_bytes=VMEM_BYTES),
        cost_estimate=pl.CostEstimate(flops=flops, bytes_accessed=byte_count, transcendentals=0),
        **options,
    )


def whole(shape):
    zeros = (0,) * len(shape)
    return pl.BlockSpec(shape, lambda *_: zeros)


def three_parts(value):
    high = value.astype(BF16).astype(F32)
    rest = value - high
    middle = rest.astype(BF16).astype(F32)
    return high, middle, rest - middle


def pick_rows(rows, count):
    shape = (count, rows[0].shape[1])
    index = lax.broadcasted_iota(jnp.int32, shape, 0)
    block = jnp.zeros(shape, F32)
    for at, row in enumerate(rows):
        block = jnp.where(index == at, row, block)
    return block


def bits_of(size):
    return [1 << b for b in range(size.bit_length() - 1)]


def gather_steps(sizes):
    return [("dp", bit) for bit in reversed(bits_of(sizes["dp"]))] + [
        ("seq", bit) for bit in reversed(bits_of(sizes["seq"]))
    ]


def swap(array, step, sizes):
    axis, bit = step
    return lax.ppermute(array, axis, [(i, i ^ bit) for i in range(sizes[axis])])


def doubled(array, steps, sizes):
    for step in steps:
        array = jnp.concatenate([array, swap(array, step, sizes)], axis=0)
    return array


def halved(array, steps, sizes):
    for step in reversed(steps):
        half = array.shape[0] // 2
        other = swap(array[half:], step, sizes)
        array = array[:half].astype(F32) + other.astype(F32)
        if half > 1:
            array = array.astype(BF16)
    return array[0]


def places(steps, sizes):
    n_seq = sizes["seq"]
    ids = jnp.arange(sizes["dp"] * n_seq, dtype=jnp.int32)
    apart = {"dp": (ids // n_seq) ^ lax.axis_index("dp"), "seq": (ids % n_seq) ^ lax.axis_index("seq")}
    place = jnp.zeros_like(ids)
    for at, (axis, bit) in enumerate(steps):
        place = place | jnp.where((apart[axis] & bit) != 0, 1 << at, 0)
    return place


def owners(steps, sizes):
    n_seq = sizes["seq"]
    at = jnp.arange(sizes["dp"] * n_seq, dtype=jnp.int32)
    own = {"dp": lax.axis_index("dp"), "seq": lax.axis_index("seq")}
    for number, (axis, bit) in enumerate(steps):
        own[axis] = own[axis] ^ jnp.where((at >> number) & 1, bit, 0)
    return own["dp"] * n_seq + own["seq"]


def prepare_kernel(x_ref, g_ref, ids_ref, xt_ref, gt_ref, inv_ref, bias_ref, *, count):
    xt = x_ref[...].astype(F32).T
    xt_ref[...] = xt.astype(BF16)
    gt_ref[...] = g_ref[...].astype(F32).T.astype(BF16)
    inv = lax.rsqrt(jnp.mean(xt * xt, axis=0, keepdims=True) + EPSILON)
    inv_ref[...] = jnp.broadcast_to(inv, inv_ref.shape)
    slots, rows = bias_ref.shape
    step = 128

    def body(i, _):
        at = pl.multiple_of(i * step, step)
        slot = lax.broadcasted_iota(jnp.int32, (step, rows), 0) + at
        times = jnp.zeros((step, rows), F32)
        for j in range(count):
            times = times + jnp.where(ids_ref[j : j + 1, :] == slot, 1.0, 0.0)
        bias_ref[pl.ds(at, step), :] = jnp.where(times > 0.0, jnp.log2(times), MASKED)
        return 0

    lax.fori_loop(0, slots // step, body, 0)


def project_kernel(xt_ref, inv_ref, w_ref, memory_ref, nt_ref, qkv_ref, mem_ref, gate_ref):
    width = xt_ref.shape[0]
    gain = w_ref[:, 3 * width :].astype(F32)[:, 8:9]
    normed = (xt_ref[...].astype(F32) * inv_ref[0:1, :] * gain).astype(BF16)
    nt_ref[...] = normed
    for part in range(3):
        qkv_ref[part * width : (part + 1) * width, :] = dot(
            w_ref[:, part * width : (part + 1) * width], normed, 0, 0
        ).astype(BF16)
    logit = dot(w_ref[:, 3 * width :], normed, 0, 0)
    gate_ref[...] = jax.nn.sigmoid(logit[0:8])
    for part in range(2):
        mem_ref[part * width : (part + 1) * width, :] = dot(
            w_ref[:, (part + 1) * width : (part + 2) * width], memory_ref[...], 0, 1
        ).astype(BF16)


def local_penalty(lengths_ref, rows, seg_count):
    seg_len = rows // seg_count
    lane = lax.broadcasted_iota(jnp.int32, (1, rows), 1)
    last = jnp.zeros((1, rows), jnp.int32)
    for seg in range(seg_count):
        last = jnp.where(lane // seg_len == seg, seg * seg_len + lengths_ref[seg], last)
    return jnp.where(lane < last, 0.0, MASKED)


def causal_bias(size):
    key = lax.broadcasted_iota(jnp.int32, (size, size), 0)
    query = lax.broadcasted_iota(jnp.int32, (size, size), 1)
    return jnp.where(key <= query, 0.0, MASKED)


def attend_kernel(
    lengths_ref, q_ref, k_ref, v_ref, mk_ref, mv_ref, gate_ref, bias_ref,
    mixed_ref, ctx_ref, rec_ref, lse_ref, lsen_ref,
    *, seg_count, scale,
):
    head = pl.program_id(0)
    size, rows = q_ref.shape
    seg_len = rows // seg_count
    penalty = local_penalty(lengths_ref, rows, seg_count)
    causal = causal_bias(TILE)
    q = q_ref[...].astype(F32) * (scale * LOG2E)
    q_high = q.astype(BF16)
    q_low = (q - q_high.astype(F32)).astype(BF16)
    queries = jnp.concatenate([q_high, q_low, jnp.ones((16, rows), BF16)], axis=0)
    keys = jnp.concatenate([k_ref[...], k_ref[...], pick_rows([penalty], 16).astype(BF16)], axis=0)
    mem_keys = jnp.concatenate([mk_ref[...], mk_ref[...]], axis=0)
    values = jnp.concatenate([v_ref[...], jnp.ones((16, rows), BF16)], axis=0)
    mem_values = jnp.concatenate([mv_ref[...], jnp.ones((16, mk_ref.shape[1]), BF16)], axis=0)
    gate = gate_ref[pl.ds(head, 1), :]
    for at in range(0, rows, TILE):
        here = slice(at, at + TILE)
        start = at // seg_len * seg_len
        score_mem = dot(mem_keys, queries[: 2 * size, here], 0, 0)
        score_loc = dot(keys[:, start : at + TILE], queries[:, here], 0, 0)
        diagonal = score_loc[at - start :] + causal
        peak = jnp.maximum(
            jnp.max(score_mem, axis=0, keepdims=True), jnp.max(diagonal, axis=0, keepdims=True)
        )
        if at > start:
            peak = jnp.maximum(peak, jnp.max(score_loc[: at - start], axis=0, keepdims=True))
        near = score_mem + bias_ref[:, here]
        near_peak = jnp.max(near, axis=0, keepdims=True)
        exp_mem = jnp.exp2(score_mem - peak).astype(BF16)
        total = dot(mem_values, exp_mem)
        exp_diag = jnp.exp2(diagonal - peak).astype(BF16)
        total = total + dot(values[:, at : at + TILE], exp_diag)
        if at > start:
            exp_loc = jnp.exp2(score_loc[: at - start] - peak).astype(BF16)
            total = total + dot(values[:, start:at], exp_loc)
        exp_near = jnp.exp2(near - near_peak).astype(BF16)
        near_total = dot(mem_values, exp_near)
        context = total[:size] / total[size : size + 1]
        recalled = near_total[:size] / near_total[size : size + 1]
        ctx_ref[:, here] = context
        rec_ref[:, here] = recalled
        lse_ref[pl.ds(head, 1), here] = peak + jnp.log2(total[size : size + 1])
        lsen_ref[pl.ds(head, 1), here] = near_peak + jnp.log2(near_total[size : size + 1])
        share = gate[:, here]
        mixed_ref[:, here] = ((1.0 - share) * context + share * recalled).astype(BF16)


def feed_kernel(
    xt_ref, gt_ref, mixed_ref, ctx_ref, rec_ref, gate_ref, gain_ref, wo_ref, up_ref, down_ref,
    block_ref, gh_ref, dm_ref, dc_ref, dn_ref, dlogit_ref, ggain_ref, gwo_ref, gup_ref, gdown_ref,
    hidden_ref, n2_ref, out_ref, gn2_ref,
    *, heads,
):
    step = pl.program_id(0)
    last = pl.num_programs(0) - 1
    width, rows = xt_ref.shape
    gain = gain_ref[...].astype(F32)[:, 9:10]

    @pl.when(step == 0)
    def _():
        hidden = xt_ref[...].astype(F32) + dot(wo_ref[...], mixed_ref[...], 0, 0)
        hidden_ref[...] = hidden
        inv = lax.rsqrt(jnp.mean(hidden * hidden, axis=0, keepdims=True) + EPSILON)
        n2_ref[...] = (hidden * inv * gain).astype(BF16)
        out_ref[...] = jnp.zeros_like(out_ref)
        gn2_ref[...] = jnp.zeros_like(gn2_ref)

    n2 = n2_ref[...]
    grad = gt_ref[...]
    pre = dot(up_ref[...], n2, 0, 0)
    coef = math.sqrt(2.0 / math.pi)
    square = pre * pre
    tanh = jnp.tanh(coef * pre * (1.0 + 0.044715 * square))
    half = 0.5 * (1.0 + tanh)
    act = (pre * half).astype(BF16)
    slope = half + 0.5 * coef * pre * (1.0 - tanh * tanh) * (1.0 + (3.0 * 0.044715) * square)
    grad_pre = (dot(down_ref[...], grad) * slope).astype(BF16)
    out_ref[...] += dot(down_ref[...], act, 0, 0)
    gn2_ref[...] += dot(up_ref[...], grad_pre)
    gdown_ref[...] = dot(act, grad, 1, 1).astype(BF16)
    gup_ref[...] = dot(n2, grad_pre, 1, 1).astype(BF16)

    @pl.when(step == last)
    def _():
        hidden = hidden_ref[...]
        block_ref[...] = (hidden + out_ref[...]).T.astype(BF16)
        inv = lax.rsqrt(jnp.mean(hidden * hidden, axis=0, keepdims=True) + EPSILON)
        unit = hidden * inv
        gn2 = gn2_ref[...]
        ggain_ref[...] = jnp.broadcast_to(
            jnp.sum(gn2 * unit, axis=1, keepdims=True), ggain_ref.shape
        )
        a = gn2 * gain
        grad_hidden = gt_ref[...].astype(F32) + inv * (
            a - unit * jnp.mean(a * unit, axis=0, keepdims=True)
        )
        gh_ref[...] = grad_hidden
        branch = grad_hidden.astype(BF16)
        gwo_ref[...] = dot(mixed_ref[...], branch, 1, 1).astype(BF16)
        grad_mixed = dot(wo_ref[...], branch)
        rounded = grad_mixed.astype(BF16)
        dm_ref[...] = rounded
        size = width // heads
        rounded = rounded.astype(F32)
        for head in range(heads):
            rows_h = slice(head * size, (head + 1) * size)
            ctx, rec = ctx_ref[rows_h, :], rec_ref[rows_h, :]
            dc = jnp.sum(rounded[rows_h] * ctx, axis=0, keepdims=True)
            dn = jnp.sum(rounded[rows_h] * rec, axis=0, keepdims=True)
            dc_ref[head : head + 1, :] = dc
            dn_ref[head : head + 1, :] = dn
            share = gate_ref[head : head + 1, :]
            moved = jnp.sum(grad_mixed[rows_h] * (rec - ctx), axis=0, keepdims=True)
            dlogit_ref[head : head + 1, :] = moved * share * (1.0 - share)


def attend_back_kernel(
    lengths_ref, q_ref, k_ref, v_ref, mk_ref, mv_ref, dm_ref, gate_ref, bias_ref,
    lse_ref, lsen_ref, dc_ref, dn_ref,
    dq_ref, dk_ref, dv_ref, dmk_ref, dmv_ref,
    *, seg_count, scale,
):
    head = pl.program_id(0)
    size, rows = q_ref.shape
    seg_len = rows // seg_count
    penalty = local_penalty(lengths_ref, rows, seg_count)
    causal = causal_bias(TILE)
    q = q_ref[...].astype(F32) * (scale * LOG2E)
    q_high = q.astype(BF16)
    q_low = (q - q_high.astype(F32)).astype(BF16)
    row = pl.ds(head, 1)
    share = gate_ref[row, :]
    shift = jnp.log2(jnp.maximum(1.0 - share, 2.0**-60)) - lse_ref[row, :]
    near_shift = jnp.log2(jnp.maximum(share, 2.0**-60)) - lsen_ref[row, :] - shift
    dc = dc_ref[row, :]
    apart = dc - dn_ref[row, :]
    ones = jnp.ones((1, rows), F32)
    mem_ones = jnp.ones((1, mk_ref.shape[1]), F32)
    mem_three = pick_rows([mem_ones] * 3, 16).astype(BF16)
    queries = jnp.concatenate(
        [q_high, q_low, pick_rows([*three_parts(shift), ones], 16).astype(BF16)], axis=0
    )
    keys = jnp.concatenate(
        [k_ref[...], k_ref[...], pick_rows([ones, ones, ones, penalty], 16).astype(BF16)], axis=0
    )
    mem_keys = jnp.concatenate([mk_ref[...], mk_ref[...], mem_three], axis=0)
    grads = jnp.concatenate([dm_ref[...], pick_rows(three_parts(-dc), 16).astype(BF16)], axis=0)
    values = jnp.concatenate([v_ref[...], pick_rows([ones] * 3, 16).astype(BF16)], axis=0)
    mem_values = jnp.concatenate([mv_ref[...], mem_three], axis=0)
    for at in range(0, rows, TILE):
        here = slice(at, at + TILE)
        start = at // seg_len * seg_len
        q_here, dm_here = q_ref[:, here], dm_ref[:, here]
        score = dot(mem_keys, queries[:, here], 0, 0)
        moved = dot(mem_values, grads[:, here], 0, 0)
        far = jnp.exp2(score)
        near = jnp.exp2(score + (bias_ref[:, here] + near_shift[:, here]))
        weight = far + near
        dscore = (weight * moved + near * apart[:, here]).astype(BF16)
        grad_mv = dot(dm_here, weight.astype(BF16), 1, 1)
        grad_mk = dot(q_here, dscore, 1, 1)
        dq = dot(mk_ref[...], dscore)
        if at == 0:
            dmv_ref[...] = grad_mv
            dmk_ref[...] = grad_mk
        else:
            dmv_ref[...] += grad_mv
            dmk_ref[...] += grad_mk
        for block in range(start, at + TILE, TILE):
            there = slice(block, block + TILE)
            score = dot(keys[:, there], queries[:, here], 0, 0)
            if block == at:
                score = score + causal
            weight = jnp.exp2(score)
            dscore = (weight * dot(values[:, there], grads[:, here], 0, 0)).astype(BF16)
            grad_v = dot(dm_here, weight.astype(BF16), 1, 1)
            grad_k = dot(q_here, dscore, 1, 1)
            dq = dq + dot(k_ref[:, there], dscore)
            if block == at:
                dv_ref[:, there] = grad_v
                dk_ref[:, there] = grad_k
            else:
                dv_ref[:, there] += grad_v
                dk_ref[:, there] += grad_k
        dq_ref[:, here] = (scale * dq).astype(BF16)
    dk_ref[...] *= scale
    dmk_ref[...] *= scale


def weight_kernel(
    nt_ref, memory_ref, dq_ref, dk_ref, dv_ref, dmk_ref, dmv_ref, dlogit_ref, gw_ref, back_ref
):
    width = nt_ref.shape[0]
    normed = nt_ref[...]
    back_ref[0:width, :] = dq_ref[...]
    back_ref[width : 2 * width, :] = dk_ref[...].astype(BF16)
    back_ref[2 * width : 3 * width, :] = dv_ref[...].astype(BF16)
    for part in range(3):
        grad = dot(normed, back_ref[part * width : (part + 1) * width, :], 1, 1)
        if part:
            source = (dmk_ref, dmv_ref)[part - 1][...]
            high = source.astype(BF16)
            low = (source - high.astype(F32)).astype(BF16)
            grad = grad + dot(memory_ref[...], high, 0, 1) + dot(memory_ref[...], low, 0, 1)
        gw_ref[:, part * width : (part + 1) * width] = grad.astype(BF16)
    side = jnp.concatenate([dlogit_ref[...], jnp.zeros((SIDE - 8, nt_ref.shape[1]), F32)], axis=0)
    back_ref[3 * width :, :] = side.astype(BF16)


def input_kernel(
    xt_ref, inv_ref, nt_ref, w_ref, back_ref, gh_ref, ggain_ref, gx_ref, side_ref
):
    width = xt_ref.shape[0]
    unit = xt_ref[...].astype(F32) * inv_ref[0:1, :]
    side = w_ref[:, 3 * width :].astype(F32)
    gain = side[:, 8:9]
    grad = dot(w_ref[...], back_ref[...])
    gain_grad = jnp.sum(grad * unit, axis=1, keepdims=True)
    b = grad * gain
    out = gh_ref[...] + inv_ref[0:1, :] * (b - unit * jnp.mean(b * unit, axis=0, keepdims=True))
    gx_ref[...] = out.T
    gate_grad = dot(nt_ref[...], back_ref[3 * width :, :], 1, 1)
    lane = lax.broadcasted_iota(jnp.int32, gate_grad.shape, 1)
    gate_grad = jnp.where(lane == 8, gain_grad, gate_grad)
    side_ref[...] = jnp.where(lane == 9, ggain_ref[...], gate_grad).astype(BF16)


def on_device(
    tokens,
    memory,
    lengths,
    neighbours,
    out_grad,
    gain_one,
    gain_two,
    w_query,
    w_key,
    w_value,
    w_gate,
    w_out,
    w_up,
    w_down,
    *,
    sizes,
):
    rows, width = tokens.shape
    heads = w_gate.shape[1]
    size = width // heads
    seg_count = lengths.shape[0]
    knn = neighbours.shape[1]
    shard = w_query.shape[0]
    devices = sizes["dp"] * sizes["seq"]
    ff = w_up.shape[1]
    scale = size ** (-0.5)

    steps = gather_steps(sizes)
    place = places(steps, sizes)
    packed = jnp.concatenate(
        [
            w_query,
            w_key,
            w_value,
            w_gate,
            gain_one[:, None],
            gain_two[:, None],
            jnp.zeros((shard, SIDE - heads - 2), BF16),
        ],
        axis=1,
    )
    columns = packed.shape[1]
    w_in = jnp.take(doubled(packed[None], steps, sizes), place, axis=0).reshape(width, columns)
    seq_steps = [("seq", bit) for bit in reversed(bits_of(sizes["seq"]))]
    mem_all = doubled(memory[None], seq_steps, sizes).reshape(-1, width)
    slots = mem_all.shape[0]
    up_full = lax.all_gather(jnp.concatenate([w_out, w_up], axis=1), ("dp", "seq"), axis=0, tiled=True)
    out_full = up_full[:, :width]
    up_full = up_full[:, width:]
    down_full = lax.all_gather(w_down, ("dp", "seq"), axis=0, tiled=True)

    own = memory.shape[0]
    owner = (neighbours // own) ^ lax.axis_index("seq")
    ids = neighbours % own
    for at, (_, bit) in enumerate(seq_steps):
        ids = ids + jnp.where((owner & bit) != 0, own << at, 0)
    ids = jnp.pad(ids.T, ((0, 8 - knn), (0, 0)))

    big = (width, rows)
    rowsz = (8, rows)
    xt, gt, inv_one, bias = call(
        functools.partial(prepare_kernel, count=knn),
        [(big, BF16), (big, BF16), (rowsz, F32), ((slots, rows), F32)],
    )(tokens, out_grad, ids)

    nt, qkv, mem_kv, gate = call(
        project_kernel,
        [(big, BF16), ((3 * width, rows), BF16), ((2 * width, slots), BF16), (rowsz, F32)],
        flops=2 * width * rows * columns,
    )(xt, inv_one, w_in, mem_all)

    def head_block(part, cols):
        return pl.BlockSpec((size, cols), lambda h, *_: (part * heads + h, 0))

    smem = pl.BlockSpec(memory_space=pltpu.SMEM)
    mixed, ctx, rec, lse, lsen = call(
        functools.partial(attend_kernel, seg_count=seg_count, scale=scale),
        [(big, BF16), (big, F32), (big, F32), (rowsz, F32), (rowsz, F32)],
        grid=(heads,),
        in_specs=[
            smem,
            head_block(0, rows),
            head_block(1, rows),
            head_block(2, rows),
            head_block(0, slots),
            head_block(1, slots),
            whole(rowsz),
            whole((slots, rows)),
        ],
        out_specs=[head_block(0, rows)] * 3 + [whole(rowsz)] * 2,
        flops=8 * width * rows * (slots + rows),
    )(lengths, qkv, qkv, qkv, mem_kv, mem_kv, gate, bias)

    chunks = ff // width
    (
        block_out,
        grad_hidden,
        dm,
        dc,
        dn,
        dlogit,
        ggain_two,
        gwo,
        gup,
        gdown,
    ) = call(
        functools.partial(feed_kernel, heads=heads),
        [
            ((rows, width), BF16),
            (big, F32),
            (big, BF16),
            (rowsz, F32),
            (rowsz, F32),
            (rowsz, F32),
            ((width, SIDE), F32),
            ((width, width), BF16),
            ((width, ff), BF16),
            ((ff, width), BF16),
        ],
        grid=(chunks,),
        in_specs=[
            whole(big),
            whole(big),
            whole(big),
            whole(big),
            whole(big),
            whole(rowsz),
            pl.BlockSpec((width, SIDE), lambda c: (0, 3 * width // SIDE)),
            whole((width, width)),
            pl.BlockSpec((width, width), lambda c: (0, c)),
            pl.BlockSpec((width, width), lambda c: (c, 0)),
        ],
        out_specs=[
            whole((rows, width)),
            whole(big),
            whole(big),
            whole(rowsz),
            whole(rowsz),
            whole(rowsz),
            whole((width, SIDE)),
            whole((width, width)),
            pl.BlockSpec((width, width), lambda c: (0, c)),
            pl.BlockSpec((width, width), lambda c: (c, 0)),
        ],
        scratch=[
            pltpu.VMEM(big, F32),
            pltpu.VMEM(big, BF16),
            pltpu.VMEM(big, F32),
            pltpu.VMEM(big, F32),
        ],
        flops=12 * width * rows * ff,
    )(xt, gt, mixed, ctx, rec, gate, w_in, out_full, up_full, down_full)

    order = owners(steps, sizes)

    def to_owners(grad):
        return jnp.take(grad.reshape(devices, -1, grad.shape[1]), order, axis=0)

    late = jnp.concatenate(
        [
            to_owners(gdown),
            to_owners(gwo),
            *[to_owners(gup[:, c * width : (c + 1) * width]) for c in range(chunks)],
        ],
        axis=1,
    )
    late = halved(late, steps, sizes)

    dq, dk, dv, dmk, dmv = call(
        functools.partial(attend_back_kernel, seg_count=seg_count, scale=scale),
        [(big, BF16), (big, F32), (big, F32), ((width, slots), F32), ((width, slots), F32)],
        grid=(heads,),
        in_specs=[
            smem,
            head_block(0, rows),
            head_block(1, rows),
            head_block(2, rows),
            head_block(0, slots),
            head_block(1, slots),
            head_block(0, rows),
            whole(rowsz),
            whole((slots, rows)),
            whole(rowsz),
            whole(rowsz),
            whole(rowsz),
            whole(rowsz),
        ],
        out_specs=[head_block(0, rows)] * 3 + [head_block(0, slots)] * 2,
        flops=20 * width * rows * (slots + rows),
    )(lengths, qkv, qkv, qkv, mem_kv, mem_kv, dm, gate, bias, lse, lsen, dc, dn)

    gw, back = call(
        weight_kernel,
        [((width, 3 * width), BF16), ((3 * width + SIDE, rows), BF16)],
        flops=8 * width * rows * 3 * width,
    )(nt, mem_all, dq, dk, dv, dmk, dmv, dlogit)
    grad_tokens, side = call(
        input_kernel,
        [((rows, width), F32), ((width, SIDE), BF16)],
        flops=2 * width * rows * columns,
    )(xt, inv_one, nt, w_in, back, grad_hidden, ggain_two)

    early = halved(to_owners(jnp.concatenate([gw, side], axis=1)), steps, sizes)
    per_down = w_down.shape[0]
    grad_up = jnp.concatenate(
        [
            late[per_down + shard * (1 + c) : per_down + shard * (2 + c)]
            for c in range(chunks)
        ],
        axis=1,
    )
    side = early[:, 3 * width :]
    return (
        block_out,
        grad_tokens,
        side[:, heads],
        side[:, heads + 1],
        early[:, :width],
        early[:, width : 2 * width],
        early[:, 2 * width : 3 * width],
        side[:, :heads],
        late[per_down : per_down + shard],
        grad_up,
        late[:per_down],
    )


def solution(mesh):
    row_split, vector = P(("dp", "seq"), None), P(("dp", "seq"))
    in_specs = (row_split, row_split, vector, row_split, row_split, vector, vector) + (row_split,) * 7
    out_specs = (row_split, row_split, vector, vector) + (row_split,) * 7
    return jax.shard_map(
        functools.partial(on_device, sizes=dict(mesh.shape)),
        mesh=mesh,
        in_specs=in_specs,
        out_specs=out_specs,
        check_vma=False,
    )
```

```python
import functools
import math

import jax
import jax.numpy as jnp
from jax import lax
from jax.experimental import pallas as pl
from jax.experimental.pallas import tpu as pltpu
from jax.sharding import PartitionSpec as P


EPSILON = 1e-06
MASKED = -1e30
LOG2E = math.log2(math.e)
F32 = jnp.float32
BF16 = jnp.bfloat16
VMEM_BYTES = 58 << 20
SIDE = 128
TILE = 256
ROWS = 16
TINY = 2.0**-80
PER_MICRO = 1.1e9


def dot(left, right, left_dim=1, right_dim=0):
    return lax.dot_general(
        left, right, (((left_dim,), (right_dim,)), ((), ())), preferred_element_type=F32
    )


def call(kernel, outs, in_specs, out_specs=None, grid=None, scratch=(), micros=0, vmem=VMEM_BYTES):
    options = {} if grid is None else dict(grid=grid)
    if out_specs is None:
        out_specs = [WHOLE] * len(outs)
    return pl.pallas_call(
        kernel,
        out_shape=[jax.ShapeDtypeStruct(shape, kind) for shape, kind in outs],
        in_specs=in_specs,
        out_specs=out_specs,
        scratch_shapes=list(scratch),
        compiler_params=pltpu.CompilerParams(vmem_limit_bytes=vmem),
        cost_estimate=pl.CostEstimate(
            flops=int(micros * PER_MICRO), bytes_accessed=0, transcendentals=0
        ),
        **options,
    )


WHOLE = pl.BlockSpec(memory_space=pltpu.VMEM)
SCALARS = pl.BlockSpec(memory_space=pltpu.SMEM)


def three_parts(value):
    high = value.astype(BF16).astype(F32)
    rest = value - high
    middle = rest.astype(BF16).astype(F32)
    return high, middle, rest - middle


def pick_rows(rows, count):
    shape = (count, rows[0].shape[1])
    index = lax.broadcasted_iota(jnp.int32, shape, 0)
    block = jnp.zeros(shape, F32)
    for at, row in enumerate(rows):
        block = jnp.where(index == at, row, block)
    return block


def bits_of(size):
    return [1 << b for b in reversed(range(size.bit_length() - 1))]


def groups_of(sizes):
    steps = [("dp", bit) for bit in bits_of(sizes["dp"])] + [("seq", bit) for bit in bits_of(sizes["seq"])]
    return [steps[at : at + 2] for at in range(0, len(steps), 2)]


def swap(array, group, mask, sizes):
    n_seq = sizes["seq"]
    apart = 0
    for at, (axis, bit) in enumerate(group):
        if mask >> at & 1:
            apart ^= bit * (n_seq if axis == "dp" else 1)
    pairs = [(i, i ^ apart) for i in range(sizes["dp"] * n_seq)]
    return lax.ppermute(array, ("dp", "seq"), pairs)


def gather_stage(pieces, group, sizes):
    array = jnp.concatenate(pieces, axis=0) if len(pieces) > 1 else pieces[0]
    return [array] + [swap(array, group, mask, sizes) for mask in range(1, 1 << len(group))]


def gathered(array, groups, sizes):
    pieces = [array[None]]
    for group in groups:
        pieces = gather_stage(pieces, group, sizes)
    return pieces


def sum_stage(pieces, groups, at, sizes):
    group = groups[at]
    terms = [pieces[0]] + [swap(pieces[mask], group, mask, sizes) for mask in range(1, 1 << len(group))]
    if at == 0:
        return terms
    count = 1 << len(groups[at - 1])
    step = terms[0].shape[0] // count
    return [
        sum(term[m * step : (m + 1) * step].astype(F32) for term in terms).astype(BF16)
        for m in range(count)
    ]


def summed(pieces, groups, sizes):
    for at in reversed(range(len(groups))):
        pieces = sum_stage(pieces, groups, at, sizes)
    return pieces


def after(earlier, later):
    return lax.optimization_barrier((earlier, later))


def owners(groups, sizes):
    n_seq = sizes["seq"]
    at = jnp.arange(sizes["dp"] * n_seq, dtype=jnp.int32)
    own = {"dp": lax.axis_index("dp"), "seq": lax.axis_index("seq")}
    for number, (axis, bit) in enumerate(step for group in groups for step in group):
        own[axis] = own[axis] ^ jnp.where((at >> number) & 1, bit, 0)
    return own["dp"] * n_seq + own["seq"]


def place_of(ids, own_index, group_steps):
    apart = ids ^ own_index
    place = jnp.zeros_like(ids)
    for at, (_, bit) in enumerate(group_steps):
        place = place + jnp.where((apart & bit) != 0, 1 << at, 0)
    return place


def blocks_of(pieces):
    number = 0
    for piece in pieces:
        for index in range(piece.shape[0]):
            yield number, piece, index
            number += 1


def rows_at(owner_ref, number, height):
    return pl.ds(pl.multiple_of(owner_ref[number] * height, height), height)


def prepare_kernel(x_ref, g_ref, ids_ref, xt_ref, gt_ref, inv_ref, times_ref, bias_ref, *, count):
    xt = x_ref[...].astype(F32).T
    xt_ref[...] = xt.astype(BF16)
    gt_ref[...] = g_ref[...].astype(F32).T.astype(BF16)
    inv = lax.rsqrt(jnp.mean(xt * xt, axis=0, keepdims=True) + EPSILON)
    inv_ref[...] = jnp.broadcast_to(inv, inv_ref.shape)
    slots, rows = bias_ref.shape
    step = 128

    def body(i, _):
        at = pl.multiple_of(i * step, step)
        slot = lax.broadcasted_iota(jnp.int32, (step, rows), 0) + at
        times = jnp.zeros((step, rows), F32)
        for j in range(count):
            times = times + jnp.where(ids_ref[j : j + 1, :] == slot, 1.0, 0.0)
        times_ref[pl.ds(at, step), :] = times.astype(BF16)
        bias_ref[pl.ds(at, step), :] = jnp.where(times > 0.0, jnp.log2(times), MASKED)
        return 0

    lax.fori_loop(0, slots // step, body, 0)


def local_penalty(lengths_ref, rows, seg_count):
    seg_len = rows // seg_count
    lane = lax.broadcasted_iota(jnp.int32, (1, rows), 1)
    last = jnp.zeros((1, rows), jnp.int32)
    for seg in range(seg_count):
        last = jnp.where(lane // seg_len == seg, seg * seg_len + lengths_ref[seg], last)
    return jnp.where(lane < last, 0.0, MASKED)


def causal_bias(size):
    key = lax.broadcasted_iota(jnp.int32, (size, size), 0)
    query = lax.broadcasted_iota(jnp.int32, (size, size), 1)
    return jnp.where(key <= query, 0.0, MASKED)


def longest(keys):
    keys = keys.astype(F32)
    return jnp.max(jnp.sum(keys * keys, axis=0, keepdims=True), axis=1, keepdims=True)


def attend_kernel(
    owner_ref, lengths_ref, xt_ref, inv_ref, memory_ref, times_ref, *refs,
    pieces, heads, seg_count, scale,
):
    w_pieces = refs[:pieces]
    (
        nt_ref, qkv_ref, mem_ref, side_ref, mixed_ref, ctx_ref, rec_ref, gate_ref, lse_ref, lsen_ref, w_ref
    ) = refs[pieces:]
    head = pl.program_id(0)
    width, rows = xt_ref.shape
    slots = memory_ref.shape[0]
    size = width // heads
    seg_len = rows // seg_count

    @pl.when(head == 0)
    def _():
        for number, piece, index in blocks_of(w_pieces):
            w_ref[rows_at(owner_ref, number, piece.shape[1]), :] = piece[index]
        side_ref[...] = w_ref[:, 3 * width :]
        gain = side_ref[...].astype(F32)[:, heads : heads + 1]
        normed = (xt_ref[...].astype(F32) * inv_ref[0:1, :] * gain).astype(BF16)
        nt_ref[...] = normed
        for part in range(3):
            columns = slice(part * width, (part + 1) * width)
            qkv_ref[columns, :] = dot(w_ref[:, columns], normed, 0, 0).astype(BF16)
        gate_ref[...] = jax.nn.sigmoid(dot(side_ref[...], normed, 0, 0)[0:heads])
        for part in range(2):
            columns = slice((part + 1) * width, (part + 2) * width)
            mem_ref[part * width : (part + 1) * width, :] = dot(
                w_ref[:, columns], memory_ref[...], 0, 1
            ).astype(BF16)

    def head_of(ref, part):
        return ref[pl.ds(pl.multiple_of(part * width + head * size, size), size), :]

    q, k, v = (head_of(qkv_ref, part) for part in range(3))
    mk, mv = (head_of(mem_ref, part) for part in range(2))
    gate = gate_ref[pl.ds(head, 1), :]
    penalty = local_penalty(lengths_ref, rows, seg_count)
    causal = causal_bias(TILE)
    q = q.astype(F32) * (scale * LOG2E)
    q_high = q.astype(BF16)
    q_low = (q - q_high.astype(F32)).astype(BF16)
    reach = jnp.sqrt(
        jnp.sum(q * q, axis=0, keepdims=True) * jnp.maximum(longest(k), longest(mk))
    ) * (1.0 + 2.0**-10)
    ones = jnp.ones((1, rows), F32)
    mem_three = pick_rows([jnp.ones((1, slots), F32)] * 3, 16).astype(BF16)
    queries = jnp.concatenate(
        [q_high, q_low, pick_rows([*three_parts(-reach), ones], 16).astype(BF16)], axis=0
    )
    keys = jnp.concatenate([k, k, pick_rows([ones, ones, ones, penalty], 16).astype(BF16)], axis=0)
    mem_keys = jnp.concatenate([mk, mk, mem_three], axis=0)
    values = jnp.concatenate([v, jnp.ones((16, rows), BF16)], axis=0)
    mem_values = jnp.concatenate([mv, jnp.ones((16, slots), BF16)], axis=0)

    def finish(here, total, near_total, peak, near_peak):
        mass, near_mass = total[size : size + 1], near_total[size : size + 1]
        context = total[:size] / mass
        recalled = near_total[:size] / near_mass
        ctx_ref[:, here] = context
        rec_ref[:, here] = recalled
        lse_ref[pl.ds(head, 1), here] = peak + jnp.log2(mass)
        lsen_ref[pl.ds(head, 1), here] = near_peak + jnp.log2(near_mass)
        share = gate[:, here]
        mixed_ref[:, here] = ((1.0 - share) * context + share * recalled).astype(BF16)
        return jnp.minimum(mass, near_mass)

    least = jnp.full((1, TILE), 1.0, F32)
    for at in range(0, rows, TILE):
        here = slice(at, at + TILE)
        start = at // seg_len * seg_len
        exp_mem = jnp.exp2(dot(mem_keys, queries[:, here], 0, 0)).astype(BF16)
        total = dot(mem_values, exp_mem)
        near_total = dot(mem_values, exp_mem * times_ref[:, here])
        score_loc = dot(keys[:, start : at + TILE], queries[:, here], 0, 0)
        exp_diag = jnp.exp2(score_loc[at - start :] + causal).astype(BF16)
        total = total + dot(values[:, at : at + TILE], exp_diag)
        if at > start:
            exp_loc = jnp.exp2(score_loc[: at - start]).astype(BF16)
            total = total + dot(values[:, start:at], exp_loc)
        least = jnp.minimum(
            least, finish(here, total, near_total, reach[:, here], reach[:, here])
        )

    @pl.when(jnp.logical_not(jnp.min(least) > TINY))
    def _():
        for at in range(0, rows, TILE):
            here = slice(at, at + TILE)
            start = at // seg_len * seg_len
            score_mem = dot(mem_keys[: 2 * size], queries[: 2 * size, here], 0, 0)
            score_loc = dot(keys[: 2 * size, start : at + TILE], queries[: 2 * size, here], 0, 0)
            allowed = dot(keys[2 * size + 3 :, start : at + TILE], queries[2 * size + 3 :, here], 0, 0)
            score_loc = score_loc + allowed
            diagonal = score_loc[at - start :] + causal
            peak = jnp.maximum(
                jnp.max(score_mem, axis=0, keepdims=True), jnp.max(diagonal, axis=0, keepdims=True)
            )
            if at > start:
                peak = jnp.maximum(peak, jnp.max(score_loc[: at - start], axis=0, keepdims=True))
            near = jnp.where(times_ref[:, here] > 0, score_mem, MASKED)
            near_peak = jnp.max(near, axis=0, keepdims=True)
            total = dot(mem_values, jnp.exp2(score_mem - peak).astype(BF16))
            total = total + dot(values[:, at : at + TILE], jnp.exp2(diagonal - peak).astype(BF16))
            if at > start:
                exp_loc = jnp.exp2(score_loc[: at - start] - peak).astype(BF16)
                total = total + dot(values[:, start:at], exp_loc)
            exp_near = jnp.exp2(near - near_peak).astype(BF16) * times_ref[:, here]
            finish(here, total, dot(mem_values, exp_near), peak, near_peak)


def feed_kernel(
    owner_ref, xt_ref, gt_ref, mixed_ref, ctx_ref, rec_ref, gate_ref, side_ref, *refs, heads, pieces
):
    w_pieces = refs[:pieces]
    block_ref, gh_ref, dm_ref, dc_ref, dn_ref, dlogit_ref, ggain_ref = refs[pieces : pieces + 7]
    g_pieces = refs[pieces + 7 : 2 * pieces + 7]
    wo_ref, up_ref, down_ref, gwo_ref, gup_ref, gdown_ref = refs[2 * pieces + 7 :]
    width, rows = xt_ref.shape
    chunks = up_ref.shape[1] // width
    size = width // heads
    low = down_ref.shape[0] // width * ROWS
    for number, piece, index in blocks_of(w_pieces):
        block = piece[index]
        down_ref[rows_at(owner_ref, number, low), :] = block[:low]
        here = rows_at(owner_ref, number, ROWS)
        wo_ref[here, :] = block[low : low + ROWS]
        for chunk in range(chunks):
            at = low + (chunk + 1) * ROWS
            up_ref[here, chunk * width : (chunk + 1) * width] = block[at : at + ROWS]

    gain = side_ref[...].astype(F32)[:, heads + 1 : heads + 2]
    hidden = xt_ref[...].astype(F32) + dot(wo_ref[...], mixed_ref[...], 0, 0)
    inv = lax.rsqrt(jnp.mean(hidden * hidden, axis=0, keepdims=True) + EPSILON)
    unit = hidden * inv
    n2 = (unit * gain).astype(BF16)
    grad = gt_ref[...]
    coef = math.sqrt(2.0 / math.pi)

    def first(chunk):
        part = slice(chunk * width, (chunk + 1) * width)
        return dot(up_ref[:, part], n2, 0, 0), dot(down_ref[part, :], grad)

    def second(pre, grad_act):
        square = pre * pre
        half = 0.5 + 0.5 * jnp.tanh(pre * (coef + (0.044715 * coef) * square))
        act = pre * half
        slope = half + act * (1.0 - half) * (2.0 * coef + (6.0 * 0.044715 * coef) * square)
        return act.astype(BF16), (grad_act * slope).astype(BF16)

    ready = first(0)
    out = gn2 = None
    for chunk in range(chunks):
        part = slice(chunk * width, (chunk + 1) * width)
        later = first(chunk + 1) if chunk + 1 < chunks else None
        act, grad_pre = second(*ready)
        ready = later
        out_part = dot(down_ref[part, :], act, 0, 0)
        gn2_part = dot(up_ref[:, part], grad_pre)
        out = out_part if out is None else out + out_part
        gn2 = gn2_part if gn2 is None else gn2 + gn2_part
        gdown_ref[part, :] = dot(act, grad, 1, 1).astype(BF16)
        gup_ref[:, part] = dot(n2, grad_pre, 1, 1).astype(BF16)

    block_ref[...] = (hidden + out).T.astype(BF16)
    ggain_ref[...] = jnp.broadcast_to(jnp.sum(gn2 * unit, axis=1, keepdims=True), ggain_ref.shape)
    a = gn2 * gain
    grad_hidden = grad.astype(F32) + inv * (a - unit * jnp.mean(a * unit, axis=0, keepdims=True))
    gh_ref[...] = grad_hidden
    branch = grad_hidden.astype(BF16)
    gwo_ref[...] = dot(mixed_ref[...], branch, 1, 1).astype(BF16)
    for number, piece, index in blocks_of(g_pieces):
        piece[index, :low] = gdown_ref[rows_at(owner_ref, number, low), :]
        here = rows_at(owner_ref, number, ROWS)
        piece[index, low : low + ROWS] = gwo_ref[here, :]
        for chunk in range(chunks):
            at = low + (chunk + 1) * ROWS
            piece[index, at : at + ROWS] = gup_ref[here, chunk * width : (chunk + 1) * width]
    grad_mixed = dot(wo_ref[...], branch)
    rounded = grad_mixed.astype(BF16)
    dm_ref[...] = rounded
    rounded = rounded.astype(F32)
    for head in range(heads):
        part = slice(head * size, (head + 1) * size)
        ctx, rec = ctx_ref[part, :], rec_ref[part, :]
        dc_ref[head : head + 1, :] = jnp.sum(rounded[part] * ctx, axis=0, keepdims=True)
        dn_ref[head : head + 1, :] = jnp.sum(rounded[part] * rec, axis=0, keepdims=True)
        share = gate_ref[head : head + 1, :]
        moved = jnp.sum(grad_mixed[part] * (rec - ctx), axis=0, keepdims=True)
        dlogit_ref[head : head + 1, :] = moved * share * (1.0 - share)


def attend_back_kernel(
    lengths_ref, q_ref, k_ref, v_ref, mk_ref, mv_ref, dm_ref, gate_ref, bias_ref,
    lse_ref, lsen_ref, dc_ref, dn_ref,
    dq_ref, dk_ref, dv_ref, dmk_ref, dmv_ref,
    dk_sum, dv_sum, dmk_sum, dmv_sum,
    *, first, seg_count, scale,
):
    size, rows = q_ref.shape
    seg_len = rows // seg_count
    penalty = local_penalty(lengths_ref, rows, seg_count)
    causal = causal_bias(TILE)
    q = q_ref[...].astype(F32) * (scale * LOG2E)
    q_high = q.astype(BF16)
    q_low = (q - q_high.astype(F32)).astype(BF16)
    row = pl.ds(pl.program_id(0) + first, 1)
    share = gate_ref[row, :]
    shift = jnp.log2(jnp.maximum(1.0 - share, 2.0**-60)) - lse_ref[row, :]
    near_shift = jnp.log2(jnp.maximum(share, 2.0**-60)) - lsen_ref[row, :] - shift
    dc = dc_ref[row, :]
    apart = dc - dn_ref[row, :]
    ones = jnp.ones((1, rows), F32)
    mem_three = pick_rows([jnp.ones((1, mk_ref.shape[1]), F32)] * 3, 16).astype(BF16)
    queries = jnp.concatenate(
        [q_high, q_low, pick_rows([*three_parts(shift), ones], 16).astype(BF16)], axis=0
    )
    keys = jnp.concatenate(
        [k_ref[...], k_ref[...], pick_rows([ones, ones, ones, penalty], 16).astype(BF16)], axis=0
    )
    mem_keys = jnp.concatenate([mk_ref[...], mk_ref[...], mem_three], axis=0)
    grads = jnp.concatenate([dm_ref[...], pick_rows(three_parts(-dc), 16).astype(BF16)], axis=0)
    values = jnp.concatenate([v_ref[...], pick_rows([ones] * 3, 16).astype(BF16)], axis=0)
    mem_values = jnp.concatenate([mv_ref[...], mem_three], axis=0)
    for at in range(0, rows, TILE):
        here = slice(at, at + TILE)
        start = at // seg_len * seg_len
        q_here, dm_here = q_ref[:, here], dm_ref[:, here]
        score = dot(mem_keys, queries[:, here], 0, 0)
        moved = dot(mem_values, grads[:, here], 0, 0)
        far = jnp.exp2(score)
        near = jnp.exp2(score + (bias_ref[:, here] + near_shift[:, here]))
        weight = far + near
        dscore = (weight * moved + near * apart[:, here]).astype(BF16)
        grad_mv = dot(dm_here, weight.astype(BF16), 1, 1)
        grad_mk = dot(q_here, dscore, 1, 1)
        dq = dot(mk_ref[...], dscore)
        if at == 0:
            dmv_sum[...] = grad_mv
            dmk_sum[...] = grad_mk
        else:
            dmv_sum[...] += grad_mv
            dmk_sum[...] += grad_mk
        for block in range(start, at + TILE, TILE):
            there = slice(block, block + TILE)
            score = dot(keys[:, there], queries[:, here], 0, 0)
            if block == at:
                score = score + causal
            weight = jnp.exp2(score)
            dscore = (weight * dot(values[:, there], grads[:, here], 0, 0)).astype(BF16)
            grad_v = dot(dm_here, weight.astype(BF16), 1, 1)
            grad_k = dot(q_here, dscore, 1, 1)
            dq = dq + dot(k_ref[:, there], dscore)
            if block == at:
                dv_sum[:, there] = grad_v
                dk_sum[:, there] = grad_k
            else:
                dv_sum[:, there] += grad_v
                dk_sum[:, there] += grad_k
        dq_ref[:, here] = (scale * dq).astype(BF16)
    dk_ref[...] = (scale * dk_sum[...]).astype(BF16)
    dv_ref[...] = dv_sum[...].astype(BF16)
    dmk_ref[...] = (scale * dmk_sum[...]).astype(BF16)
    dmv_ref[...] = dmv_sum[...].astype(BF16)


def weight_kernel(
    owner_ref, nt_ref, memory_ref, side_ref, dlogit_ref, ggain_ref, *refs, calls, pieces, heads, w_count
):
    backs = [refs[5 * at : 5 * at + 5] for at in range(calls)]
    refs = refs[5 * calls :]
    w_pieces, refs = refs[:w_count], refs[w_count:]
    g_pieces, (back_ref, gw_ref) = refs[:pieces], refs[pieces:]
    width, rows = nt_ref.shape
    normed = nt_ref[...]
    for part in range(3):
        at = part * width
        for back in backs:
            back_ref[at : at + back[part].shape[0], :] = back[part][...]
            at += back[part].shape[0]
    side = jnp.concatenate([dlogit_ref[...], jnp.zeros((SIDE - heads, rows), F32)], axis=0)
    back_ref[3 * width :, :] = side.astype(BF16)
    for part in range(3):
        columns = slice(part * width, (part + 1) * width)
        gw_ref[:, columns] = dot(normed, back_ref[columns, :], 1, 1)
    gw_ref[:, 3 * width :] = dot(normed, back_ref[3 * width :, :], 1, 1)
    by_rows = []
    for number, piece, index in blocks_of(w_pieces):
        here = rows_at(owner_ref, number, ROWS)
        by_rows.append((here, jnp.sum(piece[index].astype(F32) * gw_ref[here, :], axis=1, keepdims=True)))
    lane = lax.broadcasted_iota(jnp.int32, (ROWS, SIDE), 1)
    for here, total in by_rows:
        gain = side_ref[here, :].astype(F32)[:, heads : heads + 1]
        block = jnp.where(lane == heads, total / gain, gw_ref[here, 3 * width :])
        gw_ref[here, 3 * width :] = jnp.where(lane == heads + 1, ggain_ref[here, :], block)
    for part in range(1, 3):
        at = part * width
        for back in backs:
            source = back[part + 2]
            gw_ref[:, at : at + source.shape[0]] += dot(memory_ref[...], source[...], 0, 1)
            at += source.shape[0]
    for number, piece, index in blocks_of(g_pieces):
        piece[index] = gw_ref[rows_at(owner_ref, number, ROWS), :].astype(BF16)


def input_kernel(owner_ref, xt_ref, inv_ref, side_ref, back_ref, gh_ref, *refs, heads):
    w_pieces, (gx_ref, w_ref) = refs[:-2], refs[-2:]
    for number, piece, index in blocks_of(w_pieces):
        w_ref[rows_at(owner_ref, number, ROWS), :] = piece[index]
    unit = xt_ref[...].astype(F32) * inv_ref[0:1, :]
    gain = side_ref[...].astype(F32)[:, heads : heads + 1]
    b = dot(w_ref[...], back_ref[...]) * gain
    out = gh_ref[...] + inv_ref[0:1, :] * (b - unit * jnp.mean(b * unit, axis=0, keepdims=True))
    gx_ref[...] = out.T


def on_device(
    tokens,
    memory,
    lengths,
    neighbours,
    out_grad,
    gain_one,
    gain_two,
    w_query,
    w_key,
    w_value,
    w_gate,
    w_out,
    w_up,
    w_down,
    *,
    sizes,
):
    rows, width = tokens.shape
    heads = w_gate.shape[1]
    size = width // heads
    seg_count = lengths.shape[0]
    knn = neighbours.shape[1]
    shard = w_query.shape[0]
    ff = w_up.shape[1]
    chunks = ff // width
    tall = w_down.shape[0]
    scale = size ** (-0.5)
    own = memory.shape[0]
    slots = own * sizes["seq"]
    blocks = width // ROWS
    low = ff // blocks

    groups = groups_of(sizes)
    owner = owners(groups, sizes)
    direct = shard == ROWS
    kernel_owner = owner if direct else jnp.arange(blocks, dtype=jnp.int32)

    packed = jnp.concatenate(
        [
            w_query,
            w_key,
            w_value,
            w_gate,
            gain_one[:, None],
            gain_two[:, None],
            jnp.zeros((shard, SIDE - heads - 2), BF16),
        ],
        axis=1,
    )
    columns = packed.shape[1]
    seq_group = [("seq", bit) for bit in bits_of(sizes["seq"])]
    mem_all = gathered(memory, [seq_group[:1], seq_group[1:]], sizes)
    mem_all = jnp.concatenate(mem_all, axis=0).reshape(slots, width)
    w_pieces = gathered(packed, groups, sizes)
    feed_packed = jnp.concatenate(
        [w_down, w_out] + [w_up[:, c * width : (c + 1) * width] for c in range(chunks)], axis=0
    )
    feed_pieces = [feed_packed[None]]
    for group in groups[:-1]:
        feed_pieces = gather_stage(feed_pieces, group, sizes)

    def in_order(pieces):
        both = jnp.concatenate(pieces, axis=0)
        return jnp.zeros_like(both).at[owner].set(both)

    def split_rows(array, *heights):
        at, parts = 0, []
        for height in heights:
            parts.append(array[:, at : at + height].reshape(-1, width))
            at += height
        return parts

    if not direct:
        w_pieces = [in_order(w_pieces).reshape(blocks, ROWS, columns)]

    def to_send(pieces, *heights):
        if direct:
            return pieces
        array = pieces[0]
        if len(heights) > 1:
            parts = split_rows(array, low, *[ROWS] * (len(heights) - 1))
            parts = [part.reshape(-1, height, width) for part, height in zip(parts, heights)]
            array = jnp.concatenate(parts, axis=1)
        else:
            array = array.reshape(-1, heights[0], array.shape[2])
        array = array[owner]
        count = 1 << len(groups[-1])
        return jnp.split(array, count, axis=0)

    ids = neighbours // own
    ids = place_of(ids, lax.axis_index("seq"), seq_group) * own + neighbours % own
    ids = jnp.pad(ids.T, ((0, 8 - knn), (0, 0)))

    big = (width, rows)
    lanes = (8, rows)
    xt, gt, inv_one, times, bias = call(
        functools.partial(prepare_kernel, count=knn),
        [(big, BF16), (big, BF16), (lanes, F32), ((slots, rows), BF16), ((slots, rows), F32)],
        [WHOLE] * 3,
        micros=7,
    )(tokens, out_grad, ids)

    def head_block(part, cols, first=0):
        return pl.BlockSpec((size, cols), lambda h: (part * heads + first + h, 0))

    nt, qkv, mem_kv, side, mixed, ctx, rec, gate, lse, lsen = call(
        functools.partial(
            attend_kernel, pieces=len(w_pieces), heads=heads, seg_count=seg_count, scale=scale
        ),
        [
            (big, BF16),
            ((3 * width, rows), BF16),
            ((2 * width, slots), BF16),
            ((width, SIDE), BF16),
            (big, BF16),
            (big, F32),
            (big, F32),
            (lanes, F32),
            (lanes, F32),
            (lanes, F32),
        ],
        [SCALARS, SCALARS] + [WHOLE] * (4 + len(w_pieces)),
        out_specs=[WHOLE] * 4 + [head_block(0, rows)] * 3 + [WHOLE] * 3,
        grid=(heads,),
        scratch=[pltpu.VMEM((width, columns), BF16)],
        micros=30,
    )(kernel_owner, lengths, xt, inv_one, mem_all, times, *w_pieces)

    mixed, feed_pieces = after(mixed, feed_pieces)
    feed_pieces = gather_stage(feed_pieces, groups[-1], sizes)
    if not direct:
        parts = split_rows(in_order(feed_pieces), tall, *[shard] * (1 + chunks))
        feed_pieces = [jnp.concatenate([part.reshape(blocks, -1, width) for part in parts], axis=1)]
    pieces = len(feed_pieces)
    feed_block = (blocks // pieces,) + feed_pieces[0].shape[1:]
    outs = call(
        functools.partial(feed_kernel, heads=heads, pieces=pieces),
        [
            ((rows, width), BF16),
            (big, F32),
            (big, BF16),
            (lanes, F32),
            (lanes, F32),
            (lanes, F32),
            ((width, SIDE), F32),
        ]
        + [(feed_block, BF16)] * pieces,
        [SCALARS] + [WHOLE] * (7 + pieces),
        scratch=[
            pltpu.VMEM(shape, BF16)
            for shape in ((width, width), (width, ff), (ff, width)) * 2
        ],
        micros=25,
    )(kernel_owner, xt, gt, mixed, ctx, rec, gate, side, *feed_pieces)
    block_out, grad_hidden, dm, dc, dn, dlogit, ggain_two = outs[:7]
    late = to_send(outs[7:], tall, *[shard] * (1 + chunks))
    late_at = len(groups)

    backs = []
    first = 0
    for count in (2, heads - 2):
        late_at -= 1
        moving = sum_stage(late, groups, late_at, sizes)
        outs = call(
            functools.partial(attend_back_kernel, first=first, seg_count=seg_count, scale=scale),
            [((size * count, rows), BF16)] * 3 + [((size * count, slots), BF16)] * 2,
            [
                SCALARS,
                head_block(0, rows, first),
                head_block(1, rows, first),
                head_block(2, rows, first),
                head_block(0, slots, first),
                head_block(1, slots, first),
                head_block(0, rows, first),
            ]
            + [WHOLE] * 6,
            out_specs=[head_block(0, rows)] * 3 + [head_block(0, slots)] * 2,
            grid=(count,),
            scratch=[pltpu.VMEM((size, rows), F32)] * 2 + [pltpu.VMEM((size, slots), F32)] * 2,
            micros=5 * count,
        )(lengths, qkv, qkv, qkv, mem_kv, mem_kv, dm, gate, bias, lse, lsen, dc, dn)
        first += count
        late, (outs, dm) = after(moving, (outs, dm))
        backs.append(outs)

    late = summed(late, groups[:late_at], sizes)
    pieces = len(w_pieces)
    *early, back = call(
        functools.partial(
            weight_kernel, calls=len(backs), pieces=pieces, heads=heads, w_count=pieces
        ),
        [((blocks // pieces, ROWS, columns), BF16)] * pieces + [((columns, rows), BF16)],
        [SCALARS] + [WHOLE] * (5 + 5 * len(backs) + pieces),
        scratch=[pltpu.VMEM((width, columns), F32)],
        micros=9,
    )(kernel_owner, nt, mem_all, side, dlogit, ggain_two, *[b for back in backs for b in back], *w_pieces)
    early = summed(to_send(early, shard), groups, sizes)
    (grad_tokens,) = call(
        functools.partial(input_kernel, heads=heads),
        [((rows, width), F32)],
        [SCALARS] + [WHOLE] * (5 + pieces),
        scratch=[pltpu.VMEM((width, columns), BF16)],
        micros=7,
    )(kernel_owner, xt, inv_one, side, back, grad_hidden, *w_pieces)

    late = sum(term[0].astype(F32) for term in late)
    early = sum(term[0].astype(F32) for term in early)
    grad_up = jnp.concatenate(
        [late[tall + shard * (1 + c) : tall + shard * (2 + c)] for c in range(chunks)], axis=1
    )
    side = early[:, 3 * width :]
    return (
        block_out,
        grad_tokens,
        side[:, heads],
        side[:, heads + 1],
        early[:, :width],
        early[:, width : 2 * width],
        early[:, 2 * width : 3 * width],
        side[:, :heads],
        late[tall : tall + shard],
        grad_up,
        late[:tall],
    )


def solution(mesh):
    row_split, vector = P(("dp", "seq"), None), P(("dp", "seq"))
    in_specs = (row_split, row_split, vector, row_split, row_split, vector, vector) + (row_split,) * 7
    out_specs = (row_split, row_split, vector, vector) + (row_split,) * 7
    return jax.shard_map(
        functools.partial(on_device, sizes=dict(mesh.shape)),
        mesh=mesh,
        in_specs=in_specs,
        out_specs=out_specs,
        check_vma=False,
    )
```

```python
import functools
import math

import jax
import jax.numpy as jnp
from jax import lax
from jax.experimental import pallas as pl
from jax.experimental.pallas import tpu as pltpu
from jax.sharding import PartitionSpec as P


EPSILON = 1e-06
MASKED = -1e30
LOG2E = math.log2(math.e)
F32 = jnp.float32
BF16 = jnp.bfloat16
SIDE = 128
TILE = 256
ROWS = 16
TINY = 2.0**-80
PER_MICRO = 1.1e9


def dot(left, right, left_dim=1, right_dim=0):
    return lax.dot_general(
        left, right, (((left_dim,), (right_dim,)), ((), ())), preferred_element_type=F32
    )


def call(kernel, outs, in_specs, out_specs=None, grid=None, scratch=(), micros=0, vmem=16):
    options = {} if grid is None else dict(grid=grid)
    if out_specs is None:
        out_specs = [WHOLE] * len(outs)
    return pl.pallas_call(
        kernel,
        out_shape=[jax.ShapeDtypeStruct(shape, kind) for shape, kind in outs],
        in_specs=in_specs,
        out_specs=out_specs,
        scratch_shapes=list(scratch),
        compiler_params=pltpu.CompilerParams(vmem_limit_bytes=vmem << 20),
        cost_estimate=pl.CostEstimate(
            flops=int(micros * PER_MICRO), bytes_accessed=0, transcendentals=0
        ),
        **options,
    )


WHOLE = pl.BlockSpec(memory_space=pltpu.VMEM)
SCALARS = pl.BlockSpec(memory_space=pltpu.SMEM)


def three_parts(value):
    high = value.astype(BF16).astype(F32)
    rest = value - high
    middle = rest.astype(BF16).astype(F32)
    return high, middle, rest - middle


def pick_rows(rows, count):
    shape = (count, rows[0].shape[1])
    index = lax.broadcasted_iota(jnp.int32, shape, 0)
    block = jnp.zeros(shape, F32)
    for at, row in enumerate(rows):
        block = jnp.where(index == at, row, block)
    return block


def bits_of(size):
    return [1 << b for b in reversed(range(size.bit_length() - 1))]


def groups_of(sizes):
    steps = [("dp", bit) for bit in bits_of(sizes["dp"])] + [("seq", bit) for bit in bits_of(sizes["seq"])]
    return [steps[at : at + 2] for at in range(0, len(steps), 2)]


def swap(array, group, mask, sizes):
    n_seq = sizes["seq"]
    apart = 0
    for at, (axis, bit) in enumerate(group):
        if mask >> at & 1:
            apart ^= bit * (n_seq if axis == "dp" else 1)
    pairs = [(i, i ^ apart) for i in range(sizes["dp"] * n_seq)]
    return lax.ppermute(array, ("dp", "seq"), pairs)


def gather_stage(pieces, group, sizes, join=True):
    if join and len(pieces) > 1:
        pieces = [jnp.concatenate(pieces, axis=0)]
    masks = range(1, 1 << len(group))
    return pieces + [swap(piece, group, mask, sizes) for mask in masks for piece in pieces]


def sum_stage(pieces, groups, at, sizes):
    group = groups[at]
    terms = [pieces[0]] + [swap(pieces[mask], group, mask, sizes) for mask in range(1, 1 << len(group))]
    if at == 0:
        return terms
    count = 1 << len(groups[at - 1])
    step = terms[0].shape[0] // count
    return [
        sum(term[m * step : (m + 1) * step].astype(F32) for term in terms).astype(BF16)
        for m in range(count)
    ]


def after(earlier, later):
    return lax.optimization_barrier((earlier, later))


def owners(groups, sizes):
    n_seq = sizes["seq"]
    at = jnp.arange(sizes["dp"] * n_seq, dtype=jnp.int32)
    own = {"dp": lax.axis_index("dp"), "seq": lax.axis_index("seq")}
    for number, (axis, bit) in enumerate(step for group in groups for step in group):
        own[axis] = own[axis] ^ jnp.where((at >> number) & 1, bit, 0)
    return own["dp"] * n_seq + own["seq"]


def place_of(ids, own_index, group_steps):
    apart = ids ^ own_index
    place = jnp.zeros_like(ids)
    for at, (_, bit) in enumerate(group_steps):
        place = place + jnp.where((apart & bit) != 0, 1 << at, 0)
    return place


def blocks_of(pieces):
    number = 0
    for piece in pieces:
        for index in range(piece.shape[0]):
            yield number, piece, index
            number += 1


def rows_at(owner_ref, number, height):
    return pl.ds(pl.multiple_of(owner_ref[number] * height, height), height)


def pack_kernel(q_ref, k_ref, v_ref, gate_ref, one_ref, two_ref, out_ref):
    height, width = q_ref.shape
    heads = gate_ref.shape[1]
    for part, ref in enumerate((q_ref, k_ref, v_ref)):
        out_ref[:, part * width : (part + 1) * width] = ref[...]
    row = lax.broadcasted_iota(jnp.int32, (height, height), 0)
    column = lax.broadcasted_iota(jnp.int32, (height, height), 1)
    lane = lax.broadcasted_iota(jnp.int32, (height, SIDE), 1)
    gate = gate_ref[...].astype(F32)
    side = jnp.concatenate([gate, jnp.zeros((height, SIDE - heads), F32)], axis=1)
    for at, ref in enumerate((one_ref, two_ref)):
        gains = jnp.where(row == column, ref[...].astype(F32), 0.0)
        side = jnp.where(lane == heads + at, jnp.sum(gains, axis=1, keepdims=True), side)
    out_ref[:, 3 * width :] = side.astype(BF16)


def prepare_kernel(
    x_ref, g_ref, ids_ref, down_ref, wo_ref, up_ref,
    xt_ref, gt_ref, inv_ref, times_ref, bias_ref, feed_ref,
    *, count,
):
    low, width = down_ref.shape
    height = wo_ref.shape[0]
    feed_ref[:low, :] = down_ref[...]
    feed_ref[low : low + height, :] = wo_ref[...]
    for chunk in range(up_ref.shape[1] // width):
        at = low + (chunk + 1) * height
        feed_ref[at : at + height, :] = up_ref[:, chunk * width : (chunk + 1) * width]
    xt = x_ref[...].astype(F32).T
    xt_ref[...] = xt.astype(BF16)
    gt_ref[...] = g_ref[...].astype(F32).T.astype(BF16)
    inv = lax.rsqrt(jnp.mean(xt * xt, axis=0, keepdims=True) + EPSILON)
    inv_ref[...] = jnp.broadcast_to(inv, inv_ref.shape)
    slots, rows = bias_ref.shape
    step = 128

    def body(i, _):
        at = pl.multiple_of(i * step, step)
        slot = lax.broadcasted_iota(jnp.int32, (step, rows), 0) + at
        times = jnp.zeros((step, rows), F32)
        for j in range(count):
            times = times + jnp.where(ids_ref[j : j + 1, :] == slot, 1.0, 0.0)
        times_ref[pl.ds(at, step), :] = times.astype(BF16)
        bias_ref[pl.ds(at, step), :] = jnp.where(times > 0.0, jnp.log2(times), MASKED)
        return 0

    lax.fori_loop(0, slots // step, body, 0)


def local_penalty(lengths_ref, rows, seg_count):
    seg_len = rows // seg_count
    lane = lax.broadcasted_iota(jnp.int32, (1, rows), 1)
    last = jnp.zeros((1, rows), jnp.int32)
    for seg in range(seg_count):
        last = jnp.where(lane // seg_len == seg, seg * seg_len + lengths_ref[seg], last)
    return jnp.where(lane < last, 0.0, MASKED)


def causal_bias(size):
    key = lax.broadcasted_iota(jnp.int32, (size, size), 0)
    query = lax.broadcasted_iota(jnp.int32, (size, size), 1)
    return jnp.where(key <= query, 0.0, MASKED)


def longest(keys):
    keys = keys.astype(F32)
    return jnp.max(jnp.sum(keys * keys, axis=0, keepdims=True), axis=1, keepdims=True)


def attend_kernel(
    owner_ref, lengths_ref, xt_ref, inv_ref, times_ref, *refs,
    pieces, mem_pieces, heads, seg_count, scale,
):
    w_pieces, memory, refs = refs[:pieces], refs[pieces : pieces + mem_pieces], refs[mem_pieces:]
    (
        nt_ref, qkv_ref, mem_ref, side_ref, mixed_ref, ctx_ref, rec_ref, gate_ref, lse_ref, lsen_ref, w_ref
    ) = refs[pieces:]
    head = pl.program_id(0)
    width, rows = xt_ref.shape
    slots = times_ref.shape[0]
    size = width // heads
    seg_len = rows // seg_count

    @pl.when(head == 0)
    def _():
        for number, piece, index in blocks_of(w_pieces):
            w_ref[rows_at(owner_ref, number, piece.shape[1]), :] = piece[index]
        side_ref[...] = w_ref[:, 3 * width :]
        gain = side_ref[...].astype(F32)[:, heads : heads + 1]
        normed = (xt_ref[...].astype(F32) * inv_ref[0:1, :] * gain).astype(BF16)
        nt_ref[...] = normed
        for part in range(3):
            columns = slice(part * width, (part + 1) * width)
            qkv_ref[columns, :] = dot(w_ref[:, columns], normed, 0, 0).astype(BF16)
        gate_ref[...] = jax.nn.sigmoid(dot(side_ref[...], normed, 0, 0)[0:heads])
        for part in range(2):
            columns = slice((part + 1) * width, (part + 2) * width)
            for at, piece in enumerate(memory):
                own = piece.shape[1]
                mem_ref[part * width : (part + 1) * width, at * own : (at + 1) * own] = dot(
                    w_ref[:, columns], piece[0], 0, 1
                ).astype(BF16)

    def head_of(ref, part):
        return ref[pl.ds(pl.multiple_of(part * width + head * size, size), size), :]

    q, k, v = (head_of(qkv_ref, part) for part in range(3))
    mk, mv = (head_of(mem_ref, part) for part in range(2))
    gate = gate_ref[pl.ds(head, 1), :]
    penalty = local_penalty(lengths_ref, rows, seg_count)
    causal = causal_bias(seg_len)
    q = q.astype(F32) * (scale * LOG2E)
    q_high = q.astype(BF16)
    q_low = (q - q_high.astype(F32)).astype(BF16)
    reach = jnp.sqrt(
        jnp.sum(q * q, axis=0, keepdims=True) * jnp.maximum(longest(k), longest(mk))
    ) * (1.0 + 2.0**-10)
    ones = jnp.ones((1, rows), F32)
    mem_three = pick_rows([jnp.ones((1, slots), F32)] * 3, 16).astype(BF16)
    queries = jnp.concatenate(
        [q_high, q_low, pick_rows([*three_parts(-reach), ones], 16).astype(BF16)], axis=0
    )
    keys = jnp.concatenate([k, k, pick_rows([ones, ones, ones, penalty], 16).astype(BF16)], axis=0)
    mem_keys = jnp.concatenate([mk, mk, mem_three], axis=0)
    values = jnp.concatenate([v, jnp.ones((16, rows), BF16)], axis=0)
    mem_values = jnp.concatenate([mv, jnp.ones((16, slots), BF16)], axis=0)

    def finish(here, total, near_total, peak, near_peak):
        mass, near_mass = total[size : size + 1], near_total[size : size + 1]
        context = total[:size] / mass
        recalled = near_total[:size] / near_mass
        ctx_ref[:, here] = context
        rec_ref[:, here] = recalled
        lse_ref[pl.ds(head, 1), here] = peak + jnp.log2(mass)
        lsen_ref[pl.ds(head, 1), here] = near_peak + jnp.log2(near_mass)
        share = gate[:, here]
        mixed_ref[:, here] = ((1.0 - share) * context + share * recalled).astype(BF16)
        return jnp.minimum(mass, near_mass)

    segments = [slice(at, at + seg_len) for at in range(0, rows, seg_len)]
    least = jnp.full((1, seg_len), 1.0, F32)
    for here in segments:
        all_keys = jnp.concatenate([mem_keys, keys[:, here]], axis=1)
        all_values = jnp.concatenate([mem_values, values[:, here]], axis=1)
        score = dot(all_keys, queries[:, here], 0, 0)
        exp_mem = jnp.exp2(score[:slots]).astype(BF16)
        exp_own = jnp.exp2(score[slots:] + causal).astype(BF16)
        total = dot(all_values, jnp.concatenate([exp_mem, exp_own], axis=0))
        near_total = dot(mem_values, exp_mem * times_ref[:, here])
        least = jnp.minimum(
            least, finish(here, total, near_total, reach[:, here], reach[:, here])
        )

    @pl.when(jnp.logical_not(jnp.min(least) > TINY))
    def _():
        zero = jnp.zeros((1, rows), F32)
        plain = jnp.concatenate(
            [q_high, q_low, pick_rows([zero, zero, zero, ones], 16).astype(BF16)], axis=0
        )
        for here in segments:
            score = dot(mem_keys, plain[:, here], 0, 0)
            score_own = dot(keys[:, here], plain[:, here], 0, 0) + causal
            near = jnp.where(times_ref[:, here] > 0, score, MASKED)
            near_peak = jnp.max(near, axis=0, keepdims=True)
            peak = jnp.maximum(
                jnp.max(score, axis=0, keepdims=True), jnp.max(score_own, axis=0, keepdims=True)
            )
            total = dot(mem_values, jnp.exp2(score - peak).astype(BF16))
            total = total + dot(values[:, here], jnp.exp2(score_own - peak).astype(BF16))
            exp_near = jnp.exp2(near - near_peak).astype(BF16) * times_ref[:, here]
            finish(here, total, dot(mem_values, exp_near), peak, near_peak)


def feed_kernel(
    owner_ref, xt_ref, gt_ref, mixed_ref, ctx_ref, rec_ref, gate_ref, side_ref, *refs, heads, pieces, sends
):
    w_pieces, refs = refs[:pieces], refs[pieces:]
    (block_ref, gh_ref, dm_ref, dc_ref, dn_ref, dlogit_ref, ggain_ref), refs = refs[:7], refs[7:]
    g_pieces, (wo_ref, up_ref, down_ref, gwo_ref, gup_ref, gdown_ref) = refs[:sends], refs[sends:]
    width, rows = xt_ref.shape
    chunks = up_ref.shape[1] // width
    size = width // heads
    low = down_ref.shape[0] // width * ROWS
    for number, piece, index in blocks_of(w_pieces):
        block = piece[index]
        down_ref[rows_at(owner_ref, number, low), :] = block[:low]
        here = rows_at(owner_ref, number, ROWS)
        wo_ref[here, :] = block[low : low + ROWS]
        for chunk in range(chunks):
            at = low + (chunk + 1) * ROWS
            up_ref[here, chunk * width : (chunk + 1) * width] = block[at : at + ROWS]

    gain = side_ref[...].astype(F32)[:, heads + 1 : heads + 2]
    hidden = xt_ref[...].astype(F32) + dot(wo_ref[...], mixed_ref[...], 0, 0)
    inv = lax.rsqrt(jnp.mean(hidden * hidden, axis=0, keepdims=True) + EPSILON)
    unit = hidden * inv
    n2 = (unit * gain).astype(BF16)
    grad = gt_ref[...]
    coef = math.sqrt(2.0 / math.pi)

    part_size = width // 2
    parts = [slice(at, at + part_size) for at in range(0, up_ref.shape[1], part_size)]

    def first(part):
        return dot(up_ref[:, part], n2, 0, 0), dot(down_ref[part, :], grad)

    def second(pre, grad_act):
        square = pre * pre
        half = 0.5 + 0.5 * jnp.tanh(pre * (coef + (0.044715 * coef) * square))
        act = pre * half
        slope = half + act * (1.0 - half) * (2.0 * coef + (6.0 * 0.044715 * coef) * square)
        return act.astype(BF16), (grad_act * slope).astype(BF16)

    ready = first(parts[0])
    out = gn2 = None
    for at, part in enumerate(parts):
        later = first(parts[at + 1]) if at + 1 < len(parts) else None
        act, grad_pre = second(*ready)
        ready = later
        out_part = dot(down_ref[part, :], act, 0, 0)
        gn2_part = dot(up_ref[:, part], grad_pre)
        out = out_part if out is None else out + out_part
        gn2 = gn2_part if gn2 is None else gn2 + gn2_part
        gdown_ref[part, :] = dot(act, grad, 1, 1).astype(BF16)
        gup_ref[:, part] = dot(n2, grad_pre, 1, 1).astype(BF16)

    block_ref[...] = (hidden + out).T.astype(BF16)
    ggain_ref[...] = jnp.broadcast_to(jnp.sum(gn2 * unit, axis=1, keepdims=True), ggain_ref.shape)
    a = gn2 * gain
    grad_hidden = grad.astype(F32) + inv * (a - unit * jnp.mean(a * unit, axis=0, keepdims=True))
    gh_ref[...] = grad_hidden
    branch = grad_hidden.astype(BF16)
    gwo_ref[...] = dot(mixed_ref[...], branch, 1, 1).astype(BF16)
    for number, piece, index in blocks_of(g_pieces):
        piece[index, :low] = gdown_ref[rows_at(owner_ref, number, low), :]
        here = rows_at(owner_ref, number, ROWS)
        piece[index, low : low + ROWS] = gwo_ref[here, :]
        for chunk in range(chunks):
            at = low + (chunk + 1) * ROWS
            piece[index, at : at + ROWS] = gup_ref[here, chunk * width : (chunk + 1) * width]
    grad_mixed = dot(wo_ref[...], branch)
    rounded = grad_mixed.astype(BF16)
    dm_ref[...] = rounded
    rounded = rounded.astype(F32)
    for head in range(heads):
        part = slice(head * size, (head + 1) * size)
        ctx, rec = ctx_ref[part, :], rec_ref[part, :]
        dc_ref[head : head + 1, :] = jnp.sum(rounded[part] * ctx, axis=0, keepdims=True)
        dn_ref[head : head + 1, :] = jnp.sum(rounded[part] * rec, axis=0, keepdims=True)
        share = gate_ref[head : head + 1, :]
        moved = jnp.sum(grad_mixed[part] * (rec - ctx), axis=0, keepdims=True)
        dlogit_ref[head : head + 1, :] = moved * share * (1.0 - share)


def attend_back_kernel(
    lengths_ref, q_ref, k_ref, v_ref, mk_ref, mv_ref, dm_ref, gate_ref, bias_ref,
    lse_ref, lsen_ref, dc_ref, dn_ref,
    dq_ref, dk_ref, dv_ref, dmk_ref, dmv_ref,
    dk_sum, dv_sum, dmk_sum, dmv_sum,
    *, first, seg_count, scale,
):
    size, rows = q_ref.shape
    seg_len = rows // seg_count
    penalty = local_penalty(lengths_ref, rows, seg_count)
    causal = causal_bias(TILE)
    q = q_ref[...].astype(F32) * (scale * LOG2E)
    q_high = q.astype(BF16)
    q_low = (q - q_high.astype(F32)).astype(BF16)
    row = pl.ds(pl.program_id(0) + first, 1)
    share = gate_ref[row, :]
    shift = jnp.log2(jnp.maximum(1.0 - share, 2.0**-60)) - lse_ref[row, :]
    near_shift = jnp.log2(jnp.maximum(share, 2.0**-60)) - lsen_ref[row, :] - shift
    dc = dc_ref[row, :]
    apart = dc - dn_ref[row, :]
    ones = jnp.ones((1, rows), F32)
    mem_three = pick_rows([jnp.ones((1, mk_ref.shape[1]), F32)] * 3, 16).astype(BF16)
    queries = jnp.concatenate(
        [q_high, q_low, pick_rows([*three_parts(shift), ones], 16).astype(BF16)], axis=0
    )
    keys = jnp.concatenate(
        [k_ref[...], k_ref[...], pick_rows([ones, ones, ones, penalty], 16).astype(BF16)], axis=0
    )
    mem_keys = jnp.concatenate([mk_ref[...], mk_ref[...], mem_three], axis=0)
    grads = jnp.concatenate([dm_ref[...], pick_rows(three_parts(-dc), 16).astype(BF16)], axis=0)
    values = jnp.concatenate([v_ref[...], pick_rows([ones] * 3, 16).astype(BF16)], axis=0)
    mem_values = jnp.concatenate([mv_ref[...], mem_three], axis=0)
    for at in range(0, rows, TILE):
        here = slice(at, at + TILE)
        start = at // seg_len * seg_len
        q_here, dm_here = q_ref[:, here].T, dm_ref[:, here].T
        score = dot(mem_keys, queries[:, here], 0, 0)
        moved = dot(mem_values, grads[:, here], 0, 0)
        far = jnp.exp2(score)
        near = jnp.exp2(score + (bias_ref[:, here] + near_shift[:, here]))
        weight = far + near
        dscore = (weight * moved + near * apart[:, here]).astype(BF16)
        grad_mv = dot(weight.astype(BF16), dm_here).T
        grad_mk = dot(dscore, q_here).T
        dq = dot(mk_ref[...], dscore)
        if at == 0:
            dmv_sum[...] = grad_mv
            dmk_sum[...] = grad_mk
        else:
            dmv_sum[...] += grad_mv
            dmk_sum[...] += grad_mk
        for block in range(start, at + TILE, TILE):
            there = slice(block, block + TILE)
            score = dot(keys[:, there], queries[:, here], 0, 0)
            if block == at:
                score = score + causal
            weight = jnp.exp2(score)
            dscore = (weight * dot(values[:, there], grads[:, here], 0, 0)).astype(BF16)
            grad_v = dot(weight.astype(BF16), dm_here).T
            grad_k = dot(dscore, q_here).T
            dq = dq + dot(k_ref[:, there], dscore)
            if block == at:
                dv_sum[:, there] = grad_v
                dk_sum[:, there] = grad_k
            else:
                dv_sum[:, there] += grad_v
                dk_sum[:, there] += grad_k
        dq_ref[:, here] = (scale * dq).astype(BF16)
    dk_ref[...] = (scale * dk_sum[...]).astype(BF16)
    dv_ref[...] = dv_sum[...].astype(BF16)
    dmk_ref[...] = (scale * dmk_sum[...]).astype(BF16)
    dmv_ref[...] = dmv_sum[...].astype(BF16)


def weight_kernel(
    owner_ref, nt_ref, side_ref, dlogit_ref, ggain_ref, *refs, calls, pieces, mem_pieces, sends, heads
):
    memory, refs = refs[:mem_pieces], refs[mem_pieces:]
    backs = [refs[5 * at : 5 * at + 5] for at in range(calls)]
    refs = refs[5 * calls :]
    w_pieces, refs = refs[:pieces], refs[pieces:]
    g_pieces, (back_ref, gw_ref) = refs[:sends], refs[sends:]
    width, rows = nt_ref.shape
    normed = nt_ref[...]
    for part in range(3):
        at = part * width
        for back in backs:
            back_ref[at : at + back[part].shape[0], :] = back[part][...]
            at += back[part].shape[0]
    side = jnp.concatenate([dlogit_ref[...], jnp.zeros((SIDE - heads, rows), F32)], axis=0)
    back_ref[3 * width :, :] = side.astype(BF16)
    for part in range(3):
        columns = slice(part * width, (part + 1) * width)
        gw_ref[:, columns] = dot(normed, back_ref[columns, :], 1, 1)
    gw_ref[:, 3 * width :] = dot(normed, back_ref[3 * width :, :], 1, 1)
    by_rows = []
    for number, piece, index in blocks_of(w_pieces):
        here = rows_at(owner_ref, number, ROWS)
        by_rows.append((here, jnp.sum(piece[index].astype(F32) * gw_ref[here, :], axis=1, keepdims=True)))
    lane = lax.broadcasted_iota(jnp.int32, (ROWS, SIDE), 1)
    for here, total in by_rows:
        gain = side_ref[here, :].astype(F32)[:, heads : heads + 1]
        block = jnp.where(lane == heads, total / gain, gw_ref[here, 3 * width :])
        gw_ref[here, 3 * width :] = jnp.where(lane == heads + 1, ggain_ref[here, :], block)
    for part in range(1, 3):
        at = part * width
        for back in backs:
            source = back[part + 2]
            grad = sum(
                dot(piece[0], source[:, i * piece.shape[1] : (i + 1) * piece.shape[1]], 0, 1)
                for i, piece in enumerate(memory)
            )
            gw_ref[:, at : at + source.shape[0]] += grad
            at += source.shape[0]
    for number, piece, index in blocks_of(g_pieces):
        piece[index] = gw_ref[rows_at(owner_ref, number, ROWS), :].astype(BF16)


def input_kernel(owner_ref, xt_ref, inv_ref, side_ref, back_ref, gh_ref, *refs, heads):
    w_pieces, (gx_ref, w_ref) = refs[:-2], refs[-2:]
    for number, piece, index in blocks_of(w_pieces):
        w_ref[rows_at(owner_ref, number, ROWS), :] = piece[index]
    unit = xt_ref[...].astype(F32) * inv_ref[0:1, :]
    gain = side_ref[...].astype(F32)[:, heads : heads + 1]
    b = dot(w_ref[...], back_ref[...]) * gain
    out = gh_ref[...] + inv_ref[0:1, :] * (b - unit * jnp.mean(b * unit, axis=0, keepdims=True))
    gx_ref[...] = out.T


def finish_feed_kernel(*refs):
    *terms, down_ref, wo_ref, up_ref = refs
    low, width = down_ref.shape
    total = sum(term[0].astype(F32) for term in terms)
    down_ref[...] = total[:low]
    height = wo_ref.shape[0]
    wo_ref[...] = total[low : low + height]
    for chunk in range(up_ref.shape[1] // width):
        at = low + (chunk + 1) * height
        up_ref[:, chunk * width : (chunk + 1) * width] = total[at : at + height]


def finish_kernel(*refs):
    *terms, q_ref, k_ref, v_ref, gate_ref, gains_ref = refs
    height, width = q_ref.shape
    total = sum(term[0].astype(F32) for term in terms)
    for part, ref in enumerate((q_ref, k_ref, v_ref)):
        ref[...] = total[:, part * width : (part + 1) * width]
    heads = gate_ref.shape[1]
    side = total[:, 3 * width :]
    gate_ref[...] = side[:, :heads]
    gains_ref[...] = side.T[heads : heads + 8]


def on_device(
    tokens,
    memory,
    lengths,
    neighbours,
    out_grad,
    gain_one,
    gain_two,
    w_query,
    w_key,
    w_value,
    w_gate,
    w_out,
    w_up,
    w_down,
    *,
    sizes,
):
    rows, width = tokens.shape
    heads = w_gate.shape[1]
    size = width // heads
    seg_count = lengths.shape[0]
    knn = neighbours.shape[1]
    shard = w_query.shape[0]
    ff = w_up.shape[1]
    chunks = ff // width
    tall = w_down.shape[0]
    scale = size ** (-0.5)
    own = memory.shape[0]
    slots = own * sizes["seq"]
    blocks = width // ROWS
    low = ff // blocks

    groups = groups_of(sizes)
    owner = owners(groups, sizes)
    direct = shard == ROWS
    kernel_owner = owner if direct else jnp.arange(blocks, dtype=jnp.int32)

    columns = 3 * width + SIDE
    if direct:
        (packed,) = call(
            pack_kernel,
            [((shard, columns), BF16)],
            [WHOLE] * 6,
            micros=1,
        )(w_query, w_key, w_value, w_gate, gain_one[None], gain_two[None])
    else:
        packed = jnp.concatenate(
            [
                w_query,
                w_key,
                w_value,
                w_gate,
                gain_one[:, None],
                gain_two[:, None],
                jnp.zeros((shard, SIDE - heads - 2), BF16),
            ],
            axis=1,
        )
    seq_group = [("seq", bit) for bit in bits_of(sizes["seq"])]
    memory_pieces = [memory[None]]
    for step in seq_group:
        memory_pieces = gather_stage(memory_pieces, [step], sizes, join=False)
    w_pieces = gather_stage([packed[None]], groups[0], sizes)

    ids = neighbours // own
    ids = place_of(ids, lax.axis_index("seq"), seq_group) * own + neighbours % own
    ids = jnp.pad(ids.T, ((0, 8 - knn), (0, 0)))
    big = (width, rows)
    lanes = (8, rows)
    feed_height = tall + shard * (1 + chunks)
    prepared = call(
        functools.partial(prepare_kernel, count=knn),
        [
            (big, BF16),
            (big, BF16),
            (lanes, F32),
            ((slots, rows), BF16),
            ((slots, rows), F32),
            ((feed_height, width), BF16),
        ],
        [WHOLE] * 6,
        micros=4,
    )(tokens, out_grad, ids, w_down, w_out, w_up)
    w_pieces, (xt, gt, inv_one, times, bias, feed_packed) = after(w_pieces, prepared)
    for at, group in enumerate(groups[1:], 1):
        w_pieces = gather_stage(w_pieces, group, sizes, join=at + 1 < len(groups))
        if at == 1:
            w_pieces[0], feed_packed = after(w_pieces[0], feed_packed)
    feed_pieces = [feed_packed[None]]
    for group in groups[:-1]:
        feed_pieces = gather_stage(feed_pieces, group, sizes)

    def in_order(pieces):
        both = jnp.concatenate(pieces, axis=0)
        return jnp.zeros_like(both).at[owner].set(both)

    def split_rows(array, *heights):
        at, parts = 0, []
        for height in heights:
            parts.append(array[:, at : at + height].reshape(-1, width))
            at += height
        return parts

    if not direct:
        w_pieces = [in_order(w_pieces).reshape(blocks, ROWS, columns)]

    def to_send(pieces, *heights):
        if direct:
            return pieces
        array = pieces[0]
        if len(heights) > 1:
            parts = split_rows(array, low, *[ROWS] * (len(heights) - 1))
            parts = [part.reshape(-1, height, width) for part, height in zip(parts, heights)]
            array = jnp.concatenate(parts, axis=1)
        else:
            array = array.reshape(-1, heights[0], array.shape[2])
        array = array[owner]
        count = 1 << len(groups[-1])
        return jnp.split(array, count, axis=0)

    def head_block(part, cols, first=0):
        return pl.BlockSpec((size, cols), lambda h: (part * heads + first + h, 0))

    nt, qkv, mem_kv, side, mixed, ctx, rec, gate, lse, lsen = call(
        functools.partial(
            attend_kernel,
            pieces=len(w_pieces),
            mem_pieces=len(memory_pieces),
            heads=heads,
            seg_count=seg_count,
            scale=scale,
        ),
        [
            (big, BF16),
            ((3 * width, rows), BF16),
            ((2 * width, slots), BF16),
            ((width, SIDE), BF16),
            (big, BF16),
            (big, F32),
            (big, F32),
            (lanes, F32),
            (lanes, F32),
            (lanes, F32),
        ],
        [SCALARS, SCALARS] + [WHOLE] * (3 + len(w_pieces) + len(memory_pieces)),
        out_specs=[WHOLE] * 4 + [head_block(0, rows)] * 3 + [WHOLE] * 3,
        grid=(heads,),
        scratch=[pltpu.VMEM((width, columns), BF16)],
        micros=22,
        vmem=20,
    )(kernel_owner, lengths, xt, inv_one, times, *w_pieces, *memory_pieces)

    mixed, feed_pieces = after(mixed, feed_pieces)
    feed_pieces = gather_stage(feed_pieces, groups[-1], sizes, join=False)
    if not direct:
        parts = split_rows(in_order(feed_pieces), tall, *[shard] * (1 + chunks))
        feed_pieces = [jnp.concatenate([part.reshape(blocks, -1, width) for part in parts], axis=1)]
    pieces = len(feed_pieces)
    sends = 1 << len(groups[-1]) if direct else 1
    feed_block = (blocks // sends,) + feed_pieces[0].shape[1:]
    outs = call(
        functools.partial(feed_kernel, heads=heads, pieces=pieces, sends=sends),
        [
            ((rows, width), BF16),
            (big, F32),
            (big, BF16),
            (lanes, F32),
            (lanes, F32),
            (lanes, F32),
            ((width, SIDE), F32),
        ]
        + [(feed_block, BF16)] * sends,
        [SCALARS] + [WHOLE] * (7 + pieces),
        scratch=[
            pltpu.VMEM(shape, BF16)
            for shape in ((width, width), (width, ff), (ff, width)) * 2
        ],
        micros=20,
        vmem=32,
    )(kernel_owner, xt, gt, mixed, ctx, rec, gate, side, *feed_pieces)
    block_out, grad_hidden, dm, dc, dn, dlogit, ggain_two = outs[:7]
    late = to_send(outs[7:], tall, *[shard] * (1 + chunks))
    late_at = len(groups)

    backs = []
    first = 0
    for count in (2, heads - 2):
        late_at -= 1
        moving = sum_stage(late, groups, late_at, sizes)
        outs = call(
            functools.partial(attend_back_kernel, first=first, seg_count=seg_count, scale=scale),
            [((size * count, rows), BF16)] * 3 + [((size * count, slots), BF16)] * 2,
            [
                SCALARS,
                head_block(0, rows, first),
                head_block(1, rows, first),
                head_block(2, rows, first),
                head_block(0, slots, first),
                head_block(1, slots, first),
                head_block(0, rows, first),
            ]
            + [WHOLE] * 6,
            out_specs=[head_block(0, rows)] * 3 + [head_block(0, slots)] * 2,
            grid=(count,),
            scratch=[pltpu.VMEM((size, rows), F32)] * 2 + [pltpu.VMEM((size, slots), F32)] * 2,
            micros=5 * count,
        )(lengths, qkv, qkv, qkv, mem_kv, mem_kv, dm, gate, bias, lse, lsen, dc, dn)
        first += count
        late, (outs, dm) = after(moving, (outs, dm))
        backs.append(outs)

    pieces = len(w_pieces)
    *early, back = call(
        functools.partial(
            weight_kernel,
            calls=len(backs),
            pieces=pieces,
            mem_pieces=len(memory_pieces),
            sends=sends,
            heads=heads,
        ),
        [((blocks // sends, ROWS, columns), BF16)] * sends + [((columns, rows), BF16)],
        [SCALARS] + [WHOLE] * (4 + len(memory_pieces) + 5 * len(backs) + pieces),
        scratch=[pltpu.VMEM((width, columns), F32)],
        micros=6,
    )(
        kernel_owner,
        nt,
        side,
        dlogit,
        ggain_two,
        *memory_pieces,
        *[b for back in backs for b in back],
        *w_pieces,
    )
    while late_at:
        late_at -= 1
        late = sum_stage(late, groups, late_at, sizes)
    early = to_send(early, shard)
    for at in reversed(range(len(groups))):
        early = sum_stage(early, groups, at, sizes)
        if at + 1 == len(groups):
            early, back = after(early, back)
    (grad_tokens,) = call(
        functools.partial(input_kernel, heads=heads),
        [((rows, width), F32)],
        [SCALARS] + [WHOLE] * (5 + pieces),
        scratch=[pltpu.VMEM((width, columns), BF16)],
        micros=6,
    )(kernel_owner, xt, inv_one, side, back, grad_hidden, *w_pieces)

    if direct:
        grad_down, grad_out, grad_up = call(
            finish_feed_kernel,
            [((tall, width), F32), ((shard, width), F32), ((shard, ff), F32)],
            [WHOLE] * len(late),
            micros=1,
        )(*late)
        grad_query, grad_key, grad_value, grad_gate, gains = call(
            finish_kernel,
            [((shard, width), F32)] * 3 + [((shard, heads), F32), ((8, shard), F32)],
            [WHOLE] * len(early),
            micros=1,
        )(*early)
        grad_one, grad_two = gains[0], gains[1]
    else:
        late = sum(term[0].astype(F32) for term in late)
        early = sum(term[0].astype(F32) for term in early)
        grad_down, grad_out = late[:tall], late[tall : tall + shard]
        grad_up = jnp.concatenate(
            [late[tall + shard * (1 + c) : tall + shard * (2 + c)] for c in range(chunks)], axis=1
        )
        grad_query, grad_key, grad_value = (
            early[:, at : at + width] for at in range(0, 3 * width, width)
        )
        side = early[:, 3 * width :]
        grad_gate, grad_one, grad_two = side[:, :heads], side[:, heads], side[:, heads + 1]
    return (
        block_out,
        grad_tokens,
        grad_one,
        grad_two,
        grad_query,
        grad_key,
        grad_value,
        grad_gate,
        grad_out,
        grad_up,
        grad_down,
    )


def solution(mesh):
    row_split, vector = P(("dp", "seq"), None), P(("dp", "seq"))
    in_specs = (row_split, row_split, vector, row_split, row_split, vector, vector) + (row_split,) * 7
    out_specs = (row_split, row_split, vector, vector) + (row_split,) * 7
    return jax.shard_map(
        functools.partial(on_device, sizes=dict(mesh.shape)),
        mesh=mesh,
        in_specs=in_specs,
        out_specs=out_specs,
        check_vma=False,
    )
```

```python
import functools
import math

import jax
import jax.numpy as jnp
from jax import lax
from jax.experimental import pallas as pl
from jax.experimental.pallas import tpu as pltpu
from jax.sharding import PartitionSpec as P


EPSILON = 1e-06
MASKED = -1e30
LOG2E = math.log2(math.e)
F32 = jnp.float32
BF16 = jnp.bfloat16
SIDE = 128
TILE = 256
ROWS = 16
TINY = 2.0**-80
PER_MICRO = 1.1e9


def dot(left, right, left_dim=1, right_dim=0):
    return lax.dot_general(
        left, right, (((left_dim,), (right_dim,)), ((), ())), preferred_element_type=F32
    )


def call(kernel, outs, in_specs, out_specs=None, grid=None, scratch=(), micros=0, vmem=16):
    options = {} if grid is None else dict(grid=grid)
    if out_specs is None:
        out_specs = [WHOLE] * len(outs)
    return pl.pallas_call(
        kernel,
        out_shape=[
            where[0](shape, kind) if where else jax.ShapeDtypeStruct(shape, kind)
            for shape, kind, *where in outs
        ],
        in_specs=in_specs,
        out_specs=out_specs,
        scratch_shapes=list(scratch),
        compiler_params=pltpu.CompilerParams(vmem_limit_bytes=vmem << 20),
        cost_estimate=pl.CostEstimate(
            flops=int(micros * PER_MICRO), bytes_accessed=0, transcendentals=0
        ),
        **options,
    )


WHOLE = pl.BlockSpec(memory_space=pltpu.VMEM)
SCALARS = pl.BlockSpec(memory_space=pltpu.SMEM)
FAR = pl.BlockSpec(memory_space=pltpu.HBM)


def far(array):
    return pltpu.with_memory_space_constraint(array, pltpu.HBM)


def three_parts(value):
    high = value.astype(BF16).astype(F32)
    rest = value - high
    middle = rest.astype(BF16).astype(F32)
    return high, middle, rest - middle


def pick_rows(rows, count):
    shape = (count, rows[0].shape[1])
    index = lax.broadcasted_iota(jnp.int32, shape, 0)
    block = jnp.zeros(shape, F32)
    for at, row in enumerate(rows):
        block = jnp.where(index == at, row, block)
    return block


def bits_of(size):
    return [1 << b for b in reversed(range(size.bit_length() - 1))]


def groups_of(sizes):
    steps = [("dp", bit) for bit in bits_of(sizes["dp"])] + [("seq", bit) for bit in bits_of(sizes["seq"])]
    return [steps[at : at + 2] for at in range(0, len(steps), 2)]


def swap(array, group, mask, sizes):
    n_seq = sizes["seq"]
    apart = 0
    for at, (axis, bit) in enumerate(group):
        if mask >> at & 1:
            apart ^= bit * (n_seq if axis == "dp" else 1)
    pairs = [(i, i ^ apart) for i in range(sizes["dp"] * n_seq)]
    return lax.ppermute(array, ("dp", "seq"), pairs)


def gather_stage(pieces, group, sizes, join=True):
    if join and len(pieces) > 1:
        pieces = [jnp.concatenate(pieces, axis=0)]
    masks = range(1, 1 << len(group))
    return pieces + [swap(piece, group, mask, sizes) for mask in masks for piece in pieces]


def sum_terms(pieces, group, sizes):
    return [pieces[0]] + [swap(pieces[mask], group, mask, sizes) for mask in range(1, 1 << len(group))]


def add_terms(terms, group):
    count = 1 << len(group)
    step = terms[0].shape[0] // count
    return [
        sum(term[m * step : (m + 1) * step].astype(F32) for term in terms).astype(BF16)
        for m in range(count)
    ]


def after(earlier, later):
    return lax.optimization_barrier((earlier, later))[1]


def owners(groups, sizes):
    n_seq = sizes["seq"]
    at = jnp.arange(sizes["dp"] * n_seq, dtype=jnp.int32)
    own = {"dp": lax.axis_index("dp"), "seq": lax.axis_index("seq")}
    for number, (axis, bit) in enumerate(step for group in groups for step in group):
        own[axis] = own[axis] ^ jnp.where((at >> number) & 1, bit, 0)
    return own["dp"] * n_seq + own["seq"]


def place_of(ids, own_index, group_steps):
    apart = ids ^ own_index
    place = jnp.zeros_like(ids)
    for at, (_, bit) in enumerate(group_steps):
        place = place + jnp.where((apart & bit) != 0, 1 << at, 0)
    return place


def blocks_of(pieces):
    number = 0
    for piece in pieces:
        for index in range(piece.shape[0]):
            yield number, piece, index
            number += 1


def rows_at(owner_ref, number, height):
    return pl.ds(pl.multiple_of(owner_ref[number] * height, height), height)


def pack_kernel(
    q_ref, k_ref, v_ref, gate_ref, one_ref, two_ref, down_ref, wo_ref, up_ref, out_ref, feed_ref
):
    height, width = q_ref.shape
    low = down_ref.shape[0]
    feed_ref[:low, :] = down_ref[...]
    feed_ref[low : low + height, :] = wo_ref[...]
    for chunk in range(up_ref.shape[1] // width):
        at = low + (chunk + 1) * height
        feed_ref[at : at + height, :] = up_ref[:, chunk * width : (chunk + 1) * width]
    heads = gate_ref.shape[0]
    for part, ref in enumerate((q_ref, k_ref, v_ref)):
        out_ref[:, part * width : (part + 1) * width] = ref[...]
    row = lax.broadcasted_iota(jnp.int32, (height, height), 0)
    column = lax.broadcasted_iota(jnp.int32, (height, height), 1)
    lane = lax.broadcasted_iota(jnp.int32, (height, SIDE), 1)
    spread = lax.broadcasted_iota(jnp.int32, (heads, SIDE), 0) == lax.broadcasted_iota(
        jnp.int32, (heads, SIDE), 1
    )
    side = dot(gate_ref[...].astype(F32), jnp.where(spread, 1.0, 0.0), 0, 0)
    for at, ref in enumerate((one_ref, two_ref)):
        gains = jnp.where(row == column, ref[...].astype(F32), 0.0)
        side = jnp.where(lane == heads + at, jnp.sum(gains, axis=1, keepdims=True), side)
    out_ref[:, 3 * width :] = side.astype(BF16)


def prepare_kernel(
    x_ref, g_ref, ids_ref,
    xt_ref, gt_ref, inv_ref, times_ref, bias_ref,
    *, count,
):
    xt = x_ref[...].astype(F32).T
    xt_ref[...] = xt.astype(BF16)
    gt_ref[...] = g_ref[...].astype(F32).T.astype(BF16)
    inv = lax.rsqrt(jnp.mean(xt * xt, axis=0, keepdims=True) + EPSILON)
    inv_ref[...] = jnp.broadcast_to(inv, inv_ref.shape)
    slots, rows = bias_ref.shape
    step = 128

    def body(i, _):
        at = pl.multiple_of(i * step, step)
        slot = lax.broadcasted_iota(jnp.int32, (step, rows), 0) + at
        times = jnp.zeros((step, rows), F32)
        for j in range(count):
            times = times + jnp.where(ids_ref[j : j + 1, :] == slot, 1.0, 0.0)
        times_ref[pl.ds(at, step), :] = times.astype(BF16)
        bias_ref[pl.ds(at, step), :] = jnp.where(times > 0.0, jnp.log2(times), MASKED)
        return 0

    lax.fori_loop(0, slots // step, body, 0)


def local_penalty(lengths_ref, rows, seg_count):
    seg_len = rows // seg_count
    lane = lax.broadcasted_iota(jnp.int32, (1, rows), 1)
    last = jnp.zeros((1, rows), jnp.int32)
    for seg in range(seg_count):
        last = jnp.where(lane // seg_len == seg, seg * seg_len + lengths_ref[seg], last)
    return jnp.where(lane < last, 0.0, MASKED)


def causal_bias(size):
    key = lax.broadcasted_iota(jnp.int32, (size, size), 0)
    query = lax.broadcasted_iota(jnp.int32, (size, size), 1)
    return jnp.where(key <= query, 0.0, MASKED)


def longest(keys):
    keys = keys.astype(F32)
    return jnp.max(jnp.sum(keys * keys, axis=0, keepdims=True), axis=1, keepdims=True)


def attend_kernel(
    owner_ref, lengths_ref, xt_far, inv_ref, times_far, *refs,
    pieces, mem_pieces, heads, seg_count, scale,
):
    w_pieces, memory, refs = refs[:pieces], refs[pieces : pieces + mem_pieces], refs[mem_pieces:]
    (
        nt_ref, qkv_ref, mem_ref, side_ref, mixed_ref, ctx_ref, rec_ref, gate_ref, lse_ref, lsen_ref,
        w_ref, xt_ref, times_ref, sems,
    ) = refs[pieces:]
    head = pl.program_id(0)
    width, rows = xt_ref.shape
    slots = times_ref.shape[0]
    size = width // heads
    seg_len = rows // seg_count

    @pl.when(head == 0)
    def _():
        x_copy = pltpu.make_async_copy(xt_far, xt_ref, sems.at[0])
        times_copy = pltpu.make_async_copy(times_far, times_ref, sems.at[1])
        x_copy.start()
        times_copy.start()
        for number, piece, index in blocks_of(w_pieces):
            w_ref[rows_at(owner_ref, number, piece.shape[1]), :] = piece[index]
        x_copy.wait()
        side_ref[...] = w_ref[:, 3 * width :]
        gain = side_ref[...].astype(F32)[:, heads : heads + 1]
        normed = (xt_ref[...].astype(F32) * inv_ref[0:1, :] * gain).astype(BF16)
        nt_ref[...] = normed
        for part in range(3):
            columns = slice(part * width, (part + 1) * width)
            qkv_ref[columns, :] = dot(w_ref[:, columns], normed, 0, 0).astype(BF16)
        gate_ref[...] = jax.nn.sigmoid(dot(side_ref[...], normed, 0, 0)[0:heads])
        for part in range(2):
            columns = slice((part + 1) * width, (part + 2) * width)
            for number, piece, index in blocks_of(memory):
                own = piece.shape[1]
                there = slice(number * own, (number + 1) * own)
                mem_ref[part * width : (part + 1) * width, there] = dot(
                    w_ref[:, columns], piece[index], 0, 1
                ).astype(BF16)
        times_copy.wait()

    def head_of(ref, part):
        return ref[pl.ds(pl.multiple_of(part * width + head * size, size), size), :]

    q, k, v = (head_of(qkv_ref, part) for part in range(3))
    mk, mv = (head_of(mem_ref, part) for part in range(2))
    gate = gate_ref[pl.ds(head, 1), :]
    penalty = local_penalty(lengths_ref, rows, seg_count)
    causal = causal_bias(seg_len)
    q = q.astype(F32) * (scale * LOG2E)
    q_high = q.astype(BF16)
    q_low = (q - q_high.astype(F32)).astype(BF16)
    reach = jnp.sqrt(
        jnp.sum(q * q, axis=0, keepdims=True) * jnp.maximum(longest(k), longest(mk))
    ) * (1.0 + 2.0**-10)
    ones = jnp.ones((1, rows), F32)
    mem_three = pick_rows([jnp.ones((1, slots), F32)] * 3, 16).astype(BF16)
    queries = jnp.concatenate(
        [q_high, q_low, pick_rows([*three_parts(-reach), ones], 16).astype(BF16)], axis=0
    )
    keys = jnp.concatenate([k, k, pick_rows([ones, ones, ones, penalty], 16).astype(BF16)], axis=0)
    mem_keys = jnp.concatenate([mk, mk, mem_three], axis=0)
    values = jnp.concatenate([v, jnp.ones((16, rows), BF16)], axis=0)
    mem_values = jnp.concatenate([mv, jnp.ones((16, slots), BF16)], axis=0)

    def finish(here, total, near_total, peak, near_peak):
        mass, near_mass = total[size : size + 1], near_total[size : size + 1]
        context = total[:size] / mass
        recalled = near_total[:size] / near_mass
        ctx_ref[:, here] = context
        rec_ref[:, here] = recalled
        lse_ref[pl.ds(head, 1), here] = peak + jnp.log2(mass)
        lsen_ref[pl.ds(head, 1), here] = near_peak + jnp.log2(near_mass)
        share = gate[:, here]
        mixed_ref[:, here] = ((1.0 - share) * context + share * recalled).astype(BF16)
        return jnp.minimum(mass, near_mass)

    segments = [slice(at, at + seg_len) for at in range(0, rows, seg_len)]
    least = jnp.full((1, seg_len), 1.0, F32)
    for here in segments:
        all_keys = jnp.concatenate([mem_keys, keys[:, here]], axis=1)
        all_values = jnp.concatenate([mem_values, values[:, here]], axis=1)
        score = dot(all_keys, queries[:, here], 0, 0)
        exp_mem = jnp.exp2(score[:slots]).astype(BF16)
        exp_own = jnp.exp2(score[slots:] + causal).astype(BF16)
        total = dot(all_values, jnp.concatenate([exp_mem, exp_own], axis=0))
        near_total = dot(mem_values, exp_mem * times_ref[:, here])
        least = jnp.minimum(
            least, finish(here, total, near_total, reach[:, here], reach[:, here])
        )

    @pl.when(jnp.logical_not(jnp.min(least) > TINY))
    def _():
        zero = jnp.zeros((1, rows), F32)
        plain = jnp.concatenate(
            [q_high, q_low, pick_rows([zero, zero, zero, ones], 16).astype(BF16)], axis=0
        )
        for here in segments:
            score = dot(mem_keys, plain[:, here], 0, 0)
            score_own = dot(keys[:, here], plain[:, here], 0, 0) + causal
            near = jnp.where(times_ref[:, here] > 0, score, MASKED)
            near_peak = jnp.max(near, axis=0, keepdims=True)
            peak = jnp.maximum(
                jnp.max(score, axis=0, keepdims=True), jnp.max(score_own, axis=0, keepdims=True)
            )
            total = dot(mem_values, jnp.exp2(score - peak).astype(BF16))
            total = total + dot(values[:, here], jnp.exp2(score_own - peak).astype(BF16))
            exp_near = jnp.exp2(near - near_peak).astype(BF16) * times_ref[:, here]
            finish(here, total, dot(mem_values, exp_near), peak, near_peak)


def feed_kernel(
    owner_ref, xt_ref, gt_ref, mixed_ref, ctx_ref, rec_ref, gate_ref, side_ref, *refs, heads, pieces, sends
):
    w_pieces, refs = refs[:pieces], refs[pieces:]
    (block_ref, gh_ref, dm_ref, dc_ref, dn_ref, dlogit_ref, ggain_ref), refs = refs[:7], refs[7:]
    g_pieces, (wo_ref, up_ref, down_ref) = refs[:sends], refs[sends:]
    width, rows = xt_ref.shape
    chunks = up_ref.shape[1] // width
    size = width // heads
    low = down_ref.shape[0] // width * ROWS
    for number, piece, index in blocks_of(w_pieces):
        block = piece[index]
        down_ref[rows_at(owner_ref, number, low), :] = block[:low]
        here = rows_at(owner_ref, number, ROWS)
        wo_ref[here, :] = block[low : low + ROWS]
        for chunk in range(chunks):
            at = low + (chunk + 1) * ROWS
            up_ref[here, chunk * width : (chunk + 1) * width] = block[at : at + ROWS]

    gain = side_ref[...].astype(F32)[:, heads + 1 : heads + 2]
    hidden = xt_ref[...].astype(F32) + dot(wo_ref[...], mixed_ref[...], 0, 0)
    inv = lax.rsqrt(jnp.mean(hidden * hidden, axis=0, keepdims=True) + EPSILON)
    unit = hidden * inv
    n2 = (unit * gain).astype(BF16)
    grad = gt_ref[...]
    coef = math.sqrt(2.0 / math.pi)

    part_size = width // 2
    parts = [slice(at, at + part_size) for at in range(0, up_ref.shape[1], part_size)]

    def first(part):
        return dot(up_ref[:, part], n2, 0, 0), dot(down_ref[part, :], grad)

    def second(pre, grad_act):
        square = pre * pre
        half = 0.5 + 0.5 * jnp.tanh(pre * (coef + (0.044715 * coef) * square))
        act = pre * half
        slope = half + act * (1.0 - half) * (2.0 * coef + (6.0 * 0.044715 * coef) * square)
        return act.astype(BF16), (grad_act * slope).astype(BF16)

    ready = first(parts[0])
    out = gn2 = None
    for at, part in enumerate(parts):
        later = first(parts[at + 1]) if at + 1 < len(parts) else None
        act, grad_pre = second(*ready)
        ready = later
        out_part = dot(down_ref[part, :], act, 0, 0)
        gn2_part = dot(up_ref[:, part], grad_pre)
        out = out_part if out is None else out + out_part
        gn2 = gn2_part if gn2 is None else gn2 + gn2_part
        down_ref[part, :] = dot(act, grad, 1, 1).astype(BF16)
        up_ref[:, part] = dot(n2, grad_pre, 1, 1).astype(BF16)

    block_ref[...] = (hidden + out).T.astype(BF16)
    ggain_ref[...] = jnp.broadcast_to(jnp.sum(gn2 * unit, axis=1, keepdims=True), ggain_ref.shape)
    a = gn2 * gain
    grad_hidden = grad.astype(F32) + inv * (a - unit * jnp.mean(a * unit, axis=0, keepdims=True))
    gh_ref[...] = grad_hidden
    branch = grad_hidden.astype(BF16)
    grad_mixed = dot(wo_ref[...], branch)
    wo_ref[...] = dot(mixed_ref[...], branch, 1, 1).astype(BF16)
    for number, piece, index in blocks_of(g_pieces):
        piece[index, :low] = down_ref[rows_at(owner_ref, number, low), :]
        here = rows_at(owner_ref, number, ROWS)
        piece[index, low : low + ROWS] = wo_ref[here, :]
        for chunk in range(chunks):
            at = low + (chunk + 1) * ROWS
            piece[index, at : at + ROWS] = up_ref[here, chunk * width : (chunk + 1) * width]
    rounded = grad_mixed.astype(BF16)
    dm_ref[...] = rounded
    rounded = rounded.astype(F32)
    for head in range(heads):
        part = slice(head * size, (head + 1) * size)
        ctx, rec = ctx_ref[part, :], rec_ref[part, :]
        dc_ref[head : head + 1, :] = jnp.sum(rounded[part] * ctx, axis=0, keepdims=True)
        dn_ref[head : head + 1, :] = jnp.sum(rounded[part] * rec, axis=0, keepdims=True)
        share = gate_ref[head : head + 1, :]
        moved = jnp.sum(grad_mixed[part] * (rec - ctx), axis=0, keepdims=True)
        dlogit_ref[head : head + 1, :] = moved * share * (1.0 - share)


def attend_back_kernel(
    lengths_ref, q_ref, k_ref, v_ref, mk_ref, mv_ref, dm_ref, gate_ref, bias_ref,
    lse_ref, lsen_ref, dc_ref, dn_ref,
    dq_ref, dk_ref, dv_ref, dmk_ref, dmv_ref,
    dk_sum, dv_sum, dmk_sum, dmv_sum,
    *, first, seg_count, scale,
):
    size, rows = q_ref.shape
    seg_len = rows // seg_count
    penalty = local_penalty(lengths_ref, rows, seg_count)
    causal = causal_bias(TILE)
    q = q_ref[...].astype(F32) * (scale * LOG2E)
    q_high = q.astype(BF16)
    q_low = (q - q_high.astype(F32)).astype(BF16)
    row = pl.ds(pl.program_id(0) + first, 1)
    share = gate_ref[row, :]
    shift = jnp.log2(jnp.maximum(1.0 - share, 2.0**-60)) - lse_ref[row, :]
    near_shift = jnp.log2(jnp.maximum(share, 2.0**-60)) - lsen_ref[row, :] - shift
    dc = dc_ref[row, :]
    apart = dc - dn_ref[row, :]
    ones = jnp.ones((1, rows), F32)
    mem_three = pick_rows([jnp.ones((1, mk_ref.shape[1]), F32)] * 3, 16).astype(BF16)
    queries = jnp.concatenate(
        [q_high, q_low, pick_rows([*three_parts(shift), ones], 16).astype(BF16)], axis=0
    )
    keys = jnp.concatenate(
        [k_ref[...], k_ref[...], pick_rows([ones, ones, ones, penalty], 16).astype(BF16)], axis=0
    )
    mem_keys = jnp.concatenate([mk_ref[...], mk_ref[...], mem_three], axis=0)
    grads = jnp.concatenate([dm_ref[...], pick_rows(three_parts(-dc), 16).astype(BF16)], axis=0)
    values = jnp.concatenate([v_ref[...], pick_rows([ones] * 3, 16).astype(BF16)], axis=0)
    mem_values = jnp.concatenate([mv_ref[...], mem_three], axis=0)
    for at in range(0, rows, TILE):
        here = slice(at, at + TILE)
        start = at // seg_len * seg_len
        q_here, dm_here = q_ref[:, here].T, dm_ref[:, here].T
        score = dot(mem_keys, queries[:, here], 0, 0)
        moved = dot(mem_values, grads[:, here], 0, 0)
        far = jnp.exp2(score)
        near = jnp.exp2(score + (bias_ref[:, here] + near_shift[:, here]))
        weight = far + near
        dscore = (weight * moved + near * apart[:, here]).astype(BF16)
        grad_mv = dot(weight.astype(BF16), dm_here).T
        grad_mk = dot(dscore, q_here).T
        dq = dot(mk_ref[...], dscore)
        if at == 0:
            dmv_sum[...] = grad_mv
            dmk_sum[...] = grad_mk
        else:
            dmv_sum[...] += grad_mv
            dmk_sum[...] += grad_mk
        for block in range(start, at + TILE, TILE):
            there = slice(block, block + TILE)
            score = dot(keys[:, there], queries[:, here], 0, 0)
            if block == at:
                score = score + causal
            weight = jnp.exp2(score)
            dscore = (weight * dot(values[:, there], grads[:, here], 0, 0)).astype(BF16)
            grad_v = dot(weight.astype(BF16), dm_here).T
            grad_k = dot(dscore, q_here).T
            dq = dq + dot(k_ref[:, there], dscore)
            if block == at:
                dv_sum[:, there] = grad_v
                dk_sum[:, there] = grad_k
            else:
                dv_sum[:, there] += grad_v
                dk_sum[:, there] += grad_k
        dq_ref[:, here] = (scale * dq).astype(BF16)
    dk_ref[...] = (scale * dk_sum[...]).astype(BF16)
    dv_ref[...] = dv_sum[...].astype(BF16)
    dmk_ref[...] = (scale * dmk_sum[...]).astype(BF16)
    dmv_ref[...] = dmv_sum[...].astype(BF16)


def weight_kernel(
    owner_ref, nt_ref, side_ref, dlogit_ref, ggain_ref, *refs, calls, pieces, mem_pieces, sends, heads
):
    memory, refs = refs[:mem_pieces], refs[mem_pieces:]
    backs = [refs[5 * at : 5 * at + 5] for at in range(calls)]
    refs = refs[5 * calls :]
    w_pieces, refs = refs[:pieces], refs[pieces:]
    g_pieces, (back_ref, gw_ref) = refs[:sends], refs[sends:]
    width, rows = nt_ref.shape
    for part in range(3):
        at = part * width
        for back in backs:
            back_ref[at : at + back[part].shape[0], :] = back[part][...]
            at += back[part].shape[0]
    side = jnp.concatenate([dlogit_ref[...], jnp.zeros((SIDE - heads, rows), F32)], axis=0)
    back_ref[3 * width :, :] = side.astype(BF16)
    normed = nt_ref[...]
    for part in range(3):
        columns = slice(part * width, (part + 1) * width)
        gw_ref[:, columns] = dot(normed, back_ref[columns, :], 1, 1)
    gw_ref[:, 3 * width :] = dot(normed, back_ref[3 * width :, :], 1, 1)
    by_rows = []
    for number, piece, index in blocks_of(w_pieces):
        here = rows_at(owner_ref, number, ROWS)
        by_rows.append((here, jnp.sum(piece[index].astype(F32) * gw_ref[here, :], axis=1, keepdims=True)))
    lane = lax.broadcasted_iota(jnp.int32, (ROWS, SIDE), 1)
    for here, total in by_rows:
        gain = side_ref[here, :].astype(F32)[:, heads : heads + 1]
        block = jnp.where(lane == heads, total / gain, gw_ref[here, 3 * width :])
        gw_ref[here, 3 * width :] = jnp.where(lane == heads + 1, ggain_ref[here, :], block)
    for part in range(1, 3):
        at = part * width
        for back in backs:
            source = back[part + 2]
            grad = sum(
                dot(piece[index], source[:, i * piece.shape[1] : (i + 1) * piece.shape[1]], 0, 1)
                for i, piece, index in blocks_of(memory)
            )
            gw_ref[:, at : at + source.shape[0]] += grad
            at += source.shape[0]
    for number, piece, index in blocks_of(g_pieces):
        piece[index] = gw_ref[rows_at(owner_ref, number, ROWS), :].astype(BF16)


def input_kernel(owner_ref, xt_ref, inv_ref, side_ref, back_ref, gh_ref, *refs, heads):
    w_pieces, (gx_ref, w_ref) = refs[:-2], refs[-2:]
    for number, piece, index in blocks_of(w_pieces):
        w_ref[rows_at(owner_ref, number, ROWS), :] = piece[index]
    unit = xt_ref[...].astype(F32) * inv_ref[0:1, :]
    gain = side_ref[...].astype(F32)[:, heads : heads + 1]
    b = dot(w_ref[...], back_ref[...]) * gain
    out = gh_ref[...] + inv_ref[0:1, :] * (b - unit * jnp.mean(b * unit, axis=0, keepdims=True))
    gx_ref[...] = out.T


def finish_feed_kernel(*refs):
    *terms, down_ref, wo_ref, up_ref = refs
    low, width = down_ref.shape
    total = sum(term[0].astype(F32) for term in terms)
    down_ref[...] = total[:low]
    height = wo_ref.shape[0]
    wo_ref[...] = total[low : low + height]
    for chunk in range(up_ref.shape[1] // width):
        at = low + (chunk + 1) * height
        up_ref[:, chunk * width : (chunk + 1) * width] = total[at : at + height]


def finish_kernel(*refs):
    *terms, q_ref, k_ref, v_ref, gate_ref, one_ref, two_ref = refs
    height, width = q_ref.shape
    total = sum(term[0].astype(F32) for term in terms)
    for part, ref in enumerate((q_ref, k_ref, v_ref)):
        ref[...] = total[:, part * width : (part + 1) * width]
    heads = gate_ref.shape[0]
    side = total[:, 3 * width :].T
    gate_ref[...] = side[:heads]
    one_ref[...] = side[heads : heads + 1]
    two_ref[...] = side[heads + 1 : heads + 2]


def on_device(
    tokens,
    memory,
    lengths,
    neighbours,
    out_grad,
    gain_one,
    gain_two,
    w_query,
    w_key,
    w_value,
    w_gate,
    w_out,
    w_up,
    w_down,
    *,
    sizes,
):
    rows, width = tokens.shape
    heads = w_gate.shape[1]
    size = width // heads
    seg_count = lengths.shape[0]
    knn = neighbours.shape[1]
    shard = w_query.shape[0]
    ff = w_up.shape[1]
    chunks = ff // width
    tall = w_down.shape[0]
    scale = size ** (-0.5)
    own = memory.shape[0]
    slots = own * sizes["seq"]
    blocks = width // ROWS
    low = ff // blocks

    groups = groups_of(sizes)
    feed_groups = [[step] for step in groups[0]] + groups[1:]
    owner = owners(groups, sizes)
    direct = shard == ROWS
    kernel_owner = owner if direct else jnp.arange(blocks, dtype=jnp.int32)

    columns = 3 * width + SIDE
    feed_height = tall + shard * (1 + chunks)
    if direct:
        packed, feed_packed = call(
            pack_kernel,
            [((shard, columns), BF16), ((feed_height, width), BF16)],
            [WHOLE] * 9,
            micros=1,
            vmem=60,
        )(
            w_query,
            w_key,
            w_value,
            w_gate.T,
            gain_one[None],
            gain_two[None],
            w_down,
            w_out,
            w_up,
        )
    else:
        packed = jnp.concatenate(
            [
                w_query,
                w_key,
                w_value,
                w_gate,
                gain_one[:, None],
                gain_two[:, None],
                jnp.zeros((shard, SIDE - heads - 2), BF16),
            ],
            axis=1,
        )
        feed_packed = jnp.concatenate(
            [w_down, w_out] + [w_up[:, c * width : (c + 1) * width] for c in range(chunks)], axis=0
        )
    seq_group = [("seq", bit) for bit in bits_of(sizes["seq"])]
    memory_pieces = [memory[None]]
    for step in seq_group:
        memory_pieces = gather_stage(memory_pieces, [step], sizes)
    w_pieces = gather_stage([packed[None]], groups[0], sizes)

    ids = neighbours // own
    ids = place_of(ids, lax.axis_index("seq"), seq_group) * own + neighbours % own
    ids = jnp.pad(ids.T, ((0, 8 - knn), (0, 0)))
    big = (width, rows)
    lanes = (8, rows)
    feed_pieces = gather_stage([feed_packed[None]], feed_groups[0], sizes)
    w_pieces = gather_stage(w_pieces, groups[1], sizes, join=len(groups) > 2)
    feed_pieces = after(w_pieces[0], feed_pieces)
    feed_pieces = gather_stage(feed_pieces, feed_groups[1], sizes)
    x_in, g_in, ids = after((w_pieces[0], feed_pieces[0]), (tokens, out_grad, ids))
    prepared = call(
        functools.partial(prepare_kernel, count=knn),
        [
            (big, BF16, pltpu.HBM),
            (big, BF16, pltpu.HBM),
            (lanes, F32),
            ((slots, rows), BF16, pltpu.HBM),
            ((slots, rows), F32, pltpu.HBM),
        ],
        [WHOLE] * 3,
        micros=4,
    )(x_in, g_in, ids)
    xt, gt, inv_one, times, bias = prepared
    feed_pieces = after(w_pieces, feed_pieces)
    w_pieces = after(prepared, w_pieces)
    for at, group in enumerate(groups[2:], 2):
        w_pieces = gather_stage(w_pieces, group, sizes, join=at + 1 < len(groups))
    for group in feed_groups[2:-1]:
        feed_pieces = gather_stage(feed_pieces, group, sizes)

    def in_order(pieces):
        both = jnp.concatenate(pieces, axis=0)
        return jnp.zeros_like(both).at[owner].set(both)

    def split_rows(array, *heights):
        at, parts = 0, []
        for height in heights:
            parts.append(array[:, at : at + height].reshape(-1, width))
            at += height
        return parts

    if not direct:
        w_pieces = [in_order(w_pieces).reshape(blocks, ROWS, columns)]

    def to_send(pieces, *heights):
        if direct:
            return pieces
        array = pieces[0]
        if len(heights) > 1:
            parts = split_rows(array, low, *[ROWS] * (len(heights) - 1))
            parts = [part.reshape(-1, height, width) for part, height in zip(parts, heights)]
            array = jnp.concatenate(parts, axis=1)
        else:
            array = array.reshape(-1, heights[0], array.shape[2])
        array = array[owner]
        count = 1 << len(groups[-1])
        return jnp.split(array, count, axis=0)

    def head_block(part, cols, first=0):
        return pl.BlockSpec((size, cols), lambda h: (part * heads + first + h, 0))

    nt, qkv, mem_kv, side, mixed, ctx, rec, gate, lse, lsen = call(
        functools.partial(
            attend_kernel,
            pieces=len(w_pieces),
            mem_pieces=len(memory_pieces),
            heads=heads,
            seg_count=seg_count,
            scale=scale,
        ),
        [
            (big, BF16, pltpu.HBM),
            ((3 * width, rows), BF16, pltpu.VMEM),
            ((2 * width, slots), BF16, pltpu.VMEM),
            ((width, SIDE), BF16),
            (big, BF16, pltpu.VMEM),
            (big, F32, pltpu.VMEM),
            (big, F32, pltpu.VMEM),
            (lanes, F32),
            (lanes, F32),
            (lanes, F32),
        ],
        [SCALARS, SCALARS, FAR, WHOLE, FAR] + [WHOLE] * (len(w_pieces) + len(memory_pieces)),
        out_specs=[WHOLE] * 4 + [head_block(0, rows)] * 3 + [WHOLE] * 3,
        grid=(heads,),
        scratch=[
            pltpu.VMEM((width, columns), BF16),
            pltpu.VMEM(big, BF16),
            pltpu.VMEM((slots, rows), BF16),
            pltpu.SemaphoreType.DMA((2,)),
        ],
        micros=22,
        vmem=24,
    )(kernel_owner, lengths, far(xt), inv_one, far(times), *w_pieces, *memory_pieces)

    feed_pieces = after(mixed, feed_pieces)
    feed_pieces = gather_stage(feed_pieces, groups[-1], sizes, join=False)
    if not direct:
        parts = split_rows(in_order(feed_pieces), tall, *[shard] * (1 + chunks))
        feed_pieces = [jnp.concatenate([part.reshape(blocks, -1, width) for part in parts], axis=1)]
    pieces = len(feed_pieces)
    sends = 1 << len(groups[-1]) if direct else 1
    feed_block = (blocks // sends,) + feed_pieces[0].shape[1:]
    outs = call(
        functools.partial(feed_kernel, heads=heads, pieces=pieces, sends=sends),
        [
            ((rows, width), BF16),
            (big, F32),
            (big, BF16),
            (lanes, F32),
            (lanes, F32),
            (lanes, F32),
            ((width, SIDE), F32),
        ]
        + [(feed_block, BF16)] * sends,
        [SCALARS] + [WHOLE] * (7 + pieces),
        scratch=[
            pltpu.VMEM(shape, BF16) for shape in ((width, width), (width, ff), (ff, width))
        ],
        micros=20,
        vmem=22,
    )(kernel_owner, xt, gt, mixed, ctx, rec, gate, side, *feed_pieces)
    block_out, grad_hidden, dm, dc, dn, dlogit, ggain_two = outs[:7]
    late = to_send(outs[7:], tall, *[shard] * (1 + chunks))
    late_at = len(feed_groups)

    backs = []
    first = 0
    for count in (1, heads - 1):
        late_at -= 1
        moving = sum_terms(late, feed_groups[late_at], sizes)
        outs = call(
            functools.partial(attend_back_kernel, first=first, seg_count=seg_count, scale=scale),
            [((size * count, rows), BF16)] * 3 + [((size * count, slots), BF16)] * 2,
            [
                SCALARS,
                head_block(0, rows, first),
                head_block(1, rows, first),
                head_block(2, rows, first),
                head_block(0, slots, first),
                head_block(1, slots, first),
                head_block(0, rows, first),
            ]
            + [WHOLE] * 6,
            out_specs=[head_block(0, rows)] * 3 + [head_block(0, slots)] * 2,
            grid=(count,),
            scratch=[pltpu.VMEM((size, rows), F32)] * 2 + [pltpu.VMEM((size, slots), F32)] * 2,
            micros=5 * count,
        )(lengths, qkv, qkv, qkv, mem_kv, mem_kv, dm, gate, bias, lse, lsen, dc, dn)
        first += count
        late = add_terms(moving, feed_groups[late_at - 1])
        outs, dm = after(late, (outs, dm))
        backs.append(outs)
    late_at -= 1
    moving = sum_terms(late, feed_groups[late_at], sizes)

    pieces = len(w_pieces)
    *early, back = call(
        functools.partial(
            weight_kernel,
            calls=len(backs),
            pieces=pieces,
            mem_pieces=len(memory_pieces),
            sends=sends,
            heads=heads,
        ),
        [((blocks // sends, ROWS, columns), BF16)] * sends + [((columns, rows), BF16)],
        [SCALARS] + [WHOLE] * (4 + len(memory_pieces) + 5 * len(backs) + pieces),
        scratch=[pltpu.VMEM((width, columns), F32)],
        micros=6,
    )(
        kernel_owner,
        nt,
        side,
        dlogit,
        ggain_two,
        *memory_pieces,
        *[b for back in backs for b in back],
        *w_pieces,
    )
    early = to_send(early, shard)
    early = sum_terms(early, groups[-1], sizes)
    for at in reversed(range(len(groups) - 1)):
        early = add_terms(early, groups[at])
        if at + 2 == len(groups):
            back = after(early, back)
        early = sum_terms(early, groups[at], sizes)
    (grad_tokens,) = call(
        functools.partial(input_kernel, heads=heads),
        [((rows, width), F32)],
        [SCALARS] + [WHOLE] * (5 + pieces),
        scratch=[pltpu.VMEM((width, columns), BF16)],
        micros=6,
    )(kernel_owner, xt, inv_one, side, back, grad_hidden, *w_pieces)

    moving = after(grad_tokens, moving)
    while late_at:
        late_at -= 1
        moving = sum_terms(add_terms(moving, feed_groups[late_at]), feed_groups[late_at], sizes)
    late = moving

    if direct:
        grad_down, grad_out, grad_up = call(
            finish_feed_kernel,
            [((tall, width), F32), ((shard, width), F32), ((shard, ff), F32)],
            [WHOLE] * len(late),
            micros=1,
        )(*late)
        grad_query, grad_key, grad_value, grad_gate, grad_one, grad_two = call(
            finish_kernel,
            [((shard, width), F32)] * 3 + [((heads, shard), F32)] + [((1, shard), F32)] * 2,
            [WHOLE] * len(early),
            micros=1,
        )(*early)
        grad_gate, grad_one, grad_two = grad_gate.T, grad_one[0], grad_two[0]
    else:
        late = sum(term[0].astype(F32) for term in late)
        early = sum(term[0].astype(F32) for term in early)
        grad_down, grad_out = late[:tall], late[tall : tall + shard]
        grad_up = jnp.concatenate(
            [late[tall + shard * (1 + c) : tall + shard * (2 + c)] for c in range(chunks)], axis=1
        )
        grad_query, grad_key, grad_value = (
            early[:, at : at + width] for at in range(0, 3 * width, width)
        )
        side = early[:, 3 * width :]
        grad_gate, grad_one, grad_two = side[:, :heads], side[:, heads], side[:, heads + 1]
    return (
        block_out,
        grad_tokens,
        grad_one,
        grad_two,
        grad_query,
        grad_key,
        grad_value,
        grad_gate,
        grad_out,
        grad_up,
        grad_down,
    )


def solution(mesh):
    row_split, vector = P(("dp", "seq"), None), P(("dp", "seq"))
    in_specs = (row_split, row_split, vector, row_split, row_split, vector, vector) + (row_split,) * 7
    out_specs = (row_split, row_split, vector, vector) + (row_split,) * 7
    return jax.shard_map(
        functools.partial(on_device, sizes=dict(mesh.shape)),
        mesh=mesh,
        in_specs=in_specs,
        out_specs=out_specs,
        check_vma=False,
    )
```

```python
import functools
import math

import jax
import jax.numpy as jnp
from jax import lax
from jax.experimental import pallas as pl
from jax.experimental.pallas import tpu as pltpu
from jax.sharding import PartitionSpec as P


EPSILON = 1e-06
MASKED = -1e30
LOG2E = math.log2(math.e)
F32 = jnp.float32
BF16 = jnp.bfloat16
SIDE = 128
TILE = 256
ROWS = 16
TINY = 2.0**-80
PER_MICRO = 1.1e9


def dot(left, right, left_dim=1, right_dim=0):
    return lax.dot_general(
        left, right, (((left_dim,), (right_dim,)), ((), ())), preferred_element_type=F32
    )


def call(kernel, outs, in_specs, out_specs=None, grid=None, scratch=(), micros=0, vmem=16):
    options = {} if grid is None else dict(grid=grid)
    if out_specs is None:
        out_specs = [WHOLE] * len(outs)
    return pl.pallas_call(
        kernel,
        out_shape=[
            where[0](shape, kind) if where else jax.ShapeDtypeStruct(shape, kind)
            for shape, kind, *where in outs
        ],
        in_specs=in_specs,
        out_specs=out_specs,
        scratch_shapes=list(scratch),
        compiler_params=pltpu.CompilerParams(vmem_limit_bytes=vmem << 20),
        cost_estimate=pl.CostEstimate(
            flops=int(micros * PER_MICRO), bytes_accessed=0, transcendentals=0
        ),
        **options,
    )


WHOLE = pl.BlockSpec(memory_space=pltpu.VMEM)
SCALARS = pl.BlockSpec(memory_space=pltpu.SMEM)
FAR = pl.BlockSpec(memory_space=pltpu.HBM)


def far(array):
    return pltpu.with_memory_space_constraint(array, pltpu.HBM)


def three_parts(value):
    high = value.astype(BF16).astype(F32)
    rest = value - high
    middle = rest.astype(BF16).astype(F32)
    return high, middle, rest - middle


def pick_rows(rows, count):
    shape = (count, rows[0].shape[1])
    index = lax.broadcasted_iota(jnp.int32, shape, 0)
    block = jnp.zeros(shape, F32)
    for at, row in enumerate(rows):
        block = jnp.where(index == at, row, block)
    return block


def bits_of(size):
    return [1 << b for b in reversed(range(size.bit_length() - 1))]


def groups_of(sizes):
    steps = [("dp", bit) for bit in bits_of(sizes["dp"])] + [("seq", bit) for bit in bits_of(sizes["seq"])]
    return [steps[at : at + 2] for at in range(0, len(steps), 2)]


def swap(array, group, mask, sizes):
    n_seq = sizes["seq"]
    apart = 0
    for at, (axis, bit) in enumerate(group):
        if mask >> at & 1:
            apart ^= bit * (n_seq if axis == "dp" else 1)
    pairs = [(i, i ^ apart) for i in range(sizes["dp"] * n_seq)]
    return lax.ppermute(array, ("dp", "seq"), pairs)


def gather_stage(pieces, group, sizes, join=True):
    if join and len(pieces) > 1:
        pieces = [jnp.concatenate(pieces, axis=0)]
    masks = range(1, 1 << len(group))
    return pieces + [swap(piece, group, mask, sizes) for mask in masks for piece in pieces]


def sum_terms(pieces, group, sizes):
    return [pieces[0]] + [swap(pieces[mask], group, mask, sizes) for mask in range(1, 1 << len(group))]


def add_terms(terms, group):
    count = 1 << len(group)
    step = terms[0].shape[0] // count
    return [
        sum(term[m * step : (m + 1) * step].astype(F32) for term in terms).astype(BF16)
        for m in range(count)
    ]


def after(earlier, later):
    return lax.optimization_barrier((earlier, later))[1]


def owners(groups, sizes):
    n_seq = sizes["seq"]
    at = jnp.arange(sizes["dp"] * n_seq, dtype=jnp.int32)
    own = {"dp": lax.axis_index("dp"), "seq": lax.axis_index("seq")}
    for number, (axis, bit) in enumerate(step for group in groups for step in group):
        own[axis] = own[axis] ^ jnp.where((at >> number) & 1, bit, 0)
    return own["dp"] * n_seq + own["seq"]


def place_of(ids, own_index, group_steps):
    apart = ids ^ own_index
    place = jnp.zeros_like(ids)
    for at, (_, bit) in enumerate(group_steps):
        place = place + jnp.where((apart & bit) != 0, 1 << at, 0)
    return place


def blocks_of(pieces):
    number = 0
    for piece in pieces:
        for index in range(piece.shape[0]):
            yield number, piece, index
            number += 1


def rows_at(owner_ref, number, height):
    return pl.ds(pl.multiple_of(owner_ref[number] * height, height), height)


def pack_kernel(
    q_ref, k_ref, v_ref, gate_ref, one_ref, two_ref, down_ref, wo_ref, up_ref, out_ref, feed_ref
):
    height, width = q_ref.shape
    low = down_ref.shape[0]
    feed_ref[:low, :] = down_ref[...]
    feed_ref[low : low + height, :] = wo_ref[...]
    for chunk in range(up_ref.shape[1] // width):
        at = low + (chunk + 1) * height
        feed_ref[at : at + height, :] = up_ref[:, chunk * width : (chunk + 1) * width]
    heads = gate_ref.shape[0]
    for part, ref in enumerate((q_ref, k_ref, v_ref)):
        out_ref[:, part * width : (part + 1) * width] = ref[...]
    row = lax.broadcasted_iota(jnp.int32, (height, height), 0)
    column = lax.broadcasted_iota(jnp.int32, (height, height), 1)
    lane = lax.broadcasted_iota(jnp.int32, (height, SIDE), 1)
    spread = lax.broadcasted_iota(jnp.int32, (heads, SIDE), 0) == lax.broadcasted_iota(
        jnp.int32, (heads, SIDE), 1
    )
    side = dot(gate_ref[...].astype(F32), jnp.where(spread, 1.0, 0.0), 0, 0)
    for at, ref in enumerate((one_ref, two_ref)):
        gains = jnp.where(row == column, ref[...].astype(F32), 0.0)
        side = jnp.where(lane == heads + at, jnp.sum(gains, axis=1, keepdims=True), side)
    out_ref[:, 3 * width :] = side.astype(BF16)


def prepare_kernel(
    x_ref, g_ref, ids_ref,
    xt_ref, gt_ref, inv_ref, times_ref,
    *, count,
):
    xt = x_ref[...].astype(F32).T
    xt_ref[...] = xt.astype(BF16)
    gt_ref[...] = g_ref[...].astype(F32).T.astype(BF16)
    inv = lax.rsqrt(jnp.mean(xt * xt, axis=0, keepdims=True) + EPSILON)
    inv_ref[...] = jnp.broadcast_to(inv, inv_ref.shape)
    slots, rows = times_ref.shape
    step = 128

    def body(i, _):
        at = pl.multiple_of(i * step, step)
        slot = lax.broadcasted_iota(jnp.int32, (step, rows), 0) + at
        times = jnp.zeros((step, rows), F32)
        for j in range(count):
            times = times + jnp.where(ids_ref[j : j + 1, :] == slot, 1.0, 0.0)
        times_ref[pl.ds(at, step), :] = times.astype(BF16)
        return 0

    lax.fori_loop(0, slots // step, body, 0)


def local_penalty(lengths_ref, rows, seg_count):
    seg_len = rows // seg_count
    lane = lax.broadcasted_iota(jnp.int32, (1, rows), 1)
    last = jnp.zeros((1, rows), jnp.int32)
    for seg in range(seg_count):
        last = jnp.where(lane // seg_len == seg, seg * seg_len + lengths_ref[seg], last)
    return jnp.where(lane < last, 0.0, MASKED)


def causal_bias(size):
    key = lax.broadcasted_iota(jnp.int32, (size, size), 0)
    query = lax.broadcasted_iota(jnp.int32, (size, size), 1)
    return jnp.where(key <= query, 0.0, MASKED)


def longest(keys):
    keys = keys.astype(F32)
    return jnp.max(jnp.sum(keys * keys, axis=0, keepdims=True), axis=1, keepdims=True)


def attend_kernel(
    owner_ref, lengths_ref, xt_far, inv_ref, times_far, *refs,
    pieces, mem_pieces, heads, seg_count, scale,
):
    w_pieces, memory, refs = refs[:pieces], refs[pieces : pieces + mem_pieces], refs[mem_pieces:]
    (
        nt_ref, qkv_ref, mem_ref, side_ref, mixed_ref, ctx_ref, rec_ref, exp_ref, gate_ref, lse_ref, lsen_ref,
        far_ref, near_ref, flags_ref, w_ref, xt_ref, times_ref, sems,
    ) = refs[pieces:]
    head = pl.program_id(0)
    width, rows = xt_ref.shape
    slots = times_ref.shape[0]
    size = width // heads
    seg_len = rows // seg_count

    @pl.when(head == 0)
    def _():
        x_copy = pltpu.make_async_copy(xt_far, xt_ref, sems.at[0])
        times_copy = pltpu.make_async_copy(times_far, times_ref, sems.at[1])
        x_copy.start()
        times_copy.start()
        for number, piece, index in blocks_of(w_pieces):
            w_ref[rows_at(owner_ref, number, piece.shape[1]), :] = piece[index]
        x_copy.wait()
        side_ref[...] = w_ref[:, 3 * width :]
        gain = side_ref[...].astype(F32)[:, heads : heads + 1]
        normed = (xt_ref[...].astype(F32) * inv_ref[0:1, :] * gain).astype(BF16)
        nt_ref[...] = normed
        for part in range(3):
            columns = slice(part * width, (part + 1) * width)
            qkv_ref[columns, :] = dot(w_ref[:, columns], normed, 0, 0).astype(BF16)
        gate_ref[...] = jax.nn.sigmoid(dot(side_ref[...], normed, 0, 0)[0:heads])
        for part in range(2):
            columns = slice((part + 1) * width, (part + 2) * width)
            for number, piece, index in blocks_of(memory):
                own = piece.shape[1]
                there = slice(number * own, (number + 1) * own)
                mem_ref[part * width : (part + 1) * width, there] = dot(
                    w_ref[:, columns], piece[index], 0, 1
                ).astype(BF16)
        times_copy.wait()

    def head_of(ref, part):
        return ref[pl.ds(pl.multiple_of(part * width + head * size, size), size), :]

    q, k, v = (head_of(qkv_ref, part) for part in range(3))
    mk, mv = (head_of(mem_ref, part) for part in range(2))
    gate = gate_ref[pl.ds(head, 1), :]
    penalty = local_penalty(lengths_ref, rows, seg_count)
    causal = causal_bias(seg_len)
    q = q.astype(F32) * (scale * LOG2E)
    q_high = q.astype(BF16)
    q_low = (q - q_high.astype(F32)).astype(BF16)
    reach = jnp.sqrt(
        jnp.sum(q * q, axis=0, keepdims=True) * jnp.maximum(longest(k), longest(mk))
    ) * (1.0 + 2.0**-10)
    ones = jnp.ones((1, rows), F32)
    mem_three = pick_rows([jnp.ones((1, slots), F32)] * 3, 16).astype(BF16)
    queries = jnp.concatenate(
        [q_high, q_low, pick_rows([*three_parts(-reach), ones], 16).astype(BF16)], axis=0
    )
    keys = jnp.concatenate([k, k, pick_rows([ones, ones, ones, penalty], 16).astype(BF16)], axis=0)
    mem_keys = jnp.concatenate([mk, mk, mem_three], axis=0)
    values = jnp.concatenate([v, jnp.ones((16, rows), BF16)], axis=0)
    mem_values = jnp.concatenate([mv, jnp.ones((16, slots), BF16)], axis=0)

    def finish(here, total, near_total, peak, near_peak):
        mass, near_mass = total[size : size + 1], near_total[size : size + 1]
        context = total[:size] / mass
        recalled = near_total[:size] / near_mass
        ctx_ref[:, here] = context
        rec_ref[:, here] = recalled
        lse_ref[pl.ds(head, 1), here] = peak + jnp.log2(mass)
        lsen_ref[pl.ds(head, 1), here] = near_peak + jnp.log2(near_mass)
        share = gate[:, here]
        far_ref[pl.ds(head, 1), here] = (1.0 - share) / mass
        near_ref[pl.ds(head, 1), here] = share / near_mass
        mixed_ref[:, here] = ((1.0 - share) * context + share * recalled).astype(BF16)
        return jnp.minimum(mass, near_mass)

    segments = [slice(at, at + seg_len) for at in range(0, rows, seg_len)]
    least = jnp.full((1, seg_len), 1.0, F32)
    for here in segments:
        all_keys = jnp.concatenate([mem_keys, keys[:, here]], axis=1)
        all_values = jnp.concatenate([mem_values, values[:, here]], axis=1)
        score = dot(all_keys, queries[:, here], 0, 0)
        exp_mem = jnp.exp2(score[:slots]).astype(BF16)
        exp_own = jnp.exp2(score[slots:] + causal).astype(BF16)
        exp_ref[:slots, here] = exp_mem
        exp_ref[slots:, here] = exp_own
        total = dot(all_values, jnp.concatenate([exp_mem, exp_own], axis=0))
        near_total = dot(mem_values, exp_mem * times_ref[:, here])
        least = jnp.minimum(
            least, finish(here, total, near_total, reach[:, here], reach[:, here])
        )

    far_off = jnp.logical_not(jnp.min(least) > TINY)
    flags_ref[head] = far_off.astype(jnp.int32)

    @pl.when(far_off)
    def _():
        zero = jnp.zeros((1, rows), F32)
        plain = jnp.concatenate(
            [q_high, q_low, pick_rows([zero, zero, zero, ones], 16).astype(BF16)], axis=0
        )
        for here in segments:
            score = dot(mem_keys, plain[:, here], 0, 0)
            score_own = dot(keys[:, here], plain[:, here], 0, 0) + causal
            near = jnp.where(times_ref[:, here] > 0, score, MASKED)
            near_peak = jnp.max(near, axis=0, keepdims=True)
            peak = jnp.maximum(
                jnp.max(score, axis=0, keepdims=True), jnp.max(score_own, axis=0, keepdims=True)
            )
            total = dot(mem_values, jnp.exp2(score - peak).astype(BF16))
            total = total + dot(values[:, here], jnp.exp2(score_own - peak).astype(BF16))
            exp_near = jnp.exp2(near - near_peak).astype(BF16) * times_ref[:, here]
            finish(here, total, dot(mem_values, exp_near), peak, near_peak)


def feed_kernel(
    owner_ref, xt_ref, gt_ref, mixed_ref, ctx_ref, rec_ref, gate_ref, side_ref, *refs, heads, pieces, sends
):
    w_pieces, refs = refs[:pieces], refs[pieces:]
    (block_ref, gh_ref, dm_ref, dc_ref, dn_ref, dlogit_ref, ggain_ref), refs = refs[:7], refs[7:]
    g_pieces, (wo_ref, up_ref, down_ref) = refs[:sends], refs[sends:]
    width, rows = xt_ref.shape
    chunks = up_ref.shape[1] // width
    size = width // heads
    low = down_ref.shape[0] // width * ROWS
    for number, piece, index in blocks_of(w_pieces):
        block = piece[index]
        down_ref[rows_at(owner_ref, number, low), :] = block[:low]
        here = rows_at(owner_ref, number, ROWS)
        wo_ref[here, :] = block[low : low + ROWS]
        for chunk in range(chunks):
            at = low + (chunk + 1) * ROWS
            up_ref[here, chunk * width : (chunk + 1) * width] = block[at : at + ROWS]

    gain = side_ref[...].astype(F32)[:, heads + 1 : heads + 2]
    hidden = xt_ref[...].astype(F32) + dot(wo_ref[...], mixed_ref[...], 0, 0)
    inv = lax.rsqrt(jnp.mean(hidden * hidden, axis=0, keepdims=True) + EPSILON)
    unit = hidden * inv
    n2 = (unit * gain).astype(BF16)
    grad = gt_ref[...]
    coef = math.sqrt(2.0 / math.pi)

    part_size = width // 2
    parts = [slice(at, at + part_size) for at in range(0, up_ref.shape[1], part_size)]

    def first(part):
        return dot(up_ref[:, part], n2, 0, 0), dot(down_ref[part, :], grad)

    def second(pre, grad_act):
        square = pre * pre
        half = 0.5 + 0.5 * jnp.tanh(pre * (coef + (0.044715 * coef) * square))
        act = pre * half
        slope = half + act * (1.0 - half) * (2.0 * coef + (6.0 * 0.044715 * coef) * square)
        return act.astype(BF16), (grad_act * slope).astype(BF16)

    ready = first(parts[0])
    out = gn2 = None
    for at, part in enumerate(parts):
        later = first(parts[at + 1]) if at + 1 < len(parts) else None
        act, grad_pre = second(*ready)
        ready = later
        out_part = dot(down_ref[part, :], act, 0, 0)
        gn2_part = dot(up_ref[:, part], grad_pre)
        out = out_part if out is None else out + out_part
        gn2 = gn2_part if gn2 is None else gn2 + gn2_part
        down_ref[part, :] = dot(act, grad, 1, 1).astype(BF16)
        up_ref[:, part] = dot(n2, grad_pre, 1, 1).astype(BF16)

    block_ref[...] = (hidden + out).T.astype(BF16)
    ggain_ref[...] = jnp.broadcast_to(jnp.sum(gn2 * unit, axis=1, keepdims=True), ggain_ref.shape)
    a = gn2 * gain
    grad_hidden = grad.astype(F32) + inv * (a - unit * jnp.mean(a * unit, axis=0, keepdims=True))
    gh_ref[...] = grad_hidden
    branch = grad_hidden.astype(BF16)
    grad_mixed = dot(wo_ref[...], branch)
    wo_ref[...] = dot(mixed_ref[...], branch, 1, 1).astype(BF16)
    for number, piece, index in blocks_of(g_pieces):
        piece[index, :low] = down_ref[rows_at(owner_ref, number, low), :]
        here = rows_at(owner_ref, number, ROWS)
        piece[index, low : low + ROWS] = wo_ref[here, :]
        for chunk in range(chunks):
            at = low + (chunk + 1) * ROWS
            piece[index, at : at + ROWS] = up_ref[here, chunk * width : (chunk + 1) * width]
    rounded = grad_mixed.astype(BF16)
    dm_ref[...] = rounded
    rounded = rounded.astype(F32)
    for head in range(heads):
        part = slice(head * size, (head + 1) * size)
        ctx, rec = ctx_ref[part, :], rec_ref[part, :]
        dc_ref[head : head + 1, :] = jnp.sum(rounded[part] * ctx, axis=0, keepdims=True)
        dn_ref[head : head + 1, :] = jnp.sum(rounded[part] * rec, axis=0, keepdims=True)
        share = gate_ref[head : head + 1, :]
        moved = jnp.sum(grad_mixed[part] * (rec - ctx), axis=0, keepdims=True)
        dlogit_ref[head : head + 1, :] = moved * share * (1.0 - share)


def attend_back_kernel(
    flags_ref, lengths_ref, q_ref, k_ref, v_ref, mk_ref, mv_ref, dm_ref, exp_ref, gate_ref, times_ref,
    lse_ref, lsen_ref, far_ref, near_ref, dc_ref, dn_ref,
    dq_ref, dk_ref, dv_ref, dmk_ref, dmv_ref,
    dk_sum, dv_sum, dmk_sum, dmv_sum,
    *, first, seg_count, scale,
):
    size, rows = q_ref.shape
    seg_len = rows // seg_count
    row = pl.ds(pl.program_id(0) + first, 1)
    dc = dc_ref[row, :]
    apart = dc - dn_ref[row, :]
    slots = mk_ref.shape[1]
    ones = jnp.ones((1, rows), F32)
    mem_three = pick_rows([jnp.ones((1, slots), F32)] * 3, 16).astype(BF16)
    grads = jnp.concatenate([dm_ref[...], pick_rows(three_parts(-dc), 16).astype(BF16)], axis=0)
    values = jnp.concatenate([v_ref[...], pick_rows([ones] * 3, 16).astype(BF16)], axis=0)
    mem_values = jnp.concatenate([mv_ref[...], mem_three], axis=0)

    far_off = flags_ref[pl.program_id(0) + first] != 0

    @pl.when(jnp.logical_not(far_off))
    def _():
        far_scale, near_scale = far_ref[row, :], near_ref[row, :]
        near_apart = near_scale * apart
        for at in range(0, rows, TILE):
            here = slice(at, at + TILE)
            start = at // seg_len * seg_len
            there = slice(start, at + TILE)
            n = at + TILE - start
            q_here, dm_here = q_ref[:, here].T, dm_ref[:, here].T
            moved = dot(jnp.concatenate([mem_values, values[:, there]], axis=1), grads[:, here], 0, 0)
            exps = exp_ref[:slots, here].astype(F32)
            times = times_ref[:, here].astype(F32)
            mix = far_scale[:, here] + near_scale[:, here] * times
            weight = exps * mix
            dscore = (exps * (mix * moved[:slots] + near_apart[:, here] * times)).astype(BF16)
            wl = exp_ref[slots : slots + n, here].astype(F32) * far_scale[:, here]
            dl = (wl * moved[slots:]).astype(BF16)
            weight = jnp.concatenate([weight.astype(BF16), wl.astype(BF16)], axis=0)
            dscore = jnp.concatenate([dscore, dl], axis=0)
            grad_v = dot(weight, dm_here).T
            grad_k = dot(dscore, q_here).T
            dq = dot(jnp.concatenate([mk_ref[...], k_ref[:, there]], axis=1), dscore)
            if at == 0:
                dmv_sum[...] = grad_v[:, :slots]
                dmk_sum[...] = grad_k[:, :slots]
            else:
                dmv_sum[...] += grad_v[:, :slots]
                dmk_sum[...] += grad_k[:, :slots]
            if n == TILE:
                dv_sum[:, there] = grad_v[:, slots:]
                dk_sum[:, there] = grad_k[:, slots:]
            else:
                dv_sum[:, start:at] += grad_v[:, slots:slots + n - TILE]
                dk_sum[:, start:at] += grad_k[:, slots:slots + n - TILE]
                dv_sum[:, here] = grad_v[:, slots + n - TILE:]
                dk_sum[:, here] = grad_k[:, slots + n - TILE:]
            dq_ref[:, here] = (scale * dq).astype(BF16)

    @pl.when(far_off)
    def _():
        penalty = local_penalty(lengths_ref, rows, seg_count)
        causal = causal_bias(TILE)
        q = q_ref[...].astype(F32) * (scale * LOG2E)
        q_high = q.astype(BF16)
        q_low = (q - q_high.astype(F32)).astype(BF16)
        share = gate_ref[row, :]
        shift = jnp.log2(jnp.maximum(1.0 - share, 2.0**-60)) - lse_ref[row, :]
        near_shift = jnp.log2(jnp.maximum(share, 2.0**-60)) - lsen_ref[row, :] - shift
        queries = jnp.concatenate(
            [q_high, q_low, pick_rows([*three_parts(shift), ones], 16).astype(BF16)], axis=0
        )
        keys = jnp.concatenate(
            [k_ref[...], k_ref[...], pick_rows([ones, ones, ones, penalty], 16).astype(BF16)], axis=0
        )
        mem_keys = jnp.concatenate([mk_ref[...], mk_ref[...], mem_three], axis=0)
        for at in range(0, rows, TILE):
            here = slice(at, at + TILE)
            start = at // seg_len * seg_len
            q_here, dm_here = q_ref[:, here].T, dm_ref[:, here].T
            score = dot(mem_keys, queries[:, here], 0, 0)
            moved = dot(mem_values, grads[:, here], 0, 0)
            far = jnp.exp2(score)
            times = times_ref[:, here].astype(F32)
            bias = jnp.where(times > 0.0, jnp.log2(times), MASKED)
            near = jnp.exp2(score + (bias + near_shift[:, here]))
            weight = far + near
            dscore = (weight * moved + near * apart[:, here]).astype(BF16)
            grad_mv = dot(weight.astype(BF16), dm_here).T
            grad_mk = dot(dscore, q_here).T
            dq = dot(mk_ref[...], dscore)
            if at == 0:
                dmv_sum[...] = grad_mv
                dmk_sum[...] = grad_mk
            else:
                dmv_sum[...] += grad_mv
                dmk_sum[...] += grad_mk
            for block in range(start, at + TILE, TILE):
                there = slice(block, block + TILE)
                score = dot(keys[:, there], queries[:, here], 0, 0)
                if block == at:
                    score = score + causal
                weight = jnp.exp2(score)
                dscore = (weight * dot(values[:, there], grads[:, here], 0, 0)).astype(BF16)
                grad_v = dot(weight.astype(BF16), dm_here).T
                grad_k = dot(dscore, q_here).T
                dq = dq + dot(k_ref[:, there], dscore)
                if block == at:
                    dv_sum[:, there] = grad_v
                    dk_sum[:, there] = grad_k
                else:
                    dv_sum[:, there] += grad_v
                    dk_sum[:, there] += grad_k
            dq_ref[:, here] = (scale * dq).astype(BF16)

    dk_ref[...] = (scale * dk_sum[...]).astype(BF16)
    dv_ref[...] = dv_sum[...].astype(BF16)
    dmk_ref[...] = (scale * dmk_sum[...]).astype(BF16)
    dmv_ref[...] = dmv_sum[...].astype(BF16)


def weight_kernel(
    owner_ref, nt_ref, side_ref, dlogit_ref, ggain_ref, *refs, calls, pieces, mem_pieces, sends, heads
):
    memory, refs = refs[:mem_pieces], refs[mem_pieces:]
    backs = [refs[5 * at : 5 * at + 5] for at in range(calls)]
    refs = refs[5 * calls :]
    w_pieces, refs = refs[:pieces], refs[pieces:]
    g_pieces, (back_ref, gw_ref) = refs[:sends], refs[sends:]
    width, rows = nt_ref.shape
    for part in range(3):
        at = part * width
        for back in backs:
            back_ref[at : at + back[part].shape[0], :] = back[part][...]
            at += back[part].shape[0]
    side = jnp.concatenate([dlogit_ref[...], jnp.zeros((SIDE - heads, rows), F32)], axis=0)
    back_ref[3 * width :, :] = side.astype(BF16)
    normed = nt_ref[...]
    for part in range(3):
        columns = slice(part * width, (part + 1) * width)
        gw_ref[:, columns] = dot(normed, back_ref[columns, :], 1, 1)
    gw_ref[:, 3 * width :] = dot(normed, back_ref[3 * width :, :], 1, 1)
    by_rows = []
    for number, piece, index in blocks_of(w_pieces):
        here = rows_at(owner_ref, number, ROWS)
        by_rows.append((here, jnp.sum(piece[index].astype(F32) * gw_ref[here, :], axis=1, keepdims=True)))
    lane = lax.broadcasted_iota(jnp.int32, (ROWS, SIDE), 1)
    for here, total in by_rows:
        gain = side_ref[here, :].astype(F32)[:, heads : heads + 1]
        block = jnp.where(lane == heads, total / gain, gw_ref[here, 3 * width :])
        gw_ref[here, 3 * width :] = jnp.where(lane == heads + 1, ggain_ref[here, :], block)
    for part in range(1, 3):
        at = part * width
        for back in backs:
            source = back[part + 2]
            grad = sum(
                dot(piece[index], source[:, i * piece.shape[1] : (i + 1) * piece.shape[1]], 0, 1)
                for i, piece, index in blocks_of(memory)
            )
            gw_ref[:, at : at + source.shape[0]] += grad
            at += source.shape[0]
    for number, piece, index in blocks_of(g_pieces):
        piece[index] = gw_ref[rows_at(owner_ref, number, ROWS), :].astype(BF16)


def input_kernel(owner_ref, xt_ref, inv_ref, side_ref, back_ref, gh_ref, *refs, heads):
    w_pieces, (gx_ref, w_ref) = refs[:-2], refs[-2:]
    for number, piece, index in blocks_of(w_pieces):
        w_ref[rows_at(owner_ref, number, ROWS), :] = piece[index]
    unit = xt_ref[...].astype(F32) * inv_ref[0:1, :]
    gain = side_ref[...].astype(F32)[:, heads : heads + 1]
    b = dot(w_ref[...], back_ref[...]) * gain
    out = gh_ref[...] + inv_ref[0:1, :] * (b - unit * jnp.mean(b * unit, axis=0, keepdims=True))
    gx_ref[...] = out.T


def finish_feed_kernel(*refs):
    *terms, down_ref, wo_ref, up_ref = refs
    low, width = down_ref.shape
    total = sum(term[0].astype(F32) for term in terms)
    down_ref[...] = total[:low]
    height = wo_ref.shape[0]
    wo_ref[...] = total[low : low + height]
    for chunk in range(up_ref.shape[1] // width):
        at = low + (chunk + 1) * height
        up_ref[:, chunk * width : (chunk + 1) * width] = total[at : at + height]


def finish_kernel(*refs):
    *terms, q_ref, k_ref, v_ref, gate_ref, one_ref, two_ref = refs
    height, width = q_ref.shape
    total = sum(term[0].astype(F32) for term in terms)
    for part, ref in enumerate((q_ref, k_ref, v_ref)):
        ref[...] = total[:, part * width : (part + 1) * width]
    heads = gate_ref.shape[0]
    side = total[:, 3 * width :].T
    gate_ref[...] = side[:heads]
    one_ref[...] = side[heads : heads + 1]
    two_ref[...] = side[heads + 1 : heads + 2]


def on_device(
    tokens,
    memory,
    lengths,
    neighbours,
    out_grad,
    gain_one,
    gain_two,
    w_query,
    w_key,
    w_value,
    w_gate,
    w_out,
    w_up,
    w_down,
    *,
    sizes,
):
    rows, width = tokens.shape
    heads = w_gate.shape[1]
    size = width // heads
    seg_count = lengths.shape[0]
    knn = neighbours.shape[1]
    shard = w_query.shape[0]
    ff = w_up.shape[1]
    chunks = ff // width
    tall = w_down.shape[0]
    scale = size ** (-0.5)
    own = memory.shape[0]
    slots = own * sizes["seq"]
    blocks = width // ROWS
    low = ff // blocks

    groups = groups_of(sizes)
    feed_groups = [[step] for step in groups[0]] + groups[1:]
    owner = owners(groups, sizes)
    direct = shard == ROWS
    kernel_owner = owner if direct else jnp.arange(blocks, dtype=jnp.int32)

    columns = 3 * width + SIDE
    feed_height = tall + shard * (1 + chunks)
    if direct:
        packed, feed_packed = call(
            pack_kernel,
            [((shard, columns), BF16), ((feed_height, width), BF16)],
            [WHOLE] * 9,
            micros=1,
            vmem=60,
        )(
            w_query,
            w_key,
            w_value,
            w_gate.T,
            gain_one[None],
            gain_two[None],
            w_down,
            w_out,
            w_up,
        )
    else:
        packed = jnp.concatenate(
            [
                w_query,
                w_key,
                w_value,
                w_gate,
                gain_one[:, None],
                gain_two[:, None],
                jnp.zeros((shard, SIDE - heads - 2), BF16),
            ],
            axis=1,
        )
        feed_packed = jnp.concatenate(
            [w_down, w_out] + [w_up[:, c * width : (c + 1) * width] for c in range(chunks)], axis=0
        )
    seq_group = [("seq", bit) for bit in bits_of(sizes["seq"])]
    memory_pieces = [memory[None]]
    for step in seq_group:
        memory_pieces = gather_stage(memory_pieces, [step], sizes)
    w_pieces = gather_stage([packed[None]], groups[0], sizes)

    ids = neighbours // own
    ids = place_of(ids, lax.axis_index("seq"), seq_group) * own + neighbours % own
    ids = jnp.pad(ids.T, ((0, 8 - knn), (0, 0)))
    big = (width, rows)
    lanes = (8, rows)
    feed_pieces = gather_stage([feed_packed[None]], feed_groups[0], sizes)
    w_pieces = gather_stage(w_pieces, groups[1], sizes, join=len(groups) > 2)
    feed_pieces = after(w_pieces[0], feed_pieces)
    feed_pieces = gather_stage(feed_pieces, feed_groups[1], sizes)
    x_in, g_in, ids = after((w_pieces[0], feed_pieces[0]), (tokens, out_grad, ids))
    prepared = call(
        functools.partial(prepare_kernel, count=knn),
        [
            (big, BF16, pltpu.HBM),
            (big, BF16, pltpu.HBM),
            (lanes, F32),
            ((slots, rows), BF16, pltpu.HBM),
        ],
        [WHOLE] * 3,
        micros=4,
    )(x_in, g_in, ids)
    xt, gt, inv_one, times = prepared
    feed_pieces = after(w_pieces, feed_pieces)
    w_pieces = after(prepared, w_pieces)
    for at, group in enumerate(groups[2:], 2):
        w_pieces = gather_stage(w_pieces, group, sizes, join=at + 1 < len(groups))
    for group in feed_groups[2:-1]:
        feed_pieces = gather_stage(feed_pieces, group, sizes)

    def in_order(pieces):
        both = jnp.concatenate(pieces, axis=0)
        return jnp.zeros_like(both).at[owner].set(both)

    def split_rows(array, *heights):
        at, parts = 0, []
        for height in heights:
            parts.append(array[:, at : at + height].reshape(-1, width))
            at += height
        return parts

    if not direct:
        w_pieces = [in_order(w_pieces).reshape(blocks, ROWS, columns)]

    def to_send(pieces, *heights):
        if direct:
            return pieces
        array = pieces[0]
        if len(heights) > 1:
            parts = split_rows(array, low, *[ROWS] * (len(heights) - 1))
            parts = [part.reshape(-1, height, width) for part, height in zip(parts, heights)]
            array = jnp.concatenate(parts, axis=1)
        else:
            array = array.reshape(-1, heights[0], array.shape[2])
        array = array[owner]
        count = 1 << len(groups[-1])
        return jnp.split(array, count, axis=0)

    def head_block(part, cols, first=0):
        return pl.BlockSpec((size, cols), lambda h: (part * heads + first + h, 0))

    exp_rows = slots + rows // seg_count
    nt, qkv, mem_kv, side, mixed, ctx, rec, exps, gate, lse, lsen, far_scale, near_scale, flags = call(
        functools.partial(
            attend_kernel,
            pieces=len(w_pieces),
            mem_pieces=len(memory_pieces),
            heads=heads,
            seg_count=seg_count,
            scale=scale,
        ),
        [
            (big, BF16, pltpu.HBM),
            ((3 * width, rows), BF16, pltpu.VMEM),
            ((2 * width, slots), BF16, pltpu.VMEM),
            ((width, SIDE), BF16),
            (big, BF16, pltpu.VMEM),
            (big, F32, pltpu.VMEM),
            (big, F32, pltpu.VMEM),
            ((heads * exp_rows, rows), BF16, pltpu.HBM),
            (lanes, F32),
            (lanes, F32),
            (lanes, F32),
            (lanes, F32),
            (lanes, F32),
            ((heads,), jnp.int32),
        ],
        [SCALARS, SCALARS, FAR, WHOLE, FAR] + [WHOLE] * (len(w_pieces) + len(memory_pieces)),
        out_specs=[WHOLE] * 4
        + [head_block(0, rows)] * 3
        + [pl.BlockSpec((exp_rows, rows), lambda h: (h, 0))]
        + [WHOLE] * 5
        + [SCALARS],
        grid=(heads,),
        scratch=[
            pltpu.VMEM((width, columns), BF16),
            pltpu.VMEM(big, BF16),
            pltpu.VMEM((slots, rows), BF16),
            pltpu.SemaphoreType.DMA((2,)),
        ],
        micros=22,
        vmem=28,
    )(kernel_owner, lengths, far(xt), inv_one, far(times), *w_pieces, *memory_pieces)

    feed_pieces[1:] = after(mixed, feed_pieces[1:])
    feed_pieces = gather_stage(feed_pieces, groups[-1], sizes, join=False)
    if not direct:
        parts = split_rows(in_order(feed_pieces), tall, *[shard] * (1 + chunks))
        feed_pieces = [jnp.concatenate([part.reshape(blocks, -1, width) for part in parts], axis=1)]
    pieces = len(feed_pieces)
    sends = 1 << len(groups[-1]) if direct else 1
    feed_block = (blocks // sends,) + feed_pieces[0].shape[1:]
    outs = call(
        functools.partial(feed_kernel, heads=heads, pieces=pieces, sends=sends),
        [
            ((rows, width), BF16),
            (big, F32),
            (big, BF16),
            (lanes, F32),
            (lanes, F32),
            (lanes, F32),
            ((width, SIDE), F32),
        ]
        + [(feed_block, BF16)] * sends,
        [SCALARS] + [WHOLE] * (7 + pieces),
        scratch=[
            pltpu.VMEM(shape, BF16) for shape in ((width, width), (width, ff), (ff, width))
        ],
        micros=20,
        vmem=22,
    )(kernel_owner, xt, gt, mixed, ctx, rec, gate, side, *feed_pieces)
    block_out, grad_hidden, dm, dc, dn, dlogit, ggain_two = outs[:7]
    late = to_send(outs[7:], tall, *[shard] * (1 + chunks))
    late_at = len(feed_groups)

    backs = []
    first = 0
    for count in (1, heads - 1):
        late_at -= 1
        moving = sum_terms(late, feed_groups[late_at], sizes)
        outs = call(
            functools.partial(attend_back_kernel, first=first, seg_count=seg_count, scale=scale),
            [((size * count, rows), BF16)] * 3 + [((size * count, slots), BF16)] * 2,
            [
                SCALARS,
                SCALARS,
                head_block(0, rows, first),
                head_block(1, rows, first),
                head_block(2, rows, first),
                head_block(0, slots, first),
                head_block(1, slots, first),
                head_block(0, rows, first),
                pl.BlockSpec((exp_rows, rows), lambda h, first=first: (first + h, 0)),
            ]
            + [WHOLE] * 8,
            out_specs=[head_block(0, rows)] * 3 + [head_block(0, slots)] * 2,
            grid=(count,),
            scratch=[pltpu.VMEM((size, rows), F32)] * 2 + [pltpu.VMEM((size, slots), F32)] * 2,
            micros=4 * count,
            vmem=24,
        )(
            flags,
            lengths,
            qkv,
            qkv,
            qkv,
            mem_kv,
            mem_kv,
            dm,
            far(exps),
            gate,
            times,
            lse,
            lsen,
            far_scale,
            near_scale,
            dc,
            dn,
        )
        first += count
        late = add_terms(moving, feed_groups[late_at - 1])
        outs, dm = after(late, (outs, dm))
        backs.append(outs)
    late_at -= 1
    moving = sum_terms(late, feed_groups[late_at], sizes)

    pieces = len(w_pieces)
    *early, back = call(
        functools.partial(
            weight_kernel,
            calls=len(backs),
            pieces=pieces,
            mem_pieces=len(memory_pieces),
            sends=sends,
            heads=heads,
        ),
        [((blocks // sends, ROWS, columns), BF16)] * sends + [((columns, rows), BF16)],
        [SCALARS] + [WHOLE] * (4 + len(memory_pieces) + 5 * len(backs) + pieces),
        scratch=[pltpu.VMEM((width, columns), F32)],
        micros=6,
    )(
        kernel_owner,
        nt,
        side,
        dlogit,
        ggain_two,
        *memory_pieces,
        *[b for back in backs for b in back],
        *w_pieces,
    )
    early = to_send(early, shard)
    early = sum_terms(early, groups[-1], sizes)
    for at in reversed(range(len(groups) - 1)):
        early = add_terms(early, groups[at])
        if at + 2 == len(groups):
            back = after(early, back)
        early = sum_terms(early, groups[at], sizes)
    (grad_tokens,) = call(
        functools.partial(input_kernel, heads=heads),
        [((rows, width), F32)],
        [SCALARS] + [WHOLE] * (5 + pieces),
        scratch=[pltpu.VMEM((width, columns), BF16)],
        micros=6,
    )(kernel_owner, xt, inv_one, side, back, grad_hidden, *w_pieces)

    moving = after(grad_tokens, moving)
    while late_at:
        late_at -= 1
        moving = sum_terms(add_terms(moving, feed_groups[late_at]), feed_groups[late_at], sizes)
    late = moving

    if direct:
        grad_down, grad_out, grad_up = call(
            finish_feed_kernel,
            [((tall, width), F32), ((shard, width), F32), ((shard, ff), F32)],
            [WHOLE] * len(late),
            micros=1,
        )(*late)
        grad_query, grad_key, grad_value, grad_gate, grad_one, grad_two = call(
            finish_kernel,
            [((shard, width), F32)] * 3 + [((heads, shard), F32)] + [((1, shard), F32)] * 2,
            [WHOLE] * len(early),
            micros=1,
        )(*early)
        grad_gate, grad_one, grad_two = grad_gate.T, grad_one[0], grad_two[0]
    else:
        late = sum(term[0].astype(F32) for term in late)
        early = sum(term[0].astype(F32) for term in early)
        grad_down, grad_out = late[:tall], late[tall : tall + shard]
        grad_up = jnp.concatenate(
            [late[tall + shard * (1 + c) : tall + shard * (2 + c)] for c in range(chunks)], axis=1
        )
        grad_query, grad_key, grad_value = (
            early[:, at : at + width] for at in range(0, 3 * width, width)
        )
        side = early[:, 3 * width :]
        grad_gate, grad_one, grad_two = side[:, :heads], side[:, heads], side[:, heads + 1]
    return (
        block_out,
        grad_tokens,
        grad_one,
        grad_two,
        grad_query,
        grad_key,
        grad_value,
        grad_gate,
        grad_out,
        grad_up,
        grad_down,
    )


def solution(mesh):
    row_split, vector = P(("dp", "seq"), None), P(("dp", "seq"))
    in_specs = (row_split, row_split, vector, row_split, row_split, vector, vector) + (row_split,) * 7
    out_specs = (row_split, row_split, vector, vector) + (row_split,) * 7
    return jax.shard_map(
        functools.partial(on_device, sizes=dict(mesh.shape)),
        mesh=mesh,
        in_specs=in_specs,
        out_specs=out_specs,
        check_vma=False,
    )
```

```python
import functools
import math

import jax
import jax.numpy as jnp
from jax import lax
from jax.experimental import pallas as pl
from jax.experimental.pallas import tpu as pltpu
from jax.sharding import PartitionSpec as P


EPSILON = 1e-06
MASKED = -1e30
LOG2E = math.log2(math.e)
F32 = jnp.float32
BF16 = jnp.bfloat16
SIDE = 128
TILE = 256
ROWS = 16
TINY = 2.0**-80
HELD = 2
PER_MICRO = 1.1e9


def dot(left, right, left_dim=1, right_dim=0):
    return lax.dot_general(
        left, right, (((left_dim,), (right_dim,)), ((), ())), preferred_element_type=F32
    )


def call(kernel, outs, in_specs, out_specs=None, grid=None, scratch=(), micros=0, vmem=16):
    options = {} if grid is None else dict(grid=grid)
    if out_specs is None:
        out_specs = [WHOLE] * len(outs)
    return pl.pallas_call(
        kernel,
        out_shape=[
            where[0](shape, kind) if where else jax.ShapeDtypeStruct(shape, kind)
            for shape, kind, *where in outs
        ],
        in_specs=in_specs,
        out_specs=out_specs,
        scratch_shapes=list(scratch),
        compiler_params=pltpu.CompilerParams(vmem_limit_bytes=vmem << 20),
        cost_estimate=pl.CostEstimate(
            flops=int(micros * PER_MICRO), bytes_accessed=0, transcendentals=0
        ),
        **options,
    )


WHOLE = pl.BlockSpec(memory_space=pltpu.VMEM)
SCALARS = pl.BlockSpec(memory_space=pltpu.SMEM)
FAR = pl.BlockSpec(memory_space=pltpu.HBM)


def far(array):
    return pltpu.with_memory_space_constraint(array, pltpu.HBM)


def three_parts(value):
    high = value.astype(BF16).astype(F32)
    rest = value - high
    middle = rest.astype(BF16).astype(F32)
    return high, middle, rest - middle


def pick_rows(rows, count):
    shape = (count, rows[0].shape[1])
    index = lax.broadcasted_iota(jnp.int32, shape, 0)
    block = jnp.zeros(shape, F32)
    for at, row in enumerate(rows):
        block = jnp.where(index == at, row, block)
    return block


def bits_of(size):
    return [1 << b for b in reversed(range(size.bit_length() - 1))]


def groups_of(sizes):
    steps = [("dp", bit) for bit in bits_of(sizes["dp"])] + [("seq", bit) for bit in bits_of(sizes["seq"])]
    return [steps[at : at + 2] for at in range(0, len(steps), 2)]


def swap(array, group, mask, sizes):
    n_seq = sizes["seq"]
    apart = 0
    for at, (axis, bit) in enumerate(group):
        if mask >> at & 1:
            apart ^= bit * (n_seq if axis == "dp" else 1)
    pairs = [(i, i ^ apart) for i in range(sizes["dp"] * n_seq)]
    return lax.ppermute(array, ("dp", "seq"), pairs)


def gather_stage(pieces, group, sizes, join=True):
    if join and len(pieces) > 1:
        pieces = [jnp.concatenate(pieces, axis=0)]
    masks = range(1, 1 << len(group))
    return pieces + [swap(piece, group, mask, sizes) for mask in masks for piece in pieces]


def sum_terms(pieces, group, sizes):
    return [pieces[0]] + [swap(pieces[mask], group, mask, sizes) for mask in range(1, 1 << len(group))]


def add_terms(terms, group):
    count = 1 << len(group)
    step = terms[0].shape[0] // count
    return [
        sum(term[m * step : (m + 1) * step].astype(F32) for term in terms).astype(BF16)
        for m in range(count)
    ]


def after(earlier, later):
    return lax.optimization_barrier((earlier, later))[1]


def owners(groups, sizes):
    n_seq = sizes["seq"]
    at = jnp.arange(sizes["dp"] * n_seq, dtype=jnp.int32)
    own = {"dp": lax.axis_index("dp"), "seq": lax.axis_index("seq")}
    for number, (axis, bit) in enumerate(step for group in groups for step in group):
        own[axis] = own[axis] ^ jnp.where((at >> number) & 1, bit, 0)
    return own["dp"] * n_seq + own["seq"]


def place_of(ids, own_index, group_steps):
    apart = ids ^ own_index
    place = jnp.zeros_like(ids)
    for at, (_, bit) in enumerate(group_steps):
        place = place + jnp.where((apart & bit) != 0, 1 << at, 0)
    return place


def blocks_of(pieces):
    number = 0
    for piece in pieces:
        for index in range(piece.shape[0]):
            yield number, piece, index
            number += 1


def rows_at(owner_ref, number, height):
    return pl.ds(pl.multiple_of(owner_ref[number] * height, height), height)


def pack_kernel(
    q_ref, k_ref, v_ref, gate_ref, one_ref, two_ref, down_ref, wo_ref, up_ref, out_ref, feed_ref
):
    height, width = q_ref.shape
    low = down_ref.shape[0]
    feed_ref[:low, :] = down_ref[...]
    feed_ref[low : low + height, :] = wo_ref[...]
    for chunk in range(up_ref.shape[1] // width):
        at = low + (chunk + 1) * height
        feed_ref[at : at + height, :] = up_ref[:, chunk * width : (chunk + 1) * width]
    heads = gate_ref.shape[0]
    for part, ref in enumerate((q_ref, k_ref, v_ref)):
        out_ref[:, part * width : (part + 1) * width] = ref[...]
    row = lax.broadcasted_iota(jnp.int32, (height, height), 0)
    column = lax.broadcasted_iota(jnp.int32, (height, height), 1)
    lane = lax.broadcasted_iota(jnp.int32, (height, SIDE), 1)
    spread = lax.broadcasted_iota(jnp.int32, (heads, SIDE), 0) == lax.broadcasted_iota(
        jnp.int32, (heads, SIDE), 1
    )
    side = dot(gate_ref[...].astype(F32), jnp.where(spread, 1.0, 0.0), 0, 0)
    for at, ref in enumerate((one_ref, two_ref)):
        gains = jnp.where(row == column, ref[...].astype(F32), 0.0)
        side = jnp.where(lane == heads + at, jnp.sum(gains, axis=1, keepdims=True), side)
    out_ref[:, 3 * width :] = side.astype(BF16)


def prepare_kernel(
    x_ref, g_ref, ids_ref,
    xt_ref, gt_ref, inv_ref, times_ref,
    *, count,
):
    xt = x_ref[...].astype(F32).T
    xt_ref[...] = xt.astype(BF16)
    gt_ref[...] = g_ref[...].astype(F32).T.astype(BF16)
    inv = lax.rsqrt(jnp.mean(xt * xt, axis=0, keepdims=True) + EPSILON)
    inv_ref[...] = jnp.broadcast_to(inv, inv_ref.shape)
    slots, rows = times_ref.shape
    step = 128

    def body(i, _):
        at = pl.multiple_of(i * step, step)
        slot = lax.broadcasted_iota(jnp.int32, (step, rows), 0) + at
        times = jnp.zeros((step, rows), F32)
        for j in range(count):
            times = times + jnp.where(ids_ref[j : j + 1, :] == slot, 1.0, 0.0)
        times_ref[pl.ds(at, step), :] = times.astype(BF16)
        return 0

    lax.fori_loop(0, slots // step, body, 0)


def local_penalty(lengths_ref, rows, seg_count):
    seg_len = rows // seg_count
    lane = lax.broadcasted_iota(jnp.int32, (1, rows), 1)
    last = jnp.zeros((1, rows), jnp.int32)
    for seg in range(seg_count):
        last = jnp.where(lane // seg_len == seg, seg * seg_len + lengths_ref[seg], last)
    return jnp.where(lane < last, 0.0, MASKED)


def causal_bias(size):
    key = lax.broadcasted_iota(jnp.int32, (size, size), 0)
    query = lax.broadcasted_iota(jnp.int32, (size, size), 1)
    return jnp.where(key <= query, 0.0, MASKED)


def longest(keys):
    keys = keys.astype(F32)
    return jnp.max(jnp.sum(keys * keys, axis=0, keepdims=True), axis=1, keepdims=True)


def attend_kernel(
    owner_ref, lengths_ref, xt_far, inv_ref, times_far, *refs,
    pieces, mem_pieces, heads, seg_count, scale,
):
    w_pieces, memory, refs = refs[:pieces], refs[pieces : pieces + mem_pieces], refs[mem_pieces:]
    (
        nt_ref, qkv_ref, mem_ref, side_ref, mixed_ref, ctx_ref, rec_ref, exp_far, exp_held, gate_ref, lse_ref, lsen_ref,
        far_ref, near_ref, flags_ref, w_ref, xt_ref, times_ref, sems, exp_sems,
    ) = refs[pieces:]
    head = pl.program_id(0)
    width, rows = xt_ref.shape
    slots = times_ref.shape[0]
    size = width // heads
    seg_len = rows // seg_count

    @pl.when(head == 0)
    def _():
        x_copy = pltpu.make_async_copy(xt_far, xt_ref, sems.at[0])
        times_copy = pltpu.make_async_copy(times_far, times_ref, sems.at[1])
        x_copy.start()
        times_copy.start()
        for number, piece, index in blocks_of(w_pieces):
            w_ref[rows_at(owner_ref, number, piece.shape[1]), :] = piece[index]
        x_copy.wait()
        side_ref[...] = w_ref[:, 3 * width :]
        gain = side_ref[...].astype(F32)[:, heads : heads + 1]
        normed = (xt_ref[...].astype(F32) * inv_ref[0:1, :] * gain).astype(BF16)
        nt_ref[...] = normed
        for part in range(3):
            columns = slice(part * width, (part + 1) * width)
            qkv_ref[columns, :] = dot(w_ref[:, columns], normed, 0, 0).astype(BF16)
        gate_ref[...] = jax.nn.sigmoid(dot(side_ref[...], normed, 0, 0)[0:heads])
        for part in range(2):
            columns = slice((part + 1) * width, (part + 2) * width)
            for number, piece, index in blocks_of(memory):
                own = piece.shape[1]
                there = slice(number * own, (number + 1) * own)
                mem_ref[part * width : (part + 1) * width, there] = dot(
                    w_ref[:, columns], piece[index], 0, 1
                ).astype(BF16)
        times_copy.wait()

    held, exp_rows = exp_held.shape[:2]
    slot = lax.rem(head, held)
    exp_ref = exp_held.at[slot]

    def exp_copy(which):
        return pltpu.make_async_copy(
            exp_held.at[lax.rem(which, held)],
            exp_far.at[pl.ds(pl.multiple_of(which * exp_rows, exp_rows), exp_rows), :],
            exp_sems.at[lax.rem(which, held)],
        )

    @pl.when(head >= held)
    def _():
        exp_copy(head - held).wait()

    def head_of(ref, part):
        return ref[pl.ds(pl.multiple_of(part * width + head * size, size), size), :]

    q, k, v = (head_of(qkv_ref, part) for part in range(3))
    mk, mv = (head_of(mem_ref, part) for part in range(2))
    gate = gate_ref[pl.ds(head, 1), :]
    penalty = local_penalty(lengths_ref, rows, seg_count)
    causal = causal_bias(seg_len)
    q = q.astype(F32) * (scale * LOG2E)
    q_high = q.astype(BF16)
    q_low = (q - q_high.astype(F32)).astype(BF16)
    reach = jnp.sqrt(
        jnp.sum(q * q, axis=0, keepdims=True) * jnp.maximum(longest(k), longest(mk))
    ) * (1.0 + 2.0**-10)
    ones = jnp.ones((1, rows), F32)
    mem_three = pick_rows([jnp.ones((1, slots), F32)] * 3, 16).astype(BF16)
    queries = jnp.concatenate(
        [q_high, q_low, pick_rows([*three_parts(-reach), ones], 16).astype(BF16)], axis=0
    )
    keys = jnp.concatenate([k, k, pick_rows([ones, ones, ones, penalty], 16).astype(BF16)], axis=0)
    mem_keys = jnp.concatenate([mk, mk, mem_three], axis=0)
    values = jnp.concatenate([v, jnp.ones((16, rows), BF16)], axis=0)
    mem_values = jnp.concatenate([mv, jnp.ones((16, slots), BF16)], axis=0)

    def finish(here, total, near_total, peak, near_peak):
        mass, near_mass = total[size : size + 1], near_total[size : size + 1]
        context = total[:size] / mass
        recalled = near_total[:size] / near_mass
        ctx_ref[:, here] = context.astype(BF16)
        rec_ref[:, here] = recalled.astype(BF16)
        lse_ref[pl.ds(head, 1), here] = peak + jnp.log2(mass)
        lsen_ref[pl.ds(head, 1), here] = near_peak + jnp.log2(near_mass)
        share = gate[:, here]
        far_ref[pl.ds(head, 1), here] = (1.0 - share) / mass
        near_ref[pl.ds(head, 1), here] = share / near_mass
        mixed_ref[:, here] = ((1.0 - share) * context + share * recalled).astype(BF16)
        return jnp.minimum(mass, near_mass)

    segments = [slice(at, at + seg_len) for at in range(0, rows, seg_len)]
    least = jnp.full((1, seg_len), 1.0, F32)
    for here in segments:
        all_keys = jnp.concatenate([mem_keys, keys[:, here]], axis=1)
        all_values = jnp.concatenate([mem_values, values[:, here]], axis=1)
        score = dot(all_keys, queries[:, here], 0, 0)
        exp_mem = jnp.exp2(score[:slots]).astype(BF16)
        exp_own = jnp.exp2(score[slots:] + causal).astype(BF16)
        exp_ref[:slots, here] = exp_mem
        exp_ref[slots:, here] = exp_own
        total = dot(all_values, jnp.concatenate([exp_mem, exp_own], axis=0))
        near_total = dot(mem_values, exp_mem * times_ref[:, here])
        least = jnp.minimum(
            least, finish(here, total, near_total, reach[:, here], reach[:, here])
        )

    @pl.when(head + held < heads)
    def _():
        exp_copy(head).start()

    far_off = jnp.logical_not(jnp.min(least) > TINY)
    flags_ref[head] = far_off.astype(jnp.int32)

    @pl.when(far_off)
    def _():
        zero = jnp.zeros((1, rows), F32)
        plain = jnp.concatenate(
            [q_high, q_low, pick_rows([zero, zero, zero, ones], 16).astype(BF16)], axis=0
        )
        for here in segments:
            score = dot(mem_keys, plain[:, here], 0, 0)
            score_own = dot(keys[:, here], plain[:, here], 0, 0) + causal
            near = jnp.where(times_ref[:, here] > 0, score, MASKED)
            near_peak = jnp.max(near, axis=0, keepdims=True)
            peak = jnp.maximum(
                jnp.max(score, axis=0, keepdims=True), jnp.max(score_own, axis=0, keepdims=True)
            )
            total = dot(mem_values, jnp.exp2(score - peak).astype(BF16))
            total = total + dot(values[:, here], jnp.exp2(score_own - peak).astype(BF16))
            exp_near = jnp.exp2(near - near_peak).astype(BF16) * times_ref[:, here]
            finish(here, total, dot(mem_values, exp_near), peak, near_peak)


def feed_kernel(
    owner_ref, xt_ref, gt_ref, mixed_ref, ctx_ref, rec_ref, gate_ref, side_ref, *refs, heads, pieces, sends
):
    w_pieces, refs = refs[:pieces], refs[pieces:]
    (block_ref, gh_ref, dm_ref, dc_ref, dn_ref, dlogit_ref, ggain_ref), refs = refs[:7], refs[7:]
    g_pieces, (wo_ref, up_ref, down_ref) = refs[:sends], refs[sends:]
    width, rows = xt_ref.shape
    chunks = up_ref.shape[1] // width
    size = width // heads
    low = down_ref.shape[0] // width * ROWS
    for number, piece, index in blocks_of(w_pieces):
        block = piece[index]
        down_ref[rows_at(owner_ref, number, low), :] = block[:low]
        here = rows_at(owner_ref, number, ROWS)
        wo_ref[here, :] = block[low : low + ROWS]
        for chunk in range(chunks):
            at = low + (chunk + 1) * ROWS
            up_ref[here, chunk * width : (chunk + 1) * width] = block[at : at + ROWS]

    gain = side_ref[...].astype(F32)[:, heads + 1 : heads + 2]
    hidden = xt_ref[...].astype(F32) + dot(wo_ref[...], mixed_ref[...], 0, 0)
    inv = lax.rsqrt(jnp.mean(hidden * hidden, axis=0, keepdims=True) + EPSILON)
    unit = hidden * inv
    n2 = (unit * gain).astype(BF16)
    grad = gt_ref[...]
    coef = math.sqrt(2.0 / math.pi)

    part_size = width // 2
    parts = [slice(at, at + part_size) for at in range(0, up_ref.shape[1], part_size)]

    def first(part):
        return dot(up_ref[:, part], n2, 0, 0), dot(down_ref[part, :], grad)

    def second(pre, grad_act):
        square = pre * pre
        half = 0.5 + 0.5 * jnp.tanh(pre * (coef + (0.044715 * coef) * square))
        act = pre * half
        slope = half + act * (1.0 - half) * (2.0 * coef + (6.0 * 0.044715 * coef) * square)
        return act.astype(BF16), (grad_act * slope).astype(BF16)

    ready = first(parts[0])
    out = gn2 = None
    for at, part in enumerate(parts):
        later = first(parts[at + 1]) if at + 1 < len(parts) else None
        act, grad_pre = second(*ready)
        ready = later
        out_part = dot(down_ref[part, :], act, 0, 0)
        gn2_part = dot(up_ref[:, part], grad_pre)
        out = out_part if out is None else out + out_part
        gn2 = gn2_part if gn2 is None else gn2 + gn2_part
        down_ref[part, :] = dot(act, grad, 1, 1).astype(BF16)
        up_ref[:, part] = dot(n2, grad_pre, 1, 1).astype(BF16)

    block_ref[...] = (hidden + out).T.astype(BF16)
    ggain_ref[...] = jnp.broadcast_to(jnp.sum(gn2 * unit, axis=1, keepdims=True), ggain_ref.shape)
    a = gn2 * gain
    grad_hidden = grad.astype(F32) + inv * (a - unit * jnp.mean(a * unit, axis=0, keepdims=True))
    gh_ref[...] = grad_hidden
    branch = grad_hidden.astype(BF16)
    grad_mixed = dot(wo_ref[...], branch)
    wo_ref[...] = dot(mixed_ref[...], branch, 1, 1).astype(BF16)
    for number, piece, index in blocks_of(g_pieces):
        piece[index, :low] = down_ref[rows_at(owner_ref, number, low), :]
        here = rows_at(owner_ref, number, ROWS)
        piece[index, low : low + ROWS] = wo_ref[here, :]
        for chunk in range(chunks):
            at = low + (chunk + 1) * ROWS
            piece[index, at : at + ROWS] = up_ref[here, chunk * width : (chunk + 1) * width]
    rounded = grad_mixed.astype(BF16)
    dm_ref[...] = rounded
    rounded = rounded.astype(F32)
    for head in range(heads):
        part = slice(head * size, (head + 1) * size)
        ctx, rec = ctx_ref[part, :].astype(F32), rec_ref[part, :].astype(F32)
        dc_ref[head : head + 1, :] = jnp.sum(rounded[part] * ctx, axis=0, keepdims=True)
        dn_ref[head : head + 1, :] = jnp.sum(rounded[part] * rec, axis=0, keepdims=True)
        share = gate_ref[head : head + 1, :]
        moved = jnp.sum(grad_mixed[part] * (rec - ctx), axis=0, keepdims=True)
        dlogit_ref[head : head + 1, :] = moved * share * (1.0 - share)


def attend_back_kernel(
    flags_ref, lengths_ref, q_ref, k_ref, v_ref, mk_ref, mv_ref, dm_ref, exp_ref, gate_ref, times_ref,
    lse_ref, lsen_ref, far_ref, near_ref, dc_ref, dn_ref,
    dq_ref, dk_ref, dv_ref, dmk_ref, dmv_ref,
    dk_sum, dv_sum, dmk_sum, dmv_sum, left_ref, rows_ref,
    *, first, seg_count, scale,
):
    size, rows = q_ref.shape
    seg_len = rows // seg_count
    if len(exp_ref.shape) == 3:
        exp_ref = exp_ref.at[lax.rem(pl.program_id(0) + first, exp_ref.shape[0])]
    row = pl.ds(pl.program_id(0) + first, 1)
    dc = dc_ref[row, :]
    apart = dc - dn_ref[row, :]
    slots = mk_ref.shape[1]
    ones = jnp.ones((1, rows), F32)
    mem_three = pick_rows([jnp.ones((1, slots), F32)] * 3, 16).astype(BF16)
    grads = jnp.concatenate([dm_ref[...], pick_rows(three_parts(-dc), 16).astype(BF16)], axis=0)
    values = jnp.concatenate([v_ref[...], pick_rows([ones] * 3, 16).astype(BF16)], axis=0)
    mem_values = jnp.concatenate([mv_ref[...], mem_three], axis=0)

    far_off = flags_ref[pl.program_id(0) + first] != 0

    @pl.when(jnp.logical_not(far_off))
    def _():
        far_scale, near_scale = far_ref[row, :], near_ref[row, :]
        near_apart = near_scale * apart
        for at in range(0, rows, TILE):
            here = slice(at, at + TILE)
            start = at // seg_len * seg_len
            there = slice(start, at + TILE)
            n = at + TILE - start
            q_here, dm_here = q_ref[:, here].T, dm_ref[:, here].T
            moved = dot(jnp.concatenate([mem_values, values[:, there]], axis=1), grads[:, here], 0, 0)
            exps = exp_ref[:slots, here].astype(F32)
            times = times_ref[:, here].astype(F32)
            mix = far_scale[:, here] + near_scale[:, here] * times
            weight = exps * mix
            dscore = (exps * (mix * moved[:slots] + near_apart[:, here] * times)).astype(BF16)
            wl = exp_ref[slots : slots + n, here].astype(F32) * far_scale[:, here]
            dl = (wl * moved[slots:]).astype(BF16)
            weight = jnp.concatenate([weight.astype(BF16), wl.astype(BF16)], axis=0)
            dscore = jnp.concatenate([dscore, dl], axis=0)
            grad_v = dot(weight, dm_here).T
            grad_k = dot(dscore, q_here).T
            dq = dot(jnp.concatenate([mk_ref[...], k_ref[:, there]], axis=1), dscore)
            if at == 0:
                dmv_sum[...] = grad_v[:, :slots]
                dmk_sum[...] = grad_k[:, :slots]
            else:
                dmv_sum[...] += grad_v[:, :slots]
                dmk_sum[...] += grad_k[:, :slots]
            if n == TILE:
                dv_sum[:, there] = grad_v[:, slots:]
                dk_sum[:, there] = grad_k[:, slots:]
            else:
                dv_sum[:, start:at] += grad_v[:, slots:slots + n - TILE]
                dk_sum[:, start:at] += grad_k[:, slots:slots + n - TILE]
                dv_sum[:, here] = grad_v[:, slots + n - TILE:]
                dk_sum[:, here] = grad_k[:, slots + n - TILE:]
            dq_ref[:, here] = (scale * dq).astype(BF16)

    @pl.when(far_off)
    def _():
        q = q_ref[...].astype(F32) * (scale * LOG2E)
        q_high = q.astype(BF16)
        q_low = (q - q_high.astype(F32)).astype(BF16)
        share = gate_ref[row, :]
        shift = jnp.log2(jnp.maximum(1.0 - share, 2.0**-60)) - lse_ref[row, :]
        near_shift = jnp.log2(jnp.maximum(share, 2.0**-60)) - lsen_ref[row, :] - shift
        penalty = local_penalty(lengths_ref, rows, seg_count)
        extra = [*three_parts(shift), ones]
        left_ref[0] = jnp.concatenate([q_high, q_low, pick_rows(extra, 16).astype(BF16)], axis=0)
        extra = [ones, ones, ones, penalty]
        left_ref[1] = jnp.concatenate(
            [k_ref[...], k_ref[...], pick_rows(extra, 16).astype(BF16)], axis=0
        )
        pad = jnp.zeros((size, rows), BF16)
        left_ref[2] = jnp.concatenate([grads, pad], axis=0)
        left_ref[3] = jnp.concatenate([values, pad], axis=0)
        rows_ref[...] = pick_rows([near_shift, apart], 8)
        mem_keys = jnp.concatenate([mk_ref[...], mk_ref[...], mem_three], axis=0)
        for ref in (dv_sum, dk_sum, dmv_sum, dmk_sum):
            ref[...] = jnp.zeros_like(ref)
        deep = size + 16

        def tile(number, _):
            at = pl.multiple_of(number * TILE, TILE)
            start = pl.multiple_of(at // seg_len * seg_len, seg_len)
            here, seg = pl.ds(at, TILE), pl.ds(start, seg_len)
            queries, grads_here = left_ref[0, :, here], left_ref[2, :deep, here]
            q_here, dm_here = q_ref[:, here].T, dm_ref[:, here].T
            score = dot(mem_keys, queries, 0, 0)
            moved = dot(mem_values, grads_here, 0, 0)
            times = times_ref[:, here].astype(F32)
            bias = jnp.where(times > 0.0, jnp.log2(times), MASKED)
            near = jnp.exp2(score + (bias + rows_ref[0:1, here]))
            weight = jnp.exp2(score) + near
            dscore = (weight * moved + near * rows_ref[1:2, here]).astype(BF16)
            dmv_sum[...] += dot(weight.astype(BF16), dm_here).T
            dmk_sum[...] += dot(dscore, q_here).T
            dq = dot(mk_ref[...], dscore)
            key = lax.broadcasted_iota(jnp.int32, (seg_len, TILE), 0)
            query = lax.broadcasted_iota(jnp.int32, (seg_len, TILE), 1) + (at - start)
            score = dot(left_ref[1, :, seg], queries, 0, 0)
            weight = jnp.exp2(jnp.where(key <= query, score, MASKED))
            dscore = (weight * dot(left_ref[3, :deep, seg], grads_here, 0, 0)).astype(BF16)
            dv_sum[:, seg] += dot(weight.astype(BF16), dm_here).T
            dk_sum[:, seg] += dot(dscore, q_here).T
            dq_ref[:, here] = (scale * (dq + dot(k_ref[:, seg], dscore))).astype(BF16)
            return 0

        lax.fori_loop(0, rows // TILE, tile, 0)

    dk_ref[...] = (scale * dk_sum[...]).astype(BF16)
    dv_ref[...] = dv_sum[...].astype(BF16)
    dmk_ref[...] = (scale * dmk_sum[...]).astype(BF16)
    dmv_ref[...] = dmv_sum[...].astype(BF16)


def weight_kernel(
    owner_ref, nt_ref, side_ref, dlogit_ref, ggain_ref, *refs, calls, pieces, mem_pieces, sends, heads
):
    memory, refs = refs[:mem_pieces], refs[mem_pieces:]
    backs = [refs[5 * at : 5 * at + 5] for at in range(calls)]
    refs = refs[5 * calls :]
    w_pieces, refs = refs[:pieces], refs[pieces:]
    g_pieces, (back_ref, gw_ref) = refs[:sends], refs[sends:]
    width, rows = nt_ref.shape
    for part in range(3):
        at = part * width
        for back in backs:
            back_ref[at : at + back[part].shape[0], :] = back[part][...]
            at += back[part].shape[0]
    side = jnp.concatenate([dlogit_ref[...], jnp.zeros((SIDE - heads, rows), F32)], axis=0)
    back_ref[3 * width :, :] = side.astype(BF16)
    normed = nt_ref[...]
    for part in range(3):
        columns = slice(part * width, (part + 1) * width)
        gw_ref[:, columns] = dot(normed, back_ref[columns, :], 1, 1)
    gw_ref[:, 3 * width :] = dot(normed, back_ref[3 * width :, :], 1, 1)
    by_rows = []
    for number, piece, index in blocks_of(w_pieces):
        here = rows_at(owner_ref, number, ROWS)
        by_rows.append((here, jnp.sum(piece[index].astype(F32) * gw_ref[here, :], axis=1, keepdims=True)))
    lane = lax.broadcasted_iota(jnp.int32, (ROWS, SIDE), 1)
    for here, total in by_rows:
        gain = side_ref[here, :].astype(F32)[:, heads : heads + 1]
        block = jnp.where(lane == heads, total / gain, gw_ref[here, 3 * width :])
        gw_ref[here, 3 * width :] = jnp.where(lane == heads + 1, ggain_ref[here, :], block)
    for part in range(1, 3):
        at = part * width
        for back in backs:
            source = back[part + 2]
            grad = sum(
                dot(piece[index], source[:, i * piece.shape[1] : (i + 1) * piece.shape[1]], 0, 1)
                for i, piece, index in blocks_of(memory)
            )
            gw_ref[:, at : at + source.shape[0]] += grad
            at += source.shape[0]
    for number, piece, index in blocks_of(g_pieces):
        piece[index] = gw_ref[rows_at(owner_ref, number, ROWS), :].astype(BF16)


def input_kernel(owner_ref, xt_ref, inv_ref, side_ref, back_ref, gh_ref, *refs, heads):
    w_pieces, (gx_ref, w_ref) = refs[:-2], refs[-2:]
    for number, piece, index in blocks_of(w_pieces):
        w_ref[rows_at(owner_ref, number, ROWS), :] = piece[index]
    unit = xt_ref[...].astype(F32) * inv_ref[0:1, :]
    gain = side_ref[...].astype(F32)[:, heads : heads + 1]
    b = dot(w_ref[...], back_ref[...]) * gain
    out = gh_ref[...] + inv_ref[0:1, :] * (b - unit * jnp.mean(b * unit, axis=0, keepdims=True))
    gx_ref[...] = out.T


def finish_feed_kernel(*refs):
    *terms, down_ref, wo_ref, up_ref = refs
    low, width = down_ref.shape
    total = sum(term[0].astype(F32) for term in terms)
    down_ref[...] = total[:low]
    height = wo_ref.shape[0]
    wo_ref[...] = total[low : low + height]
    for chunk in range(up_ref.shape[1] // width):
        at = low + (chunk + 1) * height
        up_ref[:, chunk * width : (chunk + 1) * width] = total[at : at + height]


def finish_kernel(*refs):
    *terms, q_ref, k_ref, v_ref, gate_ref, one_ref, two_ref = refs
    height, width = q_ref.shape
    total = sum(term[0].astype(F32) for term in terms)
    for part, ref in enumerate((q_ref, k_ref, v_ref)):
        ref[...] = total[:, part * width : (part + 1) * width]
    heads = gate_ref.shape[0]
    side = total[:, 3 * width :].T
    gate_ref[...] = side[:heads]
    one_ref[...] = side[heads : heads + 1]
    two_ref[...] = side[heads + 1 : heads + 2]


def on_device(
    tokens,
    memory,
    lengths,
    neighbours,
    out_grad,
    gain_one,
    gain_two,
    w_query,
    w_key,
    w_value,
    w_gate,
    w_out,
    w_up,
    w_down,
    *,
    sizes,
):
    rows, width = tokens.shape
    heads = w_gate.shape[1]
    size = width // heads
    seg_count = lengths.shape[0]
    knn = neighbours.shape[1]
    shard = w_query.shape[0]
    ff = w_up.shape[1]
    chunks = ff // width
    tall = w_down.shape[0]
    scale = size ** (-0.5)
    own = memory.shape[0]
    slots = own * sizes["seq"]
    blocks = width // ROWS
    low = ff // blocks

    groups = groups_of(sizes)
    feed_groups = [[step] for step in groups[0]] + groups[1:]
    owner = owners(groups, sizes)
    direct = shard == ROWS
    kernel_owner = owner if direct else jnp.arange(blocks, dtype=jnp.int32)

    columns = 3 * width + SIDE
    feed_height = tall + shard * (1 + chunks)
    if direct:
        packed, feed_packed = call(
            pack_kernel,
            [((shard, columns), BF16), ((feed_height, width), BF16)],
            [WHOLE] * 9,
            micros=1,
            vmem=60,
        )(
            w_query,
            w_key,
            w_value,
            w_gate.T,
            gain_one[None],
            gain_two[None],
            w_down,
            w_out,
            w_up,
        )
    else:
        packed = jnp.concatenate(
            [
                w_query,
                w_key,
                w_value,
                w_gate,
                gain_one[:, None],
                gain_two[:, None],
                jnp.zeros((shard, SIDE - heads - 2), BF16),
            ],
            axis=1,
        )
        feed_packed = jnp.concatenate(
            [w_down, w_out] + [w_up[:, c * width : (c + 1) * width] for c in range(chunks)], axis=0
        )
    seq_group = [("seq", bit) for bit in bits_of(sizes["seq"])]
    memory_pieces = [memory[None]]
    for step in seq_group:
        memory_pieces = gather_stage(memory_pieces, [step], sizes)
    w_pieces = gather_stage([packed[None]], groups[0], sizes)

    ids = neighbours // own
    ids = place_of(ids, lax.axis_index("seq"), seq_group) * own + neighbours % own
    ids = jnp.pad(ids.T, ((0, 8 - knn), (0, 0)))
    big = (width, rows)
    lanes = (8, rows)
    feed_pieces = gather_stage([feed_packed[None]], feed_groups[0], sizes)
    w_pieces = gather_stage(w_pieces, groups[1], sizes, join=len(groups) > 2)
    feed_pieces = after(w_pieces[0], feed_pieces)
    feed_pieces = gather_stage(feed_pieces, feed_groups[1], sizes)
    x_in, g_in, ids = after((w_pieces[0], feed_pieces[0]), (tokens, out_grad, ids))
    prepared = call(
        functools.partial(prepare_kernel, count=knn),
        [
            (big, BF16, pltpu.HBM),
            (big, BF16, pltpu.HBM),
            (lanes, F32),
            ((slots, rows), BF16, pltpu.HBM),
        ],
        [WHOLE] * 3,
        micros=4,
    )(x_in, g_in, ids)
    xt, gt, inv_one, times = prepared
    feed_pieces = after(w_pieces, feed_pieces)
    w_pieces = after(prepared, w_pieces)
    for at, group in enumerate(groups[2:], 2):
        w_pieces = gather_stage(w_pieces, group, sizes, join=at + 1 < len(groups))
    for group in feed_groups[2:-1]:
        feed_pieces = gather_stage(feed_pieces, group, sizes)

    def in_order(pieces):
        both = jnp.concatenate(pieces, axis=0)
        return jnp.zeros_like(both).at[owner].set(both)

    def split_rows(array, *heights):
        at, parts = 0, []
        for height in heights:
            parts.append(array[:, at : at + height].reshape(-1, width))
            at += height
        return parts

    if not direct:
        w_pieces = [in_order(w_pieces).reshape(blocks, ROWS, columns)]

    def to_send(pieces, *heights):
        if direct:
            return pieces
        array = pieces[0]
        if len(heights) > 1:
            parts = split_rows(array, low, *[ROWS] * (len(heights) - 1))
            parts = [part.reshape(-1, height, width) for part, height in zip(parts, heights)]
            array = jnp.concatenate(parts, axis=1)
        else:
            array = array.reshape(-1, heights[0], array.shape[2])
        array = array[owner]
        count = 1 << len(groups[-1])
        return jnp.split(array, count, axis=0)

    def head_block(part, cols, first=0):
        return pl.BlockSpec((size, cols), lambda h: (part * heads + first + h, 0))

    exp_rows = slots + rows // seg_count
    nt, qkv, mem_kv, side, mixed, ctx, rec, exps, exps_held, gate, lse, lsen, far_scale, near_scale, flags = call(
        functools.partial(
            attend_kernel,
            pieces=len(w_pieces),
            mem_pieces=len(memory_pieces),
            heads=heads,
            seg_count=seg_count,
            scale=scale,
        ),
        [
            (big, BF16, pltpu.HBM),
            ((3 * width, rows), BF16, pltpu.VMEM),
            ((2 * width, slots), BF16, pltpu.VMEM),
            ((width, SIDE), BF16),
            (big, BF16, pltpu.VMEM),
            (big, BF16, pltpu.VMEM),
            (big, BF16, pltpu.VMEM),
            (((heads - HELD) * exp_rows, rows), BF16, pltpu.HBM),
            ((HELD, exp_rows, rows), BF16, pltpu.VMEM),
            (lanes, F32),
            (lanes, F32),
            (lanes, F32),
            (lanes, F32),
            (lanes, F32),
            ((heads,), jnp.int32),
        ],
        [SCALARS, SCALARS, FAR, WHOLE, FAR] + [WHOLE] * (len(w_pieces) + len(memory_pieces)),
        out_specs=[WHOLE] * 4
        + [head_block(0, rows)] * 3
        + [FAR]
        + [WHOLE] * 6
        + [SCALARS],
        grid=(heads,),
        scratch=[
            pltpu.VMEM((width, columns), BF16),
            pltpu.VMEM(big, BF16),
            pltpu.VMEM((slots, rows), BF16),
            pltpu.SemaphoreType.DMA((2,)),
            pltpu.SemaphoreType.DMA((HELD,)),
        ],
        micros=22,
        vmem=28,
    )(kernel_owner, lengths, far(xt), inv_one, far(times), *w_pieces, *memory_pieces)

    feed_pieces[1:] = after(mixed, feed_pieces[1:])
    feed_pieces = gather_stage(feed_pieces, groups[-1], sizes, join=False)
    if not direct:
        parts = split_rows(in_order(feed_pieces), tall, *[shard] * (1 + chunks))
        feed_pieces = [jnp.concatenate([part.reshape(blocks, -1, width) for part in parts], axis=1)]
    pieces = len(feed_pieces)
    sends = 1 << len(groups[-1]) if direct else 1
    feed_block = (blocks // sends,) + feed_pieces[0].shape[1:]
    outs = call(
        functools.partial(feed_kernel, heads=heads, pieces=pieces, sends=sends),
        [
            ((rows, width), BF16),
            (big, F32),
            (big, BF16),
            (lanes, F32),
            (lanes, F32),
            (lanes, F32),
            ((width, SIDE), F32),
        ]
        + [(feed_block, BF16)] * sends,
        [SCALARS] + [WHOLE] * (7 + pieces),
        scratch=[
            pltpu.VMEM(shape, BF16) for shape in ((width, width), (width, ff), (ff, width))
        ],
        micros=20,
        vmem=21,
    )(kernel_owner, xt, gt, mixed, ctx, rec, gate, side, *feed_pieces)
    block_out, grad_hidden, dm, dc, dn, dlogit, ggain_two = outs[:7]
    late = to_send(outs[7:], tall, *[shard] * (1 + chunks))
    late_at = len(feed_groups)

    backs = []
    for first, count in ((heads - HELD, HELD), (0, heads - HELD)):
        held = first > 0
        late_at -= 1
        moving = sum_terms(late, feed_groups[late_at], sizes)
        outs = call(
            functools.partial(attend_back_kernel, first=first, seg_count=seg_count, scale=scale),
            [((size * count, rows), BF16)] * 3 + [((size * count, slots), BF16)] * 2,
            [
                SCALARS,
                SCALARS,
                head_block(0, rows, first),
                head_block(1, rows, first),
                head_block(2, rows, first),
                head_block(0, slots, first),
                head_block(1, slots, first),
                head_block(0, rows, first),
                WHOLE if held else pl.BlockSpec((exp_rows, rows), lambda h: (h, 0)),
            ]
            + [WHOLE] * 8,
            out_specs=[head_block(0, rows)] * 3 + [head_block(0, slots)] * 2,
            grid=(count,),
            scratch=[pltpu.VMEM((size, rows), F32)] * 2
            + [pltpu.VMEM((size, slots), F32)] * 2
            + [pltpu.VMEM((4, 2 * size + 16, rows), BF16), pltpu.VMEM(lanes, F32)],
            micros=4 * count,
            vmem=24,
        )(
            flags,
            lengths,
            qkv,
            qkv,
            qkv,
            mem_kv,
            mem_kv,
            dm,
            exps_held if held else far(exps),
            gate,
            times,
            lse,
            lsen,
            far_scale,
            near_scale,
            dc,
            dn,
        )
        late = add_terms(moving, feed_groups[late_at - 1])
        dm = after(late, dm)
        backs.insert(0, outs)
    late_at -= 1
    moving = sum_terms(late, feed_groups[late_at], sizes)

    pieces = len(w_pieces)
    *early, back = call(
        functools.partial(
            weight_kernel,
            calls=len(backs),
            pieces=pieces,
            mem_pieces=len(memory_pieces),
            sends=sends,
            heads=heads,
        ),
        [((blocks // sends, ROWS, columns), BF16)] * sends + [((columns, rows), BF16)],
        [SCALARS] + [WHOLE] * (4 + len(memory_pieces) + 5 * len(backs) + pieces),
        scratch=[pltpu.VMEM((width, columns), F32)],
        micros=6,
    )(
        kernel_owner,
        nt,
        side,
        dlogit,
        ggain_two,
        *memory_pieces,
        *[b for back in backs for b in back],
        *w_pieces,
    )
    early = to_send(early, shard)
    early = sum_terms(early, groups[-1], sizes)
    for at in reversed(range(len(groups) - 1)):
        early = add_terms(early, groups[at])
        if at + 2 == len(groups):
            back = after(early, back)
        early = sum_terms(early, groups[at], sizes)
    (grad_tokens,) = call(
        functools.partial(input_kernel, heads=heads),
        [((rows, width), F32)],
        [SCALARS] + [WHOLE] * (5 + pieces),
        scratch=[pltpu.VMEM((width, columns), BF16)],
        micros=6,
    )(kernel_owner, xt, inv_one, side, back, grad_hidden, *w_pieces)

    moving = after(grad_tokens, moving)
    while late_at:
        late_at -= 1
        moving = sum_terms(add_terms(moving, feed_groups[late_at]), feed_groups[late_at], sizes)
    late = moving

    if direct:
        grad_down, grad_out, grad_up = call(
            finish_feed_kernel,
            [((tall, width), F32), ((shard, width), F32), ((shard, ff), F32)],
            [WHOLE] * len(late),
            micros=1,
        )(*late)
        grad_query, grad_key, grad_value, grad_gate, grad_one, grad_two = call(
            finish_kernel,
            [((shard, width), F32)] * 3 + [((heads, shard), F32)] + [((1, shard), F32)] * 2,
            [WHOLE] * len(early),
            micros=1,
        )(*early)
        grad_gate, grad_one, grad_two = grad_gate.T, grad_one[0], grad_two[0]
    else:
        late = sum(term[0].astype(F32) for term in late)
        early = sum(term[0].astype(F32) for term in early)
        grad_down, grad_out = late[:tall], late[tall : tall + shard]
        grad_up = jnp.concatenate(
            [late[tall + shard * (1 + c) : tall + shard * (2 + c)] for c in range(chunks)], axis=1
        )
        grad_query, grad_key, grad_value = (
            early[:, at : at + width] for at in range(0, 3 * width, width)
        )
        side = early[:, 3 * width :]
        grad_gate, grad_one, grad_two = side[:, :heads], side[:, heads], side[:, heads + 1]
    return (
        block_out,
        grad_tokens,
        grad_one,
        grad_two,
        grad_query,
        grad_key,
        grad_value,
        grad_gate,
        grad_out,
        grad_up,
        grad_down,
    )


def solution(mesh):
    row_split, vector = P(("dp", "seq"), None), P(("dp", "seq"))
    in_specs = (row_split, row_split, vector, row_split, row_split, vector, vector) + (row_split,) * 7
    out_specs = (row_split, row_split, vector, vector) + (row_split,) * 7
    return jax.shard_map(
        functools.partial(on_device, sizes=dict(mesh.shape)),
        mesh=mesh,
        in_specs=in_specs,
        out_specs=out_specs,
        check_vma=False,
    )
```

```python
import functools
import math

import jax
import jax.numpy as jnp
from jax import lax
from jax.experimental import pallas as pl
from jax.experimental.pallas import tpu as pltpu
from jax.sharding import PartitionSpec as P


EPSILON = 1e-06
MASKED = -1e30
LOG2E = math.log2(math.e)
F32 = jnp.float32
BF16 = jnp.bfloat16
SIDE = 128
TILE = 256
ROWS = 16
TINY = 2.0**-80
HELD = 2
PER_MICRO = 1.1e9


def dot(left, right, left_dim=1, right_dim=0):
    return lax.dot_general(
        left, right, (((left_dim,), (right_dim,)), ((), ())), preferred_element_type=F32
    )


def call(kernel, outs, in_specs, out_specs=None, grid=None, scratch=(), micros=0, vmem=16):
    options = {} if grid is None else dict(grid=grid)
    if out_specs is None:
        out_specs = [WHOLE] * len(outs)
    return pl.pallas_call(
        kernel,
        out_shape=[
            where[0](shape, kind) if where else jax.ShapeDtypeStruct(shape, kind)
            for shape, kind, *where in outs
        ],
        in_specs=in_specs,
        out_specs=out_specs,
        scratch_shapes=list(scratch),
        compiler_params=pltpu.CompilerParams(vmem_limit_bytes=vmem << 20),
        cost_estimate=pl.CostEstimate(
            flops=int(micros * PER_MICRO), bytes_accessed=0, transcendentals=0
        ),
        **options,
    )


WHOLE = pl.BlockSpec(memory_space=pltpu.VMEM)
SCALARS = pl.BlockSpec(memory_space=pltpu.SMEM)
FAR = pl.BlockSpec(memory_space=pltpu.HBM)


def far(array):
    return pltpu.with_memory_space_constraint(array, pltpu.HBM)


def three_parts(value):
    high = value.astype(BF16).astype(F32)
    rest = value - high
    middle = rest.astype(BF16).astype(F32)
    return high, middle, rest - middle


def pick_rows(rows, count):
    shape = (count, rows[0].shape[1])
    index = lax.broadcasted_iota(jnp.int32, shape, 0)
    block = jnp.zeros(shape, F32)
    for at, row in enumerate(rows):
        block = jnp.where(index == at, row, block)
    return block


def bits_of(size):
    return [1 << b for b in reversed(range(size.bit_length() - 1))]


def groups_of(sizes):
    steps = [("dp", bit) for bit in bits_of(sizes["dp"])] + [("seq", bit) for bit in bits_of(sizes["seq"])]
    return [steps[at : at + 2] for at in range(0, len(steps), 2)]


def swap(array, group, mask, sizes):
    n_seq = sizes["seq"]
    apart = 0
    for at, (axis, bit) in enumerate(group):
        if mask >> at & 1:
            apart ^= bit * (n_seq if axis == "dp" else 1)
    pairs = [(i, i ^ apart) for i in range(sizes["dp"] * n_seq)]
    return lax.ppermute(array, ("dp", "seq"), pairs)


def gather_stage(pieces, group, sizes, join=True):
    if join and len(pieces) > 1:
        pieces = [jnp.concatenate(pieces, axis=0)]
    masks = range(1, 1 << len(group))
    return pieces + [swap(piece, group, mask, sizes) for mask in masks for piece in pieces]


def sum_terms(pieces, group, sizes):
    return [pieces[0]] + [swap(pieces[mask], group, mask, sizes) for mask in range(1, 1 << len(group))]


def add_terms(terms, group):
    count = 1 << len(group)
    step = terms[0].shape[0] // count
    return [
        sum(term[m * step : (m + 1) * step].astype(F32) for term in terms).astype(BF16)
        for m in range(count)
    ]


def after(earlier, later):
    return lax.optimization_barrier((earlier, later))[1]


def owners(groups, sizes):
    n_seq = sizes["seq"]
    at = jnp.arange(sizes["dp"] * n_seq, dtype=jnp.int32)
    own = {"dp": lax.axis_index("dp"), "seq": lax.axis_index("seq")}
    for number, (axis, bit) in enumerate(step for group in groups for step in group):
        own[axis] = own[axis] ^ jnp.where((at >> number) & 1, bit, 0)
    return own["dp"] * n_seq + own["seq"]


def place_of(ids, own_index, group_steps):
    apart = ids ^ own_index
    place = jnp.zeros_like(ids)
    for at, (_, bit) in enumerate(group_steps):
        place = place + jnp.where((apart & bit) != 0, 1 << at, 0)
    return place


def blocks_of(pieces):
    number = 0
    for piece in pieces:
        for index in range(piece.shape[0]):
            yield number, piece, index
            number += 1


def rows_at(owner_ref, number, height):
    return pl.ds(pl.multiple_of(owner_ref[number] * height, height), height)


def pack_kernel(
    q_ref, k_ref, v_ref, gate_ref, one_ref, two_ref, down_ref, wo_ref, up_ref, out_ref, feed_ref
):
    height, width = q_ref.shape
    low = down_ref.shape[0]
    feed_ref[:low, :] = down_ref[...]
    feed_ref[low : low + height, :] = wo_ref[...]
    for chunk in range(up_ref.shape[1] // width):
        at = low + (chunk + 1) * height
        feed_ref[at : at + height, :] = up_ref[:, chunk * width : (chunk + 1) * width]
    heads = gate_ref.shape[0]
    for part, ref in enumerate((q_ref, k_ref, v_ref)):
        out_ref[:, part * width : (part + 1) * width] = ref[...]
    row = lax.broadcasted_iota(jnp.int32, (height, height), 0)
    column = lax.broadcasted_iota(jnp.int32, (height, height), 1)
    lane = lax.broadcasted_iota(jnp.int32, (height, SIDE), 1)
    spread = lax.broadcasted_iota(jnp.int32, (heads, SIDE), 0) == lax.broadcasted_iota(
        jnp.int32, (heads, SIDE), 1
    )
    side = dot(gate_ref[...].astype(F32), jnp.where(spread, 1.0, 0.0), 0, 0)
    for at, ref in enumerate((one_ref, two_ref)):
        gains = jnp.where(row == column, ref[...].astype(F32), 0.0)
        side = jnp.where(lane == heads + at, jnp.sum(gains, axis=1, keepdims=True), side)
    out_ref[:, 3 * width :] = side.astype(BF16)


def prepare_kernel(
    x_ref, g_ref, ids_ref,
    xt_ref, gt_ref, inv_ref, times_ref,
    *, count,
):
    xt = x_ref[...].astype(F32).T
    xt_ref[...] = xt.astype(BF16)
    gt_ref[...] = g_ref[...].astype(F32).T.astype(BF16)
    inv = lax.rsqrt(jnp.mean(xt * xt, axis=0, keepdims=True) + EPSILON)
    inv_ref[...] = jnp.broadcast_to(inv, inv_ref.shape)
    slots, rows = times_ref.shape
    step = 128

    def body(i, _):
        at = pl.multiple_of(i * step, step)
        slot = lax.broadcasted_iota(jnp.int32, (step, rows), 0) + at
        times = jnp.zeros((step, rows), F32)
        for j in range(count):
            times = times + jnp.where(ids_ref[j : j + 1, :] == slot, 1.0, 0.0)
        times_ref[pl.ds(at, step), :] = times.astype(BF16)
        return 0

    lax.fori_loop(0, slots // step, body, 0)


def local_penalty(lengths_ref, rows, seg_count):
    seg_len = rows // seg_count
    lane = lax.broadcasted_iota(jnp.int32, (1, rows), 1)
    last = jnp.zeros((1, rows), jnp.int32)
    for seg in range(seg_count):
        last = jnp.where(lane // seg_len == seg, seg * seg_len + lengths_ref[seg], last)
    return jnp.where(lane < last, 0.0, MASKED)


def causal_bias(size):
    key = lax.broadcasted_iota(jnp.int32, (size, size), 0)
    query = lax.broadcasted_iota(jnp.int32, (size, size), 1)
    return jnp.where(key <= query, 0.0, MASKED)


def longest(keys):
    keys = keys.astype(F32)
    return jnp.max(jnp.sum(keys * keys, axis=0, keepdims=True), axis=1, keepdims=True)


def attend_kernel(
    owner_ref, lengths_ref, xt_far, inv_ref, times_far, *refs,
    pieces, mem_pieces, heads, seg_count, scale,
):
    w_pieces, memory, refs = refs[:pieces], refs[pieces : pieces + mem_pieces], refs[mem_pieces:]
    (
        nt_ref, qkv_ref, mem_ref, side_ref, mixed_ref, ctx_ref, rec_ref, exp_far, exp_held, gate_ref, lse_ref, lsen_ref,
        far_ref, near_ref, flags_ref, w_ref, xt_ref, times_ref, sems, exp_sems,
    ) = refs[pieces:]
    head = pl.program_id(0)
    width, rows = xt_ref.shape
    slots = times_ref.shape[0]
    size = width // heads
    seg_len = rows // seg_count

    @pl.when(head == 0)
    def _():
        x_copy = pltpu.make_async_copy(xt_far, xt_ref, sems.at[0])
        times_copy = pltpu.make_async_copy(times_far, times_ref, sems.at[1])
        x_copy.start()
        times_copy.start()
        for number, piece, index in blocks_of(w_pieces):
            w_ref[rows_at(owner_ref, number, piece.shape[1]), :] = piece[index]
        x_copy.wait()
        side_ref[...] = w_ref[:, 3 * width :]
        gain = side_ref[...].astype(F32)[:, heads : heads + 1]
        normed = (xt_ref[...].astype(F32) * inv_ref[0:1, :] * gain).astype(BF16)
        nt_ref[...] = normed
        for part in range(3):
            columns = slice(part * width, (part + 1) * width)
            qkv_ref[columns, :] = dot(w_ref[:, columns], normed, 0, 0).astype(BF16)
        gate_ref[...] = jax.nn.sigmoid(dot(side_ref[...], normed, 0, 0)[0:heads])
        for part in range(2):
            columns = slice((part + 1) * width, (part + 2) * width)
            for number, piece, index in blocks_of(memory):
                own = piece.shape[1]
                there = slice(number * own, (number + 1) * own)
                mem_ref[part * width : (part + 1) * width, there] = dot(
                    w_ref[:, columns], piece[index], 0, 1
                ).astype(BF16)
        times_copy.wait()

    held, exp_rows = exp_held.shape[:2]
    slot = lax.rem(head, held)
    exp_ref = exp_held.at[slot]

    def exp_copy(which):
        return pltpu.make_async_copy(
            exp_held.at[lax.rem(which, held)],
            exp_far.at[pl.ds(pl.multiple_of(which * exp_rows, exp_rows), exp_rows), :],
            exp_sems.at[lax.rem(which, held)],
        )

    @pl.when(head >= held)
    def _():
        exp_copy(head - held).wait()

    def head_of(ref, part):
        return ref[pl.ds(pl.multiple_of(part * width + head * size, size), size), :]

    q, k, v = (head_of(qkv_ref, part) for part in range(3))
    mk, mv = (head_of(mem_ref, part) for part in range(2))
    gate = gate_ref[pl.ds(head, 1), :]
    penalty = local_penalty(lengths_ref, rows, seg_count)
    causal = causal_bias(seg_len)
    q = q.astype(F32) * (scale * LOG2E)
    q_high = q.astype(BF16)
    q_low = (q - q_high.astype(F32)).astype(BF16)
    reach = jnp.sqrt(
        jnp.sum(q * q, axis=0, keepdims=True) * jnp.maximum(longest(k), longest(mk))
    ) * (1.0 + 2.0**-10)
    ones = jnp.ones((1, rows), F32)
    mem_three = pick_rows([jnp.ones((1, slots), F32)] * 3, 16).astype(BF16)
    queries = jnp.concatenate(
        [q_high, q_low, pick_rows([*three_parts(-reach), ones], 16).astype(BF16)], axis=0
    )
    keys = jnp.concatenate([k, k, pick_rows([ones, ones, ones, penalty], 16).astype(BF16)], axis=0)
    mem_keys = jnp.concatenate([mk, mk, mem_three], axis=0)
    values = jnp.concatenate([v, jnp.ones((16, rows), BF16)], axis=0)
    mem_values = jnp.concatenate([mv, jnp.ones((16, slots), BF16)], axis=0)

    def finish(here, total, near_total, peak, near_peak):
        mass, near_mass = total[size : size + 1], near_total[size : size + 1]
        context = total[:size] / mass
        recalled = near_total[:size] / near_mass
        ctx_ref[:, here] = context.astype(BF16)
        rec_ref[:, here] = recalled.astype(BF16)
        lse_ref[pl.ds(head, 1), here] = peak + jnp.log2(mass)
        lsen_ref[pl.ds(head, 1), here] = near_peak + jnp.log2(near_mass)
        share = gate[:, here]
        far_ref[pl.ds(head, 1), here] = (1.0 - share) / mass
        near_ref[pl.ds(head, 1), here] = share / near_mass
        mixed_ref[:, here] = ((1.0 - share) * context + share * recalled).astype(BF16)
        return jnp.minimum(mass, near_mass)

    segments = [slice(at, at + seg_len) for at in range(0, rows, seg_len)]
    least = jnp.full((1, seg_len), 1.0, F32)
    for here in segments:
        all_keys = jnp.concatenate([mem_keys, keys[:, here]], axis=1)
        all_values = jnp.concatenate([mem_values, values[:, here]], axis=1)
        score = dot(all_keys, queries[:, here], 0, 0)
        exp_mem = jnp.exp2(score[:slots]).astype(BF16)
        exp_own = jnp.exp2(score[slots:] + causal).astype(BF16)
        exp_ref[:slots, here] = exp_mem
        exp_ref[slots:, here] = exp_own
        total = dot(all_values, jnp.concatenate([exp_mem, exp_own], axis=0))
        near_total = dot(mem_values, exp_mem * times_ref[:, here])
        least = jnp.minimum(
            least, finish(here, total, near_total, reach[:, here], reach[:, here])
        )

    @pl.when(head + held < heads)
    def _():
        exp_copy(head).start()

    far_off = jnp.logical_not(jnp.min(least) > TINY)
    flags_ref[head] = far_off.astype(jnp.int32)

    @pl.when(far_off)
    def _():
        zero = jnp.zeros((1, rows), F32)
        plain = jnp.concatenate(
            [q_high, q_low, pick_rows([zero, zero, zero, ones], 16).astype(BF16)], axis=0
        )
        for here in segments:
            score = dot(mem_keys, plain[:, here], 0, 0)
            score_own = dot(keys[:, here], plain[:, here], 0, 0) + causal
            near = jnp.where(times_ref[:, here] > 0, score, MASKED)
            near_peak = jnp.max(near, axis=0, keepdims=True)
            peak = jnp.maximum(
                jnp.max(score, axis=0, keepdims=True), jnp.max(score_own, axis=0, keepdims=True)
            )
            total = dot(mem_values, jnp.exp2(score - peak).astype(BF16))
            total = total + dot(values[:, here], jnp.exp2(score_own - peak).astype(BF16))
            exp_near = jnp.exp2(near - near_peak).astype(BF16) * times_ref[:, here]
            finish(here, total, dot(mem_values, exp_near), peak, near_peak)


def feed_kernel(
    owner_ref, xt_ref, gt_ref, mixed_ref, ctx_ref, rec_ref, gate_ref, side_ref, *refs, heads, pieces, sends
):
    w_pieces, refs = refs[:pieces], refs[pieces:]
    (block_ref, gh_ref, dm_ref, dc_ref, dn_ref, dlogit_ref, ggain_ref), refs = refs[:7], refs[7:]
    g_pieces, (wo_ref, up_ref, down_ref) = refs[:sends], refs[sends:]
    width, rows = xt_ref.shape
    chunks = up_ref.shape[1] // width
    size = width // heads
    low = down_ref.shape[0] // width * ROWS
    for number, piece, index in blocks_of(w_pieces):
        block = piece[index]
        down_ref[rows_at(owner_ref, number, low), :] = block[:low]
        here = rows_at(owner_ref, number, ROWS)
        wo_ref[here, :] = block[low : low + ROWS]
        for chunk in range(chunks):
            at = low + (chunk + 1) * ROWS
            up_ref[here, chunk * width : (chunk + 1) * width] = block[at : at + ROWS]

    gain = side_ref[...].astype(F32)[:, heads + 1 : heads + 2]
    hidden = xt_ref[...].astype(F32) + dot(wo_ref[...], mixed_ref[...], 0, 0)
    inv = lax.rsqrt(jnp.mean(hidden * hidden, axis=0, keepdims=True) + EPSILON)
    unit = hidden * inv
    n2 = (unit * gain).astype(BF16)
    grad = gt_ref[...]
    coef = math.sqrt(2.0 / math.pi)

    part_size = width // 2
    parts = [slice(at, at + part_size) for at in range(0, up_ref.shape[1], part_size)]

    def first(part):
        return dot(up_ref[:, part], n2, 0, 0), dot(down_ref[part, :], grad)

    def second(pre, grad_act):
        square = pre * pre
        half = 0.5 + 0.5 * jnp.tanh(pre * (coef + (0.044715 * coef) * square))
        act = pre * half
        slope = half + act * (1.0 - half) * (2.0 * coef + (6.0 * 0.044715 * coef) * square)
        return act.astype(BF16), (grad_act * slope).astype(BF16)

    ready = first(parts[0])
    out = gn2 = None
    for at, part in enumerate(parts):
        later = first(parts[at + 1]) if at + 1 < len(parts) else None
        act, grad_pre = second(*ready)
        ready = later
        out_part = dot(down_ref[part, :], act, 0, 0)
        gn2_part = dot(up_ref[:, part], grad_pre)
        out = out_part if out is None else out + out_part
        gn2 = gn2_part if gn2 is None else gn2 + gn2_part
        down_ref[part, :] = dot(act, grad, 1, 1).astype(BF16)
        up_ref[:, part] = dot(n2, grad_pre, 1, 1).astype(BF16)

    block_ref[...] = (hidden + out).T.astype(BF16)
    ggain_ref[...] = jnp.broadcast_to(jnp.sum(gn2 * unit, axis=1, keepdims=True), ggain_ref.shape)
    a = gn2 * gain
    grad_hidden = grad.astype(F32) + inv * (a - unit * jnp.mean(a * unit, axis=0, keepdims=True))
    gh_ref[...] = grad_hidden
    branch = grad_hidden.astype(BF16)
    grad_mixed = dot(wo_ref[...], branch)
    wo_ref[...] = dot(mixed_ref[...], branch, 1, 1).astype(BF16)
    for number, piece, index in blocks_of(g_pieces):
        piece[index, :low] = down_ref[rows_at(owner_ref, number, low), :]
        here = rows_at(owner_ref, number, ROWS)
        piece[index, low : low + ROWS] = wo_ref[here, :]
        for chunk in range(chunks):
            at = low + (chunk + 1) * ROWS
            piece[index, at : at + ROWS] = up_ref[here, chunk * width : (chunk + 1) * width]
    rounded = grad_mixed.astype(BF16)
    dm_ref[...] = rounded
    rounded = rounded.astype(F32)
    for head in range(heads):
        part = slice(head * size, (head + 1) * size)
        ctx, rec = ctx_ref[part, :].astype(F32), rec_ref[part, :].astype(F32)
        dc_ref[head : head + 1, :] = jnp.sum(rounded[part] * ctx, axis=0, keepdims=True)
        dn_ref[head : head + 1, :] = jnp.sum(rounded[part] * rec, axis=0, keepdims=True)
        share = gate_ref[head : head + 1, :]
        moved = jnp.sum(grad_mixed[part] * (rec - ctx), axis=0, keepdims=True)
        dlogit_ref[head : head + 1, :] = moved * share * (1.0 - share)


def attend_back_kernel(
    flags_ref, lengths_ref, q_ref, k_ref, v_ref, mk_ref, mv_ref, dm_ref, exp_ref, gate_ref, times_ref,
    lse_ref, lsen_ref, far_ref, near_ref, dc_ref, dn_ref,
    dq_ref, dk_ref, dv_ref, dmk_ref, dmv_ref,
    dk_sum, dv_sum, dmk_sum, dmv_sum, left_ref, rows_ref,
    *, first, seg_count, scale,
):
    size, rows = q_ref.shape
    seg_len = rows // seg_count
    if len(exp_ref.shape) == 3:
        exp_ref = exp_ref.at[lax.rem(pl.program_id(0) + first, exp_ref.shape[0])]
    row = pl.ds(pl.program_id(0) + first, 1)
    dc = dc_ref[row, :]
    apart = dc - dn_ref[row, :]
    slots = mk_ref.shape[1]
    ones = jnp.ones((1, rows), F32)
    mem_three = pick_rows([jnp.ones((1, slots), F32)] * 3, 16).astype(BF16)
    grads = jnp.concatenate([dm_ref[...], pick_rows(three_parts(-dc), 16).astype(BF16)], axis=0)
    values = jnp.concatenate([v_ref[...], pick_rows([ones] * 3, 16).astype(BF16)], axis=0)
    mem_values = jnp.concatenate([mv_ref[...], mem_three], axis=0)

    far_off = flags_ref[pl.program_id(0) + first] != 0

    @pl.when(jnp.logical_not(far_off))
    def _():
        far_scale, near_scale = far_ref[row, :], near_ref[row, :]
        near_apart = near_scale * apart
        for at in range(0, rows, TILE):
            here = slice(at, at + TILE)
            start = at // seg_len * seg_len
            there = slice(start, at + TILE)
            n = at + TILE - start
            q_here, dm_here = q_ref[:, here].T, dm_ref[:, here].T
            moved = dot(jnp.concatenate([mem_values, values[:, there]], axis=1), grads[:, here], 0, 0)
            exps = exp_ref[:slots, here].astype(F32)
            times = times_ref[:, here].astype(F32)
            mix = far_scale[:, here] + near_scale[:, here] * times
            weight = exps * mix
            dscore = (exps * (mix * moved[:slots] + near_apart[:, here] * times)).astype(BF16)
            wl = exp_ref[slots : slots + n, here].astype(F32) * far_scale[:, here]
            dl = (wl * moved[slots:]).astype(BF16)
            weight = jnp.concatenate([weight.astype(BF16), wl.astype(BF16)], axis=0)
            dscore = jnp.concatenate([dscore, dl], axis=0)
            grad_v = dot(weight, dm_here).T
            grad_k = dot(dscore, q_here).T
            dq = dot(jnp.concatenate([mk_ref[...], k_ref[:, there]], axis=1), dscore)
            if at == 0:
                dmv_sum[...] = grad_v[:, :slots]
                dmk_sum[...] = grad_k[:, :slots]
            else:
                dmv_sum[...] += grad_v[:, :slots]
                dmk_sum[...] += grad_k[:, :slots]
            if n == TILE:
                dv_sum[:, there] = grad_v[:, slots:]
                dk_sum[:, there] = grad_k[:, slots:]
            else:
                dv_sum[:, start:at] += grad_v[:, slots:slots + n - TILE]
                dk_sum[:, start:at] += grad_k[:, slots:slots + n - TILE]
                dv_sum[:, here] = grad_v[:, slots + n - TILE:]
                dk_sum[:, here] = grad_k[:, slots + n - TILE:]
            dq_ref[:, here] = (scale * dq).astype(BF16)

    @pl.when(far_off)
    def _():
        q = q_ref[...].astype(F32) * (scale * LOG2E)
        q_high = q.astype(BF16)
        q_low = (q - q_high.astype(F32)).astype(BF16)
        share = gate_ref[row, :]
        shift = jnp.log2(jnp.maximum(1.0 - share, 2.0**-60)) - lse_ref[row, :]
        near_shift = jnp.log2(jnp.maximum(share, 2.0**-60)) - lsen_ref[row, :] - shift
        penalty = local_penalty(lengths_ref, rows, seg_count)
        extra = [*three_parts(shift), ones]
        left_ref[0] = jnp.concatenate([q_high, q_low, pick_rows(extra, 16).astype(BF16)], axis=0)
        extra = [ones, ones, ones, penalty]
        left_ref[1] = jnp.concatenate(
            [k_ref[...], k_ref[...], pick_rows(extra, 16).astype(BF16)], axis=0
        )
        pad = jnp.zeros((size, rows), BF16)
        left_ref[2] = jnp.concatenate([grads, pad], axis=0)
        left_ref[3] = jnp.concatenate([values, pad], axis=0)
        rows_ref[...] = pick_rows([near_shift, apart], 8)
        mem_keys = jnp.concatenate([mk_ref[...], mk_ref[...], mem_three], axis=0)
        for ref in (dv_sum, dk_sum, dmv_sum, dmk_sum):
            ref[...] = jnp.zeros_like(ref)
        deep = size + 16

        def tile(number, _):
            at = pl.multiple_of(number * TILE, TILE)
            start = pl.multiple_of(at // seg_len * seg_len, seg_len)
            here, seg = pl.ds(at, TILE), pl.ds(start, seg_len)
            queries, grads_here = left_ref[0, :, here], left_ref[2, :deep, here]
            q_here, dm_here = q_ref[:, here].T, dm_ref[:, here].T
            score = dot(mem_keys, queries, 0, 0)
            moved = dot(mem_values, grads_here, 0, 0)
            times = times_ref[:, here].astype(F32)
            bias = jnp.where(times > 0.0, jnp.log2(times), MASKED)
            near = jnp.exp2(score + (bias + rows_ref[0:1, here]))
            weight = jnp.exp2(score) + near
            dscore = (weight * moved + near * rows_ref[1:2, here]).astype(BF16)
            dmv_sum[...] += dot(weight.astype(BF16), dm_here).T
            dmk_sum[...] += dot(dscore, q_here).T
            dq = dot(mk_ref[...], dscore)
            key = lax.broadcasted_iota(jnp.int32, (seg_len, TILE), 0)
            query = lax.broadcasted_iota(jnp.int32, (seg_len, TILE), 1) + (at - start)
            score = dot(left_ref[1, :, seg], queries, 0, 0)
            weight = jnp.exp2(jnp.where(key <= query, score, MASKED))
            dscore = (weight * dot(left_ref[3, :deep, seg], grads_here, 0, 0)).astype(BF16)
            dv_sum[:, seg] += dot(weight.astype(BF16), dm_here).T
            dk_sum[:, seg] += dot(dscore, q_here).T
            dq_ref[:, here] = (scale * (dq + dot(k_ref[:, seg], dscore))).astype(BF16)
            return 0

        lax.fori_loop(0, rows // TILE, tile, 0)

    dk_ref[...] = (scale * dk_sum[...]).astype(BF16)
    dv_ref[...] = dv_sum[...].astype(BF16)
    dmk_ref[...] = (scale * dmk_sum[...]).astype(BF16)
    dmv_ref[...] = dmv_sum[...].astype(BF16)


def weight_kernel(
    owner_ref, nt_ref, side_ref, dlogit_ref, ggain_ref, *refs, calls, pieces, mem_pieces, sends, heads
):
    memory, refs = refs[:mem_pieces], refs[mem_pieces:]
    backs = [refs[5 * at : 5 * at + 5] for at in range(calls)]
    refs = refs[5 * calls :]
    w_pieces, refs = refs[:pieces], refs[pieces:]
    g_pieces, (back_ref, gw_ref) = refs[:sends], refs[sends:]
    width, rows = nt_ref.shape
    for part in range(3):
        at = part * width
        for back in backs:
            back_ref[at : at + back[part].shape[0], :] = back[part][...]
            at += back[part].shape[0]
    side = jnp.concatenate([dlogit_ref[...], jnp.zeros((SIDE - heads, rows), F32)], axis=0)
    back_ref[3 * width :, :] = side.astype(BF16)
    normed = nt_ref[...]
    for part in range(3):
        columns = slice(part * width, (part + 1) * width)
        gw_ref[:, columns] = dot(normed, back_ref[columns, :], 1, 1)
    gw_ref[:, 3 * width :] = dot(normed, back_ref[3 * width :, :], 1, 1)
    by_rows = []
    for number, piece, index in blocks_of(w_pieces):
        here = rows_at(owner_ref, number, ROWS)
        by_rows.append((here, jnp.sum(piece[index].astype(F32) * gw_ref[here, :], axis=1, keepdims=True)))
    lane = lax.broadcasted_iota(jnp.int32, (ROWS, SIDE), 1)
    for here, total in by_rows:
        gain = side_ref[here, :].astype(F32)[:, heads : heads + 1]
        block = jnp.where(lane == heads, total / gain, gw_ref[here, 3 * width :])
        gw_ref[here, 3 * width :] = jnp.where(lane == heads + 1, ggain_ref[here, :], block)
    for part in range(1, 3):
        at = part * width
        for back in backs:
            source = back[part + 2]
            grad = sum(
                dot(piece[index], source[:, i * piece.shape[1] : (i + 1) * piece.shape[1]], 0, 1)
                for i, piece, index in blocks_of(memory)
            )
            gw_ref[:, at : at + source.shape[0]] += grad
            at += source.shape[0]
    for number, piece, index in blocks_of(g_pieces):
        piece[index] = gw_ref[rows_at(owner_ref, number, ROWS), :].astype(BF16)


def input_kernel(owner_ref, xt_ref, inv_ref, side_ref, back_ref, gh_ref, *refs, heads):
    w_pieces, (gx_ref, w_ref) = refs[:-2], refs[-2:]
    for number, piece, index in blocks_of(w_pieces):
        w_ref[rows_at(owner_ref, number, ROWS), :] = piece[index]
    unit = xt_ref[...].astype(F32) * inv_ref[0:1, :]
    gain = side_ref[...].astype(F32)[:, heads : heads + 1]
    b = dot(w_ref[...], back_ref[...]) * gain
    out = gh_ref[...] + inv_ref[0:1, :] * (b - unit * jnp.mean(b * unit, axis=0, keepdims=True))
    gx_ref[...] = out.T


def finish_feed_kernel(*refs):
    *terms, down_ref, wo_ref, up_ref = refs
    low, width = down_ref.shape
    total = sum(term[0].astype(F32) for term in terms)
    down_ref[...] = total[:low]
    height = wo_ref.shape[0]
    wo_ref[...] = total[low : low + height]
    for chunk in range(up_ref.shape[1] // width):
        at = low + (chunk + 1) * height
        up_ref[:, chunk * width : (chunk + 1) * width] = total[at : at + height]


def finish_kernel(*refs):
    *terms, q_ref, k_ref, v_ref, gate_ref, one_ref, two_ref = refs
    height, width = q_ref.shape
    total = sum(term[0].astype(F32) for term in terms)
    for part, ref in enumerate((q_ref, k_ref, v_ref)):
        ref[...] = total[:, part * width : (part + 1) * width]
    heads = gate_ref.shape[0]
    side = total[:, 3 * width :].T
    gate_ref[...] = side[:heads]
    one_ref[...] = side[heads : heads + 1]
    two_ref[...] = side[heads + 1 : heads + 2]


def on_device(
    tokens,
    memory,
    lengths,
    neighbours,
    out_grad,
    gain_one,
    gain_two,
    w_query,
    w_key,
    w_value,
    w_gate,
    w_out,
    w_up,
    w_down,
    *,
    sizes,
):
    rows, width = tokens.shape
    heads = w_gate.shape[1]
    size = width // heads
    seg_count = lengths.shape[0]
    knn = neighbours.shape[1]
    shard = w_query.shape[0]
    ff = w_up.shape[1]
    chunks = ff // width
    tall = w_down.shape[0]
    scale = size ** (-0.5)
    own = memory.shape[0]
    slots = own * sizes["seq"]
    blocks = width // ROWS
    low = ff // blocks

    groups = groups_of(sizes)
    feed_groups = [[step] for step in groups[0]] + groups[1:]
    owner = owners(groups, sizes)
    direct = shard == ROWS
    kernel_owner = owner if direct else jnp.arange(blocks, dtype=jnp.int32)

    columns = 3 * width + SIDE
    feed_height = tall + shard * (1 + chunks)
    if direct:
        packed, feed_packed = call(
            pack_kernel,
            [((shard, columns), BF16), ((feed_height, width), BF16)],
            [WHOLE] * 9,
            micros=1,
            vmem=60,
        )(
            w_query,
            w_key,
            w_value,
            w_gate.T,
            gain_one[None],
            gain_two[None],
            w_down,
            w_out,
            w_up,
        )
    else:
        packed = jnp.concatenate(
            [
                w_query,
                w_key,
                w_value,
                w_gate,
                gain_one[:, None],
                gain_two[:, None],
                jnp.zeros((shard, SIDE - heads - 2), BF16),
            ],
            axis=1,
        )
        feed_packed = jnp.concatenate(
            [w_down, w_out] + [w_up[:, c * width : (c + 1) * width] for c in range(chunks)], axis=0
        )
    seq_group = [("seq", bit) for bit in bits_of(sizes["seq"])]
    memory_pieces = [memory[None]]
    for step in seq_group:
        memory_pieces = gather_stage(memory_pieces, [step], sizes)
    w_pieces = gather_stage([packed[None]], groups[0], sizes)

    ids = neighbours // own
    ids = place_of(ids, lax.axis_index("seq"), seq_group) * own + neighbours % own
    ids = jnp.pad(ids.T, ((0, 8 - knn), (0, 0)))
    big = (width, rows)
    lanes = (8, rows)
    feed_pieces = gather_stage([feed_packed[None]], feed_groups[0], sizes)
    w_pieces = gather_stage(w_pieces, groups[1], sizes, join=len(groups) > 2)
    feed_pieces = after(w_pieces[0], feed_pieces)
    feed_pieces = gather_stage(feed_pieces, feed_groups[1], sizes)
    x_in, g_in, ids = after((w_pieces[0], feed_pieces[0]), (tokens, out_grad, ids))
    prepared = call(
        functools.partial(prepare_kernel, count=knn),
        [
            (big, BF16, pltpu.HBM),
            (big, BF16, pltpu.HBM),
            (lanes, F32),
            ((slots, rows), BF16, pltpu.HBM),
        ],
        [WHOLE] * 3,
        micros=4,
    )(x_in, g_in, ids)
    xt, gt, inv_one, times = prepared
    feed_pieces = after(w_pieces, feed_pieces)
    w_pieces = after(prepared, w_pieces)
    for at, group in enumerate(groups[2:], 2):
        w_pieces = gather_stage(w_pieces, group, sizes, join=at + 1 < len(groups))
    for group in feed_groups[2:-1]:
        feed_pieces = gather_stage(feed_pieces, group, sizes)

    def in_order(pieces):
        both = jnp.concatenate(pieces, axis=0)
        return jnp.zeros_like(both).at[owner].set(both)

    def split_rows(array, *heights):
        at, parts = 0, []
        for height in heights:
            parts.append(array[:, at : at + height].reshape(-1, width))
            at += height
        return parts

    if not direct:
        w_pieces = [in_order(w_pieces).reshape(blocks, ROWS, columns)]

    def to_send(pieces, *heights):
        if direct:
            return pieces
        array = pieces[0]
        if len(heights) > 1:
            parts = split_rows(array, low, *[ROWS] * (len(heights) - 1))
            parts = [part.reshape(-1, height, width) for part, height in zip(parts, heights)]
            array = jnp.concatenate(parts, axis=1)
        else:
            array = array.reshape(-1, heights[0], array.shape[2])
        array = array[owner]
        count = 1 << len(groups[-1])
        return jnp.split(array, count, axis=0)

    def head_block(part, cols, first=0):
        return pl.BlockSpec((size, cols), lambda h: (part * heads + first + h, 0))

    exp_rows = slots + rows // seg_count
    nt, qkv, mem_kv, side, mixed, ctx, rec, exps, exps_held, gate, lse, lsen, far_scale, near_scale, flags = call(
        functools.partial(
            attend_kernel,
            pieces=len(w_pieces),
            mem_pieces=len(memory_pieces),
            heads=heads,
            seg_count=seg_count,
            scale=scale,
        ),
        [
            (big, BF16, pltpu.HBM),
            ((3 * width, rows), BF16, pltpu.VMEM),
            ((2 * width, slots), BF16, pltpu.VMEM),
            ((width, SIDE), BF16),
            (big, BF16, pltpu.VMEM),
            (big, BF16, pltpu.VMEM),
            (big, BF16, pltpu.VMEM),
            (((heads - HELD) * exp_rows, rows), BF16, pltpu.HBM),
            ((HELD, exp_rows, rows), BF16, pltpu.VMEM),
            (lanes, F32),
            (lanes, F32),
            (lanes, F32),
            (lanes, F32),
            (lanes, F32),
            ((heads,), jnp.int32),
        ],
        [SCALARS, SCALARS, FAR, WHOLE, FAR] + [WHOLE] * (len(w_pieces) + len(memory_pieces)),
        out_specs=[WHOLE] * 4
        + [head_block(0, rows)] * 3
        + [FAR]
        + [WHOLE] * 6
        + [SCALARS],
        grid=(heads,),
        scratch=[
            pltpu.VMEM((width, columns), BF16),
            pltpu.VMEM(big, BF16),
            pltpu.VMEM((slots, rows), BF16),
            pltpu.SemaphoreType.DMA((2,)),
            pltpu.SemaphoreType.DMA((HELD,)),
        ],
        micros=22,
        vmem=28,
    )(kernel_owner, lengths, far(xt), inv_one, far(times), *w_pieces, *memory_pieces)

    feed_pieces[1:] = after(mixed, feed_pieces[1:])
    feed_pieces = gather_stage(feed_pieces, groups[-1], sizes, join=False)
    if not direct:
        parts = split_rows(in_order(feed_pieces), tall, *[shard] * (1 + chunks))
        feed_pieces = [jnp.concatenate([part.reshape(blocks, -1, width) for part in parts], axis=1)]
    pieces = len(feed_pieces)
    sends = 1 << len(groups[-1]) if direct else 1
    feed_block = (blocks // sends,) + feed_pieces[0].shape[1:]
    outs = call(
        functools.partial(feed_kernel, heads=heads, pieces=pieces, sends=sends),
        [
            ((rows, width), BF16),
            (big, F32),
            (big, BF16),
            (lanes, F32),
            (lanes, F32),
            (lanes, F32),
            ((width, SIDE), F32),
        ]
        + [(feed_block, BF16)] * sends,
        [SCALARS] + [WHOLE] * (7 + pieces),
        scratch=[
            pltpu.VMEM(shape, BF16) for shape in ((width, width), (width, ff), (ff, width))
        ],
        micros=20,
        vmem=21,
    )(kernel_owner, xt, gt, mixed, ctx, rec, gate, side, *feed_pieces)
    block_out, grad_hidden, dm, dc, dn, dlogit, ggain_two = outs[:7]
    late = to_send(outs[7:], tall, *[shard] * (1 + chunks))
    late_at = len(feed_groups)

    backs = []
    for first, count in ((heads - HELD, HELD), (0, heads - HELD)):
        held = first > 0
        late_at -= 1
        moving = sum_terms(late, feed_groups[late_at], sizes)
        outs = call(
            functools.partial(attend_back_kernel, first=first, seg_count=seg_count, scale=scale),
            [((size * count, rows), BF16)] * 3 + [((size * count, slots), BF16)] * 2,
            [
                SCALARS,
                SCALARS,
                head_block(0, rows, first),
                head_block(1, rows, first),
                head_block(2, rows, first),
                head_block(0, slots, first),
                head_block(1, slots, first),
                head_block(0, rows, first),
                WHOLE if held else pl.BlockSpec((exp_rows, rows), lambda h: (h, 0)),
            ]
            + [WHOLE] * 8,
            out_specs=[head_block(0, rows)] * 3 + [head_block(0, slots)] * 2,
            grid=(count,),
            scratch=[pltpu.VMEM((size, rows), F32)] * 2
            + [pltpu.VMEM((size, slots), F32)] * 2
            + [pltpu.VMEM((4, 2 * size + 16, rows), BF16), pltpu.VMEM(lanes, F32)],
            micros=4 * count,
            vmem=24,
        )(
            flags,
            lengths,
            qkv,
            qkv,
            qkv,
            mem_kv,
            mem_kv,
            dm,
            exps_held if held else far(exps),
            gate,
            times,
            lse,
            lsen,
            far_scale,
            near_scale,
            dc,
            dn,
        )
        late = add_terms(moving, feed_groups[late_at - 1])
        dm = after(late, dm)
        backs.insert(0, outs)
    late_at -= 1
    moving = sum_terms(late, feed_groups[late_at], sizes)

    pieces = len(w_pieces)
    *early, back = call(
        functools.partial(
            weight_kernel,
            calls=len(backs),
            pieces=pieces,
            mem_pieces=len(memory_pieces),
            sends=sends,
            heads=heads,
        ),
        [((blocks // sends, ROWS, columns), BF16)] * sends + [((columns, rows), BF16)],
        [SCALARS] + [WHOLE] * (4 + len(memory_pieces) + 5 * len(backs) + pieces),
        scratch=[pltpu.VMEM((width, columns), F32)],
        micros=6,
    )(
        kernel_owner,
        nt,
        side,
        dlogit,
        ggain_two,
        *memory_pieces,
        *[b for back in backs for b in back],
        *w_pieces,
    )
    early = to_send(early, shard)
    early = sum_terms(early, groups[-1], sizes)
    for at in reversed(range(len(groups) - 1)):
        early = add_terms(early, groups[at])
        if at + 2 == len(groups):
            back, moving = after(early, (back, moving))
        early = sum_terms(early, groups[at], sizes)
    (grad_tokens,) = call(
        functools.partial(input_kernel, heads=heads),
        [((rows, width), F32)],
        [SCALARS] + [WHOLE] * (5 + pieces),
        scratch=[pltpu.VMEM((width, columns), BF16)],
        micros=6,
    )(kernel_owner, xt, inv_one, side, back, grad_hidden, *w_pieces)

    while late_at:
        late_at -= 1
        moving = sum_terms(add_terms(moving, feed_groups[late_at]), feed_groups[late_at], sizes)
    late = moving

    if direct:
        grad_down, grad_out, grad_up = call(
            finish_feed_kernel,
            [((tall, width), F32), ((shard, width), F32), ((shard, ff), F32)],
            [WHOLE] * len(late),
            micros=1,
        )(*late)
        grad_query, grad_key, grad_value, grad_gate, grad_one, grad_two = call(
            finish_kernel,
            [((shard, width), F32)] * 3 + [((heads, shard), F32)] + [((1, shard), F32)] * 2,
            [WHOLE] * len(early),
            micros=1,
        )(*early)
        grad_gate, grad_one, grad_two = grad_gate.T, grad_one[0], grad_two[0]
    else:
        late = sum(term[0].astype(F32) for term in late)
        early = sum(term[0].astype(F32) for term in early)
        grad_down, grad_out = late[:tall], late[tall : tall + shard]
        grad_up = jnp.concatenate(
            [late[tall + shard * (1 + c) : tall + shard * (2 + c)] for c in range(chunks)], axis=1
        )
        grad_query, grad_key, grad_value = (
            early[:, at : at + width] for at in range(0, 3 * width, width)
        )
        side = early[:, 3 * width :]
        grad_gate, grad_one, grad_two = side[:, :heads], side[:, heads], side[:, heads + 1]
    return (
        block_out,
        grad_tokens,
        grad_one,
        grad_two,
        grad_query,
        grad_key,
        grad_value,
        grad_gate,
        grad_out,
        grad_up,
        grad_down,
    )


def solution(mesh):
    row_split, vector = P(("dp", "seq"), None), P(("dp", "seq"))
    in_specs = (row_split, row_split, vector, row_split, row_split, vector, vector) + (row_split,) * 7
    out_specs = (row_split, row_split, vector, vector) + (row_split,) * 7
    return jax.shard_map(
        functools.partial(on_device, sizes=dict(mesh.shape)),
        mesh=mesh,
        in_specs=in_specs,
        out_specs=out_specs,
        check_vma=False,
    )
```
